32 devices in a mesh: dp: 32 (over z, y, x, core).
Axes of the slice: x: 2, y: 2, z: 4, core: 2. Of those that a mesh axis runs over, the one named last changes fastest.
Arguments:
- tokens: bfloat16 [65536, 768], P('dp'), may hold values from -6 to 6
- eigvecs: float32 [512, 128, 16], P('dp'), may hold values from -6 to 6
- counts: int32 [512, 2], P('dp'), may hold values from 16 to 84, as said below
- endpoints: int32 [512, 128, 2], P('dp'), may hold values from 0 to 41, as said below
- cotangent: bfloat16 [65536, 768], P('dp'), may hold values from -80 to 80
- attend_in: float32 [768, 2304], P('dp'), may hold values from -0.21875 to 0.21875
- attend_in_first: float32 [768, 2304], P('dp'), may hold values from -0.00036621094 to 0.00036621094
- attend_in_second: float32 [768, 2304], P('dp'), may hold values from 2.7995772e-10 to 1.1198309e-09
- attend_out: float32 [768, 768], P(None, 'dp'), may hold values from -1.75 to 1.75
- attend_out_first: float32 [768, 768], P(None, 'dp'), may hold values from -0.00036621094 to 0.00036621094
- attend_out_second: float32 [768, 768], P(None, 'dp'), may hold values from 2.7995772e-10 to 1.1198309e-09
- feed_up: float32 [768, 768], P('dp'), may hold values from -0.21875 to 0.21875
- feed_up_first: float32 [768, 768], P('dp'), may hold values from -0.00036621094 to 0.00036621094
- feed_up_second: float32 [768, 768], P('dp'), may hold values from 2.7995772e-10 to 1.1198309e-09
- feed_down: float32 [768, 768], P(None, 'dp'), may hold values from -0.21875 to 0.21875
- feed_down_first: float32 [768, 768], P(None, 'dp'), may hold values from -0.00036621094 to 0.00036621094
- feed_down_second: float32 [768, 768], P(None, 'dp'), may hold values from 2.7995772e-10 to 1.1198309e-09
- label_in: float32 [32, 768], P(None, 'dp'), may hold values from -1 to 1
- label_in_first: float32 [32, 768], P(None, 'dp'), may hold values from -0.00036621094 to 0.00036621094
- label_in_second: float32 [32, 768], P(None, 'dp'), may hold values from 2.7995772e-10 to 1.1198309e-09
- vectors: float32 [11, 768], P(None, 'dp'), may hold values from -6 to 6, as said below
- vectors_first: float32 [11, 768], P(None, 'dp'), may hold values from -0.00036621094 to 0.00036621094
- vectors_second: float32 [11, 768], P(None, 'dp'), may hold values from 2.7995772e-10 to 1.1198309e-09
- step_count: int32 [], replicated, may hold values from 2 to 21
- learn_rate: float32 [], replicated, may hold values from 0.2 to 0.4
Outputs:
- layer_out: bfloat16 [65536, 768], P('dp')
- tokens_grad: float32 [65536, 768], P('dp')
- grad_norm: float32 [], replicated
- attend_in_grad: float32 [768, 2304], P('dp')
- attend_in_first_new: float32 [768, 2304], P('dp')
- attend_in_second_new: float32 [768, 2304], P('dp')
- attend_in_new: float32 [768, 2304], P('dp')
- attend_out_grad: float32 [768, 768], P(None, 'dp')
- attend_out_first_new: float32 [768, 768], P(None, 'dp')
- attend_out_second_new: float32 [768, 768], P(None, 'dp')
- attend_out_new: float32 [768, 768], P(None, 'dp')
- feed_up_grad: float32 [768, 768], P('dp')
- feed_up_first_new: float32 [768, 768], P('dp')
- feed_up_second_new: float32 [768, 768], P('dp')
- feed_up_new: float32 [768, 768], P('dp')
- feed_down_grad: float32 [768, 768], P(None, 'dp')
- feed_down_first_new: float32 [768, 768], P(None, 'dp')
- feed_down_second_new: float32 [768, 768], P(None, 'dp')
- feed_down_new: float32 [768, 768], P(None, 'dp')
- label_in_grad: float32 [32, 768], P(None, 'dp')
- label_in_first_new: float32 [32, 768], P(None, 'dp')
- label_in_second_new: float32 [32, 768], P(None, 'dp')
- label_in_new: float32 [32, 768], P(None, 'dp')
- vectors_grad: float32 [11, 768], P(None, 'dp')
- vectors_first_new: float32 [11, 768], P(None, 'dp')
- vectors_second_new: float32 [11, 768], P(None, 'dp')
- vectors_new: float32 [11, 768], P(None, 'dp')
The draws below stay inside these ranges and needn't reach their ends.
Inputs may be any that keep to these rules, and one draw needn't show every extreme that they name: `counts`: row m holds molecule m's node count and then its edge count; the edge count lies between the node count and twice it. `endpoints`: entry j of a molecule holds two different nodes below its node count; entries at or beyond its edge count are not used. `vectors`: rows 0 and 5 are positive.
All inputs are finite; a program needn't handle non-finite values.
Results may differ from the reference program's by a relative error of at most 0.012.
The reference program's roundings to bfloat16 on the way count: a program that leaves them out, or rounds other values in their place, can miss the bound.
Values may be sent and summed in bfloat16 or wider, within the bound.
A program may use at most 192 MiB of HBM per device.

```python
import math
import jax
import jax.numpy as jnp
from jax import lax

D = 768
HEADS = 32
HEAD_DIM = 24
FF = 768
LAP = 16
SEQ = 128
NVEC = 11
MOLS = 512
TOKENS = 65536
NPARAM = 3571968


def molecule_counts(key):
    base_key = jax.random.fold_in(key, 11)
    node_count = jax.random.randint(jax.random.fold_in(base_key, 1), (MOLS,), SEQ // 8, SEQ // 3 + 1)
    raw_extra = jax.random.randint(jax.random.fold_in(base_key, 2), (MOLS,), 0, 1 << 20)
    edge_count = node_count + raw_extra % (node_count + 1)
    places = jnp.arange(MOLS)
    node_count = jnp.where(places == 0, SEQ // 3, jnp.where(places == 1, SEQ // 8, node_count))
    edge_count = jnp.where(places == 0, 2 * (SEQ // 3), jnp.where(places == 1, SEQ // 8, edge_count))
    return (node_count.astype(jnp.int32), edge_count.astype(jnp.int32))


def draw_counts(key, part):
    node_count, edge_count = molecule_counts(key)
    return jnp.stack([node_count, edge_count], -1).astype(jnp.int32)


def draw_endpoints(key, part):
    node_count, edge_count = molecule_counts(key)
    base_key = jax.random.fold_in(key, 23)
    raw_first = jax.random.randint(jax.random.fold_in(base_key, 1), (MOLS, SEQ), 0, 1 << 20)
    raw_second = jax.random.randint(jax.random.fold_in(base_key, 2), (MOLS, SEQ), 0, 1 << 20)
    node_col = node_count[:, None]
    first_end = raw_first % node_col
    second_end = (first_end + 1 + raw_second % (node_col - 1)) % node_col
    leading = jnp.arange(SEQ)[None, :] == 0
    first_end = jnp.where(leading, node_col - 1, first_end)
    second_end = jnp.where(leading, 0, second_end)
    return jnp.stack([first_end, second_end], -1).astype(jnp.int32)


def draw_vectors(key, part):
    places = jnp.arange(D, dtype=jnp.float32)[None, :] / D
    rising = 3.0 ** (0.5 * places)
    row_index = jnp.arange(NVEC)[:, None]
    roughness = jnp.exp(0.2 * jax.random.normal(jax.random.fold_in(key, 1), (NVEC, D), jnp.float32))
    spread = jax.random.normal(jax.random.fold_in(key, 2), (NVEC, D), jnp.float32)
    is_gain = jnp.logical_or(row_index == 0, row_index == 5)
    is_type = row_index >= 9
    return jnp.where(is_gain, rising * roughness, jnp.where(is_type, 0.5 * spread, 0.3 * spread))


def draw_cotangent(key, part):
    places = jnp.arange(D, dtype=jnp.float32)[None, :] / D
    column_scale = 3.0 ** (0.5 * places) * jnp.exp(jax.random.uniform(jax.random.fold_in(key, 1), (1, D), jnp.float32, -0.5, 0.5))
    row_scale = 10.0 ** jax.random.uniform(jax.random.fold_in(key, 2), (TOKENS, 1), jnp.float32, -0.4, 0.6)
    values = jax.random.normal(jax.random.fold_in(key, 3), (TOKENS, D), jnp.float32)
    return (values * column_scale * row_scale).astype(jnp.bfloat16)


def block_scale(rng, shape, cuts, least, largest):
    gain = 1.0
    for axis_at, parts in cuts:
        draws = jax.random.uniform(jax.random.fold_in(jax.random.fold_in(rng, 6), axis_at), (parts,), jnp.float32, least / len(cuts), largest / len(cuts))
        gain = gain * jnp.repeat(jnp.exp(draws), shape[axis_at] // parts).reshape((-1,) + (1,) * (len(shape) - 1 - axis_at))
    return gain


def scatter_about(key, extent, width, reach, split=(), kind=jnp.bfloat16):
    level = block_scale(key, extent, split, -0.22, 0.18) if split else 1.0
    entries = jax.random.normal(key, extent, jnp.float32) * width * level
    return jnp.minimum(jnp.maximum(entries, -reach), reach).astype(kind)


def setup_inputs(seed: int = 0) -> dict:
    seeds = jax.random.split(jax.random.key(seed), 26)
    tokens = scatter_about(seeds[0], (TOKENS, D), 1.0, 6.0, ((0, 32),))
    eigvecs = scatter_about(seeds[1], (MOLS, SEQ, LAP), 1.0, 6.0, ((0, 32),), jnp.float32)
    counts = draw_counts(jax.random.fold_in(seeds[25], 71), 0)
    endpoints = draw_endpoints(jax.random.fold_in(seeds[25], 71), 0)
    cotangent = draw_cotangent(jax.random.fold_in(seeds[25], 71), 0)
    attend_in = scatter_about(seeds[5], (D, 3 * D), D ** -0.5, 0.21875, ((0, 32),), jnp.float32)
    attend_in_first = scatter_about(seeds[6], (D, 3 * D), (0.11 * NPARAM ** -0.5), 0.00036621094, ((0, 32),), jnp.float32)
    attend_in_second = jnp.clip(jnp.exp(math.log(1.1198308946802626e-09) - 1.3862944 * jax.random.uniform(seeds[7], (D, 3 * D), jnp.float32) ** block_scale(seeds[7], (D, 3 * D), ((0, 32),), -0.2, 0.2)), 2.7995772367006566e-10, 1.1198308946802626e-09)
    attend_out = scatter_about(seeds[8], (D, D), (2 * D // SEQ) ** -0.5, 1.75, ((1, 32),), jnp.float32)
    attend_out_first = scatter_about(seeds[9], (D, D), (0.11 * NPARAM ** -0.5), 0.00036621094, ((1, 32),), jnp.float32)
    attend_out_second = jnp.clip(jnp.exp(math.log(1.1198308946802626e-09) - 1.3862944 * jax.random.uniform(seeds[10], (D, D), jnp.float32) ** block_scale(seeds[10], (D, D), ((1, 32),), -0.2, 0.2)), 2.7995772367006566e-10, 1.1198308946802626e-09)
    feed_up = scatter_about(seeds[11], (D, FF), D ** -0.5, 0.21875, ((0, 32),), jnp.float32)
    feed_up_first = scatter_about(seeds[12], (D, FF), (0.11 * NPARAM ** -0.5), 0.00036621094, ((0, 32),), jnp.float32)
    feed_up_second = jnp.clip(jnp.exp(math.log(1.1198308946802626e-09) - 1.3862944 * jax.random.uniform(seeds[13], (D, FF), jnp.float32) ** block_scale(seeds[13], (D, FF), ((0, 32),), -0.2, 0.2)), 2.7995772367006566e-10, 1.1198308946802626e-09)
    feed_down = scatter_about(seeds[14], (FF, D), FF ** -0.5, 0.21875, ((1, 32),), jnp.float32)
    feed_down_first = scatter_about(seeds[15], (FF, D), (0.11 * NPARAM ** -0.5), 0.00036621094, ((1, 32),), jnp.float32)
    feed_down_second = jnp.clip(jnp.exp(math.log(1.1198308946802626e-09) - 1.3862944 * jax.random.uniform(seeds[16], (FF, D), jnp.float32) ** block_scale(seeds[16], (FF, D), ((1, 32),), -0.2, 0.2)), 2.7995772367006566e-10, 1.1198308946802626e-09)
    label_in = scatter_about(seeds[17], (2 * LAP, D), (2 * LAP) ** -0.5, 1.0, ((1, 32),), jnp.float32)
    label_in_first = scatter_about(seeds[18], (2 * LAP, D), (0.11 * NPARAM ** -0.5), 0.00036621094, ((1, 32),), jnp.float32)
    label_in_second = jnp.clip(jnp.exp(math.log(1.1198308946802626e-09) - 1.3862944 * jax.random.uniform(seeds[19], (2 * LAP, D), jnp.float32) ** block_scale(seeds[19], (2 * LAP, D), ((1, 32),), -0.2, 0.2)), 2.7995772367006566e-10, 1.1198308946802626e-09)
    vectors = draw_vectors(jax.random.fold_in(seeds[25], 71), 0)
    vectors_first = scatter_about(seeds[21], (NVEC, D), (0.11 * NPARAM ** -0.5), 0.00036621094, ((1, 32),), jnp.float32)
    vectors_second = jnp.clip(jnp.exp(math.log(1.1198308946802626e-09) - 1.3862944 * jax.random.uniform(seeds[22], (NVEC, D), jnp.float32) ** block_scale(seeds[22], (NVEC, D), ((1, 32),), -0.2, 0.2)), 2.7995772367006566e-10, 1.1198308946802626e-09)
    step_count = jax.random.randint(seeds[23], (), 2, 22).astype(jnp.int32)
    learn_rate = jnp.clip(jnp.exp(jax.random.uniform(seeds[24], (), jnp.float32, math.log(0.2), math.log(0.4))), 0.2, 0.4)
    return dict(tokens=tokens, eigvecs=eigvecs, counts=counts, endpoints=endpoints, cotangent=cotangent, attend_in=attend_in, attend_in_first=attend_in_first, attend_in_second=attend_in_second, attend_out=attend_out, attend_out_first=attend_out_first, attend_out_second=attend_out_second, feed_up=feed_up, feed_up_first=feed_up_first, feed_up_second=feed_up_second, feed_down=feed_down, feed_down_first=feed_down_first, feed_down_second=feed_down_second, label_in=label_in, label_in_first=label_in_first, label_in_second=label_in_second, vectors=vectors, vectors_first=vectors_first, vectors_second=vectors_second, step_count=step_count, learn_rate=learn_rate)


@jax.custom_vjp
def low(v):
    return lax.optimization_barrier(v.astype(jnp.bfloat16)).astype(jnp.float32)

@jax.custom_vjp
def low_back(v):
    return v

def low_keep(v):
    return (low(v), None)

def low_pass(kept, grad):
    return (grad,)

def back_keep(v):
    return (v, None)

def back_low(kept, grad):
    return (low(grad),)
low.defvjp(low_keep, low_pass)
low_back.defvjp(back_keep, back_low)
EPS_NORM = 1e-05
MASK_FILL = -1000000000.0
SQRT_HALF = 0.7071067811865476
BETA_ONE = 0.9
BETA_TWO = 0.999
ADAM_EPS = 1e-08
DECAY_RATE = 0.01
CLIP_LIMIT = 1.0
NORM_EPS = 1e-06

def both_ways(values):
    return low_back(low(values))

def matmul(left_side, right_side):
    return jnp.dot(left_side, right_side, precision=lax.Precision.HIGHEST, preferred_element_type=jnp.float32)

def gelu_exact(values):
    return values * 0.5 * (1.0 + lax.erf(values * SQRT_HALF))

def layer_norm(values, gain_row, shift_row):
    centred = values - lax.optimization_barrier(jnp.mean(values, -1, keepdims=True))
    recip_std = lax.rsqrt(lax.optimization_barrier(jnp.mean(centred * centred, -1, keepdims=True)) + EPS_NORM)
    return centred * recip_std * gain_row + shift_row

def identifiers(eigvecs, counts, endpoints):
    mol_count, seq_len = (endpoints.shape[0], endpoints.shape[1])
    places = jnp.arange(seq_len, dtype=jnp.int32)[None, :]
    node_count = counts[:, 0:1]
    edge_count = counts[:, 1:2]
    is_node = places < node_count
    is_edge = jnp.logical_and(places >= node_count, places < node_count + edge_count)
    edge_slot = jnp.clip(places - node_count, 0, seq_len - 1).astype(jnp.int32)
    first_end = jnp.take_along_axis(endpoints[:, :, 0], edge_slot, 1)
    second_end = jnp.take_along_axis(endpoints[:, :, 1], edge_slot, 1)
    source = jnp.where(is_node, places, first_end).astype(jnp.int32)
    target = jnp.where(is_node, places, second_end).astype(jnp.int32)
    left_half = jnp.take_along_axis(eigvecs, source[:, :, None], 1)
    right_half = jnp.take_along_axis(eigvecs, target[:, :, None], 1)
    is_live = jnp.logical_or(is_node, is_edge)
    labels = jnp.concatenate([left_half, right_half], -1) * is_live[:, :, None].astype(eigvecs.dtype)
    return (labels.reshape(mol_count * seq_len, -1), is_node.reshape(-1).astype(eigvecs.dtype), is_edge.reshape(-1).astype(eigvecs.dtype), is_live)

def forward(tokens_f, masters, labels, is_node, is_edge, is_live):
    weight_in, weight_out, weight_up, weight_down, weight_label, vector_rows = [low(master) for master in masters]
    model_width = weight_out.shape[0]
    mol_count, seq_len = (is_live.shape[0], is_live.shape[1])
    label_term = low_back(matmul(low(labels), weight_label))
    embedded = tokens_f + label_term + is_node[:, None] * vector_rows[9] + is_edge[:, None] * vector_rows[10]
    input_one = low(layer_norm(embedded, vector_rows[0], vector_rows[1]))
    bias_row = jnp.concatenate([vector_rows[2], jnp.zeros_like(vector_rows[2]), vector_rows[3]])
    projected = both_ways(matmul(input_one, weight_in) + bias_row)
    queries = projected[:, :model_width].reshape(mol_count, seq_len, HEADS, HEAD_DIM)
    key_heads = projected[:, model_width:2 * model_width].reshape(mol_count, seq_len, HEADS, HEAD_DIM)
    value_heads = projected[:, 2 * model_width:].reshape(mol_count, seq_len, HEADS, HEAD_DIM)
    scores = jnp.einsum('mqhd,mkhd->mhqk', queries, key_heads, precision=lax.Precision.HIGHEST) * HEAD_DIM ** (-0.5)
    scores = low_back(scores)
    scores = jnp.where(is_live[:, None, None, :], scores, MASK_FILL)
    maxima = lax.optimization_barrier(jnp.max(scores, -1, keepdims=True))
    exponent = jnp.exp(scores - maxima)
    shares = low(exponent / lax.optimization_barrier(jnp.sum(exponent, -1, keepdims=True)))
    attended = jnp.einsum('mhqk,mkhd->mqhd', shares, value_heads, precision=lax.Precision.HIGHEST)
    attended = both_ways(attended.reshape(mol_count * seq_len, model_width))
    middle = embedded + low_back(matmul(attended, weight_out) + vector_rows[4])
    input_two = low(layer_norm(middle, vector_rows[5], vector_rows[6]))
    pre_act = low_back(matmul(input_two, weight_up) + vector_rows[7])
    activated = low(gelu_exact(pre_act))
    return middle + low_back(matmul(activated, weight_down) + vector_rows[8])

def adam_update(master, first_old, second_old, gradient, step_f, learn_rate, decay_flag):
    first_new = BETA_ONE * first_old + (1.0 - BETA_ONE) * gradient
    second_new = BETA_TWO * second_old + (1.0 - BETA_TWO) * gradient * gradient
    moment_hat = first_new / (1.0 - BETA_ONE ** step_f)
    second_hat = second_new / (1.0 - BETA_TWO ** step_f)
    change = moment_hat / (jnp.sqrt(second_hat) + ADAM_EPS)
    if decay_flag:
        change = change + DECAY_RATE * master
    return (first_new, second_new, master - learn_rate * change)

def reference(tokens, eigvecs, counts, endpoints, cotangent, attend_in, attend_in_first, attend_in_second, attend_out, attend_out_first, attend_out_second, feed_up, feed_up_first, feed_up_second, feed_down, feed_down_first, feed_down_second, label_in, label_in_first, label_in_second, vectors, vectors_first, vectors_second, step_count, learn_rate):
    masters = (attend_in, attend_out, feed_up, feed_down, label_in, vectors)
    firsts = (attend_in_first, attend_out_first, feed_up_first, feed_down_first, label_in_first, vectors_first)
    seconds = (attend_in_second, attend_out_second, feed_up_second, feed_down_second, label_in_second, vectors_second)
    labels, is_node, is_edge, is_live = identifiers(eigvecs, counts, endpoints)
    group_mols = max(1, min(MOLS, 4096 // SEQ))
    rounds = MOLS // group_mols
    group_rows = group_mols * SEQ

    def split_rows(values):
        return values.reshape((rounds, group_rows) + values.shape[1:])
    inputs = (split_rows(tokens.astype(jnp.float32)), split_rows(cotangent.astype(jnp.float32)), split_rows(labels), split_rows(is_node), split_rows(is_edge), is_live.reshape(rounds, group_mols, SEQ))

    def one_group(running, pieces):
        tokens_f, back_rows, label_rows, node_rows, edge_rows, live_rows = pieces

        def run_layer(inner_tokens, inner_masters):
            return forward(inner_tokens, inner_masters, label_rows, node_rows, edge_rows, live_rows)
        result, pull_back = jax.vjp(run_layer, tokens_f, masters)
        tokens_back, master_back = pull_back(back_rows)
        running = jax.tree.map(lambda before, addend: before + addend, running, master_back)
        return (running, (result.astype(jnp.bfloat16), tokens_back))
    zero_grads = jax.tree.map(jnp.zeros_like, masters)
    gradients, (outputs, token_grads) = lax.scan(one_group, zero_grads, inputs)
    squares = sum((jnp.sum(gradient * gradient) for gradient in gradients))
    grad_norm = jnp.sqrt(squares)
    factor = jnp.minimum(1.0, CLIP_LIMIT / (grad_norm + NORM_EPS))
    step_f = step_count.astype(jnp.float32)
    results = []
    for position in range(6):
        clipped = gradients[position] * factor
        first_new, second_new, master_new = adam_update(masters[position], firsts[position], seconds[position], clipped, step_f, learn_rate, position < 5)
        results.append((clipped, first_new, second_new, master_new))
    return (outputs.reshape(TOKENS, D), token_grads.reshape(TOKENS, D), grad_norm, results[0][0], results[0][1], results[0][2], results[0][3], results[1][0], results[1][1], results[1][2], results[1][3], results[2][0], results[2][1], results[2][2], results[2][3], results[3][0], results[3][1], results[3][2], results[3][3], results[4][0], results[4][1], results[4][2], results[4][3], results[5][0], results[5][1], results[5][2], results[5][3])
```

```python
import functools
import math

import jax
import jax.numpy as jnp
from jax import lax
from jax.experimental import pallas as pl
from jax.experimental.pallas import tpu as pltpu
from jax.sharding import PartitionSpec as P

HEADS = 32
EPS_NORM = 1e-05
MASK_FILL = -1e30
SQRT_HALF = 0.7071067811865476
INV_SQRT_TWO_PI = 0.3989422804014327
BETA_ONE = 0.9
BETA_TWO = 0.999
ADAM_EPS = 1e-08
DECAY_RATE = 0.01
CLIP_LIMIT = 1.0
NORM_EPS = 1e-06
LOG2E = 1.4426950408889634

BF = jnp.bfloat16
F32 = jnp.float32
MESH = pl.DeviceIdType.MESH
LANES = 128
VMEM_LIMIT = 60 << 20

SMALL = 128
NODE, EDGE = 32, 33
GAIN1, SHIFT1, QBIAS, VBIAS, OBIAS, GAIN2, SHIFT2, UBIAS, DBIAS = range(34, 43)


def nn(a, b):
    return lax.dot_general(a, b, (((1,), (0,)), ((), ())), preferred_element_type=F32)


def nt(a, b):
    return lax.dot_general(a, b, (((1,), (1,)), ((), ())), preferred_element_type=F32)


def tn(a, b):
    return lax.dot_general(a, b, (((0,), (0,)), ((), ())), preferred_element_type=F32)


def layer_stats(values):
    centred = values - jnp.mean(values, -1, keepdims=True)
    recip_std = lax.rsqrt(jnp.mean(centred * centred, -1, keepdims=True) + EPS_NORM)
    return centred * recip_std, recip_std


def norm_back(grad_out, normed, recip_std, gain_row):
    scaled = grad_out * gain_row
    return recip_std * (
        scaled
        - jnp.mean(scaled, -1, keepdims=True)
        - normed * jnp.mean(scaled * normed, -1, keepdims=True)
    )


class Heads:
    def __init__(self, width):
        self.dim = width // HEADS
        span = 1
        while (span * self.dim) % LANES:
            span *= 2
        self.block = span
        self.tiles = span * self.dim // LANES
        self.blocks = HEADS // span

    def first(self, head):
        return head * self.dim // LANES

    def last(self, head):
        return ((head + 1) * self.dim - 1) // LANES

    def heads_of(self, tile):
        return [h for h in range(self.block) if self.first(h) <= tile <= self.last(h)]

    def mask(self, tile, head):
        lane = lax.broadcasted_iota(jnp.int32, (1, LANES), 1) + tile * LANES
        inside = jnp.logical_and(lane >= head * self.dim, lane < (head + 1) * self.dim)
        return inside.astype(F32).astype(BF)


def only(value, mask):
    return value * mask


def pair_rows(hd, tiles_of, pair):
    h0, h1 = 2 * pair, 2 * pair + 1
    lo, hi = hd.first(h0), hd.last(h1)
    rows = []
    for h in (h0, h1):
        parts = []
        for t in range(lo, hi + 1):
            if hd.first(h) <= t <= hd.last(h):
                parts.append(only(tiles_of[t], hd.mask(t, h)))
            else:
                parts.append(jnp.zeros_like(tiles_of[t]))
        rows.append(parts[0] if len(parts) == 1 else jnp.concatenate(parts, 1))
    return jnp.concatenate(rows, 0)


def pair_full(hd, tiles_of, pair):
    lo, hi = hd.first(2 * pair), hd.last(2 * pair + 1)
    parts = [tiles_of[t] for t in range(lo, hi + 1)]
    return parts[0] if len(parts) == 1 else jnp.concatenate(parts, 1)


def tile_rows(hd, tile_value, tile):
    return jnp.concatenate([only(tile_value, hd.mask(tile, h)) for h in hd.heads_of(tile)], 0)


def front_kernel(
    counts, tokens, eig, ends, cot, w_in, w_out, w_up, w_down, small,
    out_o, proj_o, lse_o, emb_o, dmid_o, dmix_o, labt_o, gout_o, gup_o, gdown_o, gvec_o,
    small_t, mixed_s, p_buf, acc_out, acc_up, acc_down, acc_vec,
    *, hd, mols, seq, steps,
):
    step = pl.program_id(0)
    width = w_in.shape[0]
    score = hd.dim ** -0.5

    @pl.when(step == 0)
    def _():
        small_t[...] = small[...].astype(F32).T
        acc_out[...] = jnp.zeros_like(acc_out)
        acc_up[...] = jnp.zeros_like(acc_up)
        acc_down[...] = jnp.zeros_like(acc_down)
        acc_vec[...] = jnp.zeros_like(acc_vec)

    row = lambda i: small_t[i : i + 1, :]
    iota0 = lax.broadcasted_iota(jnp.int32, (seq, seq), 0)
    iota1 = lax.broadcasted_iota(jnp.int32, (seq, seq), 1)
    token_row = lax.broadcasted_iota(jnp.int32, (1, seq), 1)
    one = lambda c: c.astype(F32).astype(BF)
    label_rows = []
    for m in range(mols):
        nodes = counts[0, step * mols + m]
        live = nodes + counts[1, step * mols + m]
        eig_f = eig[m]
        eig_low = eig_f.astype(BF)
        shift = one(jnp.logical_and(iota1 - iota0 == nodes, iota1 < live))
        halves = []
        for end in range(2):
            pick = one(iota0 == ends[m, end : end + 1, :])
            edge_lab = nn(eig_low, pick).astype(BF)
            moved = nn(edge_lab, shift)
            halves.append(jnp.where(token_row < nodes, eig_f, moved))
        is_node = (token_row < nodes).astype(F32)
        is_edge = jnp.logical_and(token_row >= nodes, token_row < live).astype(F32)
        kind = jnp.where(lax.broadcasted_iota(jnp.int32, (16, seq), 0) == 0, is_node,
                         jnp.where(lax.broadcasted_iota(jnp.int32, (16, seq), 0) == 1, is_edge, 0.0))
        lab = jnp.concatenate(halves + [kind], 0)
        labt_o[m] = lab.astype(BF)
        pad = jnp.zeros((SMALL - lab.shape[0], seq), F32)
        label_rows.append(jnp.concatenate([lab, pad], 0).T.astype(BF))
    labels = jnp.concatenate(label_rows, 0)
    embedded = tokens[...].astype(F32) + nn(labels, small_t[...].astype(BF))
    emb_o[...] = embedded
    normed, recip = layer_stats(embedded)
    input_one = (normed * row(GAIN1) + row(SHIFT1)).astype(BF)
    for part in range(3):
        cols = slice(part * width, (part + 1) * width)
        value = nn(input_one, w_in[:, cols])
        if part == 0:
            value = value + row(QBIAS)
        if part == 2:
            value = value + row(VBIAS)
        proj_o[:, cols] = value.astype(BF)

    for m in range(mols):
        nodes = counts[0, step * mols + m]
        live = nodes + counts[1, step * mols + m]
        key_live = lax.broadcasted_iota(jnp.int32, (seq, 2 * seq), 0) < live
        rows = slice(m * seq, (m + 1) * seq)
        for b in range(hd.blocks):
            base = b * hd.tiles * LANES
            get = lambda part: [
                proj_o[rows, part * width + base + t * LANES : part * width + base + (t + 1) * LANES]
                for t in range(hd.tiles)
            ]
            q, k, v = get(0), get(1), get(2)
            for pair in range(hd.block // 2):
                scores = nt(pair_full(hd, k, pair), pair_rows(hd, q, pair))
                scores = jnp.where(key_live, scores, MASK_FILL)
                top = jnp.max(scores, 0, keepdims=True)
                ex = jnp.exp2((scores - top) * (score * LOG2E))
                total = jnp.sum(ex, 0, keepdims=True)
                shares = ex * (1.0 / total)
                lse_o[m, b * (hd.block // 2) + pair : b * (hd.block // 2) + pair + 1, :] = (
                    top + jnp.log2(total) * (1.0 / (score * LOG2E))
                )
                for i in range(2):
                    h = 2 * pair + i
                    p_buf[:, h * seq : (h + 1) * seq] = shares[:, i * seq : (i + 1) * seq].T.astype(BF)
            for t in range(hd.tiles):
                hs = hd.heads_of(t)
                mixed = nn(p_buf[:, hs[0] * seq : (hs[-1] + 1) * seq], tile_rows(hd, v[t], t))
                mixed_s[rows, base + t * LANES : base + (t + 1) * LANES] = mixed.astype(BF)

    mixed = mixed_s[...]
    middle = embedded + (nt(mixed, w_out[...]) + row(OBIAS))
    normed2, recip2 = layer_stats(middle)
    input_two = (normed2 * row(GAIN2) + row(SHIFT2)).astype(BF)
    pre = nn(input_two, w_up[...]) + row(UBIAS)
    half_erf = 0.5 * (1.0 + lax.erf(pre * SQRT_HALF))
    act = (pre * half_erf).astype(BF)
    slope = half_erf + pre * jnp.exp(-0.5 * pre * pre) * INV_SQRT_TWO_PI
    out_o[...] = (middle + (nt(act, w_down[...]) + row(DBIAS))).astype(BF)
    back = cot[...]
    back_f = back.astype(F32)
    d_pre_f = nn(back, w_down[...]) * slope
    d_pre = d_pre_f.astype(BF)
    acc_down[...] += tn(back, act)
    acc_up[...] += tn(input_two, d_pre)
    d_in2 = nt(d_pre, w_up[...])
    d_mid = back_f + norm_back(d_in2, normed2, recip2, row(GAIN2))
    dmid_o[...] = d_mid
    branch = d_mid.astype(BF)
    acc_out[...] += tn(branch, mixed)
    dmix_o[...] = nn(branch, w_out[...]).astype(BF)
    add = lambda v: jnp.sum(v, 0, keepdims=True)
    sums = {
        OBIAS: add(branch.astype(F32)),
        GAIN2: add(d_in2 * normed2),
        SHIFT2: add(d_in2),
        UBIAS: add(d_pre.astype(F32)),
        DBIAS: add(back_f),
    }
    for i, v in sums.items():
        acc_vec[i - 34 : i - 33, :] += v

    @pl.when(step == steps - 1)
    def _():
        gout_o[...] = acc_out[...].astype(BF)
        gup_o[...] = acc_up[...].astype(BF)
        gdown_o[...] = acc_down[...].astype(BF)
        gvec_o[...] = acc_vec[...]


def back_kernel(
    counts, proj, lse, emb, dmid, dmix, labt, w_in, small, gvec,
    tg_o, gin_o, gsmall_o,
    small_t, pt_buf, dst_buf, ds_buf, dproj_s, acc_in, acc_vec, acc_lab,
    *, hd, mols, seq, steps,
):
    step = pl.program_id(0)
    width = w_in.shape[0]
    score = hd.dim ** -0.5

    @pl.when(step == 0)
    def _():
        small_t[...] = small[...].astype(F32).T
        acc_in[...] = jnp.zeros_like(acc_in)
        acc_vec[...] = gvec[...]
        acc_lab[...] = jnp.zeros_like(acc_lab)

    row = lambda i: small_t[i : i + 1, :]
    for m in range(mols):
        nodes = counts[0, step * mols + m]
        live = nodes + counts[1, step * mols + m]
        key_live = lax.broadcasted_iota(jnp.int32, (seq, 2 * seq), 0) < live
        rows = slice(m * seq, (m + 1) * seq)
        for b in range(hd.blocks):
            base = b * hd.tiles * LANES
            get = lambda ref, part: [
                ref[rows, part * width + base + t * LANES : part * width + base + (t + 1) * LANES]
                for t in range(hd.tiles)
            ]
            q, k, v, do = get(proj, 0), get(proj, 1), get(proj, 2), get(dmix, 0)
            for pair in range(hd.block // 2):
                scores = nt(pair_full(hd, k, pair), pair_rows(hd, q, pair))
                scores = jnp.where(key_live, scores, MASK_FILL)
                at = b * (hd.block // 2) + pair
                p = jnp.exp2((scores - lse[m, at : at + 1, :]) * (score * LOG2E))
                dp = nt(pair_full(hd, v, pair), pair_rows(hd, do, pair))
                inner = jnp.sum(p * dp, 0, keepdims=True)
                ds = p * (dp - inner)
                cols = slice(2 * pair * seq, (2 * pair + 2) * seq)
                pt_buf[:, cols] = p.astype(BF)
                dst_buf[:, cols] = ds.astype(BF)
                for i in range(2):
                    h = 2 * pair + i
                    ds_buf[:, h * seq : (h + 1) * seq] = ds[:, i * seq : (i + 1) * seq].T.astype(BF)
            for t in range(hd.tiles):
                hs = hd.heads_of(t)
                span = slice(hs[0] * seq, (hs[-1] + 1) * seq)
                at = base + t * LANES
                d_v = nn(pt_buf[:, span], tile_rows(hd, do[t], t))
                d_k = nn(dst_buf[:, span], tile_rows(hd, q[t], t)) * score
                d_q = nn(ds_buf[:, span], tile_rows(hd, k[t], t)) * score
                dproj_s[rows, at : at + LANES] = d_q.astype(BF)
                dproj_s[rows, width + at : width + at + LANES] = d_k.astype(BF)
                dproj_s[rows, 2 * width + at : 2 * width + at + LANES] = d_v.astype(BF)

    normed, recip = layer_stats(emb[...])
    input_one = (normed * row(GAIN1) + row(SHIFT1)).astype(BF)
    d_proj = dproj_s[...]
    acc_in[...] += tn(input_one, d_proj)
    d_in1 = nt(d_proj, w_in[...])
    tg = dmid[...] + norm_back(d_in1, normed, recip, row(GAIN1))
    tg_o[...] = tg
    tg_hi = tg.astype(BF)
    tg_lo = (tg - tg_hi.astype(F32)).astype(BF)
    lab = jnp.concatenate([labt[m] for m in range(mols)], 1)
    acc_lab[...] += nn(lab, tg_hi)
    acc_lab[32:48, :] += nn(lab[32:48, :], tg_lo)
    add = lambda v: jnp.sum(v, 0, keepdims=True)
    sums = {
        GAIN1: add(d_in1 * normed),
        SHIFT1: add(d_in1),
        QBIAS: add(d_proj[:, :width].astype(F32)),
        VBIAS: add(d_proj[:, 2 * width :].astype(F32)),
    }
    for i, v in sums.items():
        acc_vec[i - 34 : i - 33, :] += v

    @pl.when(step == steps - 1)
    def _():
        gin_o[...] = acc_in[...].astype(BF)
        full = jnp.concatenate(
            [acc_lab[0:32, :], acc_lab[32:34, :], acc_vec[0:9, :], jnp.zeros((SMALL - 43, width), F32)], 0
        )
        gsmall_o[...] = full.T.astype(BF)


def whole(shape):
    return pl.BlockSpec(shape, lambda *_: (0,) * len(shape), pipeline_mode=pl.Buffered(1))


def out_whole(shape):
    return pl.BlockSpec(shape, lambda *_: (0,) * len(shape))


def layer(tokens, eig_t, counts_t, ends_t, cot, w_in, w_out, w_up, w_down, small, mols_step):
    count, width = tokens.shape
    mols_all, lap, seq = eig_t.shape
    hd = Heads(width)
    steps = mols_all // mols_step
    rows = mols_step * seq
    tok = lambda w: pl.BlockSpec((rows, w), lambda i, *_: (i, 0))
    mol = lambda a, b: pl.BlockSpec((mols_step, a, b), lambda i, *_: (i, 0, 0))
    params = pltpu.CompilerParams(vmem_limit_bytes=VMEM_LIMIT, dimension_semantics=("arbitrary",))
    sq = (width, width)
    front = pl.pallas_call(
        functools.partial(front_kernel, hd=hd, mols=mols_step, seq=seq, steps=steps),
        grid_spec=pltpu.PrefetchScalarGridSpec(
            num_scalar_prefetch=1,
            grid=(steps,),
            in_specs=[tok(width), mol(lap, seq), mol(2, seq), tok(width), whole((width, 3 * width)),
                      whole(sq), whole(sq), whole(sq), whole((width, SMALL))],
            out_specs=[tok(width), tok(3 * width), mol(HEADS // 2, 2 * seq), tok(width), tok(width), tok(width),
                       mol(48, seq), out_whole(sq), out_whole(sq), out_whole(sq), out_whole((16, width))],
            scratch_shapes=[
                pltpu.VMEM((SMALL, width), F32),
                pltpu.VMEM((rows, width), BF),
                pltpu.VMEM((seq, hd.block * seq), BF),
                pltpu.VMEM(sq, F32), pltpu.VMEM(sq, F32), pltpu.VMEM(sq, F32),
                pltpu.VMEM((16, width), F32),
            ],
        ),
        out_shape=[
            jax.ShapeDtypeStruct((count, width), BF),
            jax.ShapeDtypeStruct((count, 3 * width), BF),
            jax.ShapeDtypeStruct((mols_all, HEADS // 2, 2 * seq), F32),
            jax.ShapeDtypeStruct((count, width), F32),
            jax.ShapeDtypeStruct((count, width), F32),
            jax.ShapeDtypeStruct((count, width), BF),
            jax.ShapeDtypeStruct((mols_all, 48, seq), BF),
            jax.ShapeDtypeStruct(sq, BF),
            jax.ShapeDtypeStruct(sq, BF),
            jax.ShapeDtypeStruct(sq, BF),
            jax.ShapeDtypeStruct((16, width), F32),
        ],
        compiler_params=params,
        name="front",
    )(counts_t, tokens, eig_t, ends_t, cot, w_in, w_out, w_up, w_down, small)
    out, proj, lse, emb, dmid, dmix, labt, g_out, g_up, g_down, g_vec = front
    tg, g_in, g_small = pl.pallas_call(
        functools.partial(back_kernel, hd=hd, mols=mols_step, seq=seq, steps=steps),
        grid_spec=pltpu.PrefetchScalarGridSpec(
            num_scalar_prefetch=1,
            grid=(steps,),
            in_specs=[tok(3 * width), mol(HEADS // 2, 2 * seq), tok(width), tok(width), tok(width), mol(48, seq),
                      whole((width, 3 * width)), whole((width, SMALL)), whole((16, width))],
            out_specs=[tok(width), out_whole((width, 3 * width)), out_whole((width, SMALL))],
            scratch_shapes=[
                pltpu.VMEM((SMALL, width), F32),
                pltpu.VMEM((seq, hd.block * seq), BF),
                pltpu.VMEM((seq, hd.block * seq), BF),
                pltpu.VMEM((seq, hd.block * seq), BF),
                pltpu.VMEM((rows, 3 * width), BF),
                pltpu.VMEM((width, 3 * width), F32),
                pltpu.VMEM((16, width), F32),
                pltpu.VMEM((48, width), F32),
            ],
        ),
        out_shape=[
            jax.ShapeDtypeStruct((count, width), F32),
            jax.ShapeDtypeStruct((width, 3 * width), BF),
            jax.ShapeDtypeStruct((width, SMALL), BF),
        ],
        compiler_params=params,
        name="back",
    )(counts_t, proj, lse, emb, dmid, dmix, labt, w_in, small, g_vec)
    return out, tg, g_in, g_out, g_up, g_down, g_small


class Plan:
    def __init__(self, count):
        self.count = count
        self.bits = count.bit_length() - 1
        self.chip_bits = self.bits - 1
        self.dims = (2,) * self.chip_bits
        near = list(range(1, min(4, self.bits)))
        self.far = list(range(self.bits - 1, near[-1], -1))
        self.turns = [near[i:] + near[:i] for i in range(len(near))]

    def order(self, part):
        return self.far + self.turns[part % len(self.turns)]

    @staticmethod
    def fits(count, rows):
        return count >= 16 and count & (count - 1) == 0 and rows % 8 == 0


def my_place(plan):
    me = lax.axis_index("dp")
    bit = [lax.rem(lax.div(me, jnp.int32(1 << b)), jnp.int32(2)) for b in range(plan.bits)]
    other = [me + (1 - 2 * bit[b]) * (1 << b) for b in range(plan.bits)]
    return me, bit, other


def greet(plan, other):
    barrier = pltpu.get_barrier_semaphore()
    for b in range(plan.bits):
        pl.semaphore_signal(barrier, inc=1, device_id=(other[b],), device_id_type=MESH)
    pl.semaphore_wait(barrier, plan.bits)


class Gather:
    def __init__(self, plan, bit, other, send, recv):
        self.plan, self.bit, self.other, self.send, self.recv = plan, bit, other, send, recv

    def cols(self, part, mine):
        buf, src, stage, at, width = part["buf"], part["src"], part["stage"], part["at"], part["width"]
        if not part["split"]:
            return pl.ds(at, width)
        half = width // 2
        which = self.bit[0] if mine else 1 - self.bit[0]
        return pl.ds(pl.multiple_of(at + which * half, LANES), half)

    def copy(self, part, phase):
        plan, i = self.plan, part["i"]
        if phase == 0:
            cols = self.cols(part, False)
            src, dst, to = part["src"].at[:, cols], part["stage"], self.other[0]
        elif phase <= plan.chip_bits:
            order = plan.order(part["turn"])
            done, b = order[: phase - 1], order[phase - 1]
            idx = tuple(
                slice(None) if bb in done else self.bit[bb] for bb in range(plan.bits - 1, 0, -1)
            )
            ref = part["buf"].at[idx + (slice(None), self.cols(part, True))]
            src, dst, to = ref, ref, self.other[b]
        else:
            ref = part["buf"].at[(slice(None),) * (plan.chip_bits + 1) + (self.cols(part, True),)]
            src, dst, to = ref, ref, self.other[0]
        return pltpu.make_async_remote_copy(
            src_ref=src, dst_ref=dst, send_sem=self.send.at[i, phase], recv_sem=self.recv.at[i, phase],
            device_id=(to,), device_id_type=MESH,
        )

    def phases(self, part):
        return self.plan.chip_bits + (2 if part["split"] else 1)

    def start(self, part, phase):
        self.copy(part, phase).start()

    def wait(self, part, phase):
        self.copy(part, phase).wait()
        if phase == 0:
            cols = self.cols(part, True)
            own, got = part["src"][:, cols], part["stage"][...]
            lower = self.bit[0] == 0
            rows = jnp.concatenate([jnp.where(lower, own, got), jnp.where(lower, got, own)], 0)
            idx = tuple(self.bit[bb] for bb in range(self.plan.bits - 1, 0, -1))
            part["buf"][idx + (slice(None), cols)] = rows.astype(BF)

    def advance(self, part, phase):
        self.wait(part, phase)
        if phase + 1 < self.phases(part):
            self.start(part, phase + 1)


def gather_kernel(
    s_in, s_out, s_up, s_down, s_small, w_in, w_out, w_up, w_down, small,
    g0, g1, g2, g3, g4, g5, g6, send, recv, *, plan, width,
):
    me, bit, other = my_place(plan)
    greet(plan, other)
    gather = Gather(plan, bit, other, send, recv)
    make = lambda i, src, buf, stage, at, wide, split, turn: dict(
        i=i, src=src, buf=buf, stage=stage, at=at, width=wide, split=split, turn=turn
    )
    parts = [
        make(0, s_small, small, g6, 0, SMALL, False, 0),
        make(1, s_in, w_in, g0, 0, width, True, 0),
        make(2, s_in, w_in, g1, width, width, True, 1),
        make(3, s_in, w_in, g2, 2 * width, width, True, 2),
        make(4, s_out, w_out, g3, 0, width, True, 0),
        make(5, s_up, w_up, g4, 0, width, True, 1),
        make(6, s_down, w_down, g5, 0, width, True, 2),
    ]
    for part in parts:
        gather.start(part, 0)
    for phase in range(plan.chip_bits + 2):
        for part in parts:
            if phase < gather.phases(part):
                gather.advance(part, phase)


def gather_call(plan, shards, width):
    s_in, s_out, s_up, s_down, s_small = shards
    rows = s_in.shape[0]
    vm = pl.BlockSpec(memory_space=pltpu.VMEM)
    buf = lambda c: jax.ShapeDtypeStruct(plan.dims + (2 * rows, c), BF)
    stage = lambda c: pltpu.VMEM((rows, c), F32)
    got = pl.pallas_call(
        functools.partial(gather_kernel, plan=plan, width=width),
        in_specs=[vm] * 5,
        out_specs=[vm] * 5,
        out_shape=[buf(3 * width), buf(width), buf(width), buf(width), buf(SMALL)],
        scratch_shapes=[stage(width // 2)] * 6 + [stage(SMALL)]
        + [pltpu.SemaphoreType.DMA((7, plan.chip_bits + 2))] * 2,
        compiler_params=pltpu.CompilerParams(
            collective_id=0, has_side_effects=True, vmem_limit_bytes=VMEM_LIMIT
        ),
        name="gather",
    )(s_in, s_out, s_up, s_down, s_small)
    return [v.reshape(-1, v.shape[-1]) for v in got]


class Scatter:
    def __init__(self, plan, bit, other, send, recv):
        self.plan, self.bit, self.other, self.send, self.recv = plan, bit, other, send, recv

    def cols(self, part, mine):
        half = part["width"] // 2
        which = self.bit[0] if mine else 1 - self.bit[0]
        return pl.ds(pl.multiple_of(part["at"] + which * half, LANES), half)

    def order(self, part):
        return self.plan.order(part["turn"])[::-1]

    def index(self, part, phase, mine):
        done, b = self.order(part)[: phase - 1], self.order(part)[phase - 1]
        idx = []
        for bb in range(self.plan.bits - 1, 0, -1):
            if bb in done:
                continue
            idx.append((self.bit[b] if mine else 1 - self.bit[b]) if bb == b else slice(None))
        return tuple(idx)

    def rows(self, which):
        r = self.plan_rows
        return pl.ds(pl.multiple_of(which * r, 8), r)

    def copy(self, part, phase):
        plan, i = self.plan, part["i"]
        every = (slice(None),) * (plan.chip_bits + 1)
        if phase == 0:
            if part["split"]:
                src = part["src"].at[every + (self.cols(part, False),)]
            else:
                src = part["src"]
            dst, to = part["slots"][0], self.other[0]
        elif phase <= plan.chip_bits:
            src = part["slots"][phase - 1].at[self.index(part, phase, False)]
            dst, to = part["slots"][phase], self.other[self.order(part)[phase - 1]]
        else:
            r = part["sum"].shape[0] // 2
            src = part["sum"].at[pl.ds(pl.multiple_of((1 - self.bit[0]) * r, 8), r)]
            dst, to = part["last"], self.other[0]
        return pltpu.make_async_remote_copy(
            src_ref=src, dst_ref=dst, send_sem=self.send.at[i, phase], recv_sem=self.recv.at[i, phase],
            device_id=(to,), device_id_type=MESH,
        )

    def phases(self, part):
        return self.plan.chip_bits + (2 if part["split"] else 1)

    def start(self, part, phase):
        self.copy(part, phase).start()

    def wait(self, part, phase):
        plan = self.plan
        self.copy(part, phase).wait()
        every = (slice(None),) * (plan.chip_bits + 1)
        if phase > plan.chip_bits:
            return
        slot = part["slots"][phase]
        if phase == 0:
            if part["split"]:
                mine = part["src"][every + (self.cols(part, True),)]
            else:
                mine = part["src"][...]
        else:
            mine = part["slots"][phase - 1][self.index(part, phase, True)]
        total = mine.astype(F32) + slot[...].astype(F32)
        if phase == plan.chip_bits:
            part["sum"][...] = total
        else:
            slot[...] = total.astype(BF)

    def advance(self, part, phase):
        self.wait(part, phase)
        if phase + 1 < self.phases(part):
            self.start(part, phase + 1)

    def finish(self, part, out):
        r = part["sum"].shape[0] // 2
        own = part["sum"][pl.ds(pl.multiple_of(self.bit[0] * r, 8), r), :]
        if not part["split"]:
            out[...] = own
            return
        half = part["width"] // 2
        out[:, self.cols(part, True)] = own
        out[:, self.cols(part, False)] = part["last"][...]


def norm_exchange(plan, me, bit, squares, mine, boxes, send, recv):
    low = 1 << min(3, plan.bits)
    value = jnp.full((8, LANES), squares, F32)
    base = 0
    for span, stride in ((low, 1), (plan.count // low, low)):
        if span == 1:
            continue
        place = lax.rem(lax.div(me, jnp.int32(stride)), jnp.int32(span))
        mine[...] = value
        copies = []
        for d in range(1, span):
            to_place = lax.rem(place + d, jnp.int32(span))
            to = me + (to_place - place) * stride
            copies.append(pltpu.make_async_remote_copy(
                src_ref=mine, dst_ref=boxes.at[base + d - 1], send_sem=send.at[base + d - 1],
                recv_sem=recv.at[base + d - 1], device_id=(to,), device_id_type=MESH,
            ))
        for c in copies:
            c.start()
        for c in copies:
            c.wait()
        for d in range(1, span):
            value = value + boxes[base + d - 1]
        base += span - 1
    return value


def ring_partners(plan, me):
    low = 1 << min(3, plan.bits)
    found = []
    for span, stride in ((low, 1), (plan.count // low, low)):
        place = lax.rem(lax.div(me, jnp.int32(stride)), jnp.int32(span))
        for d in range(1, span):
            found.append(me + (lax.rem(place + d, jnp.int32(span)) - place) * stride)
    return found


def scatter_kernel(g_in, g_out, g_up, g_down, g_small, o_in, o_out, o_up, o_down, o_small, o_norm, *rest, plan, width):
    k = plan.chip_bits + 1
    slots = [rest[i * k : (i + 1) * k] for i in range(7)]
    rest = rest[7 * k :]
    sums, rest = rest[:7], rest[7:]
    lasts, rest = rest[:6], rest[6:]
    send, recv, mine, boxes, nsend, nrecv = rest
    me, bit, other = my_place(plan)
    barrier = pltpu.get_barrier_semaphore()
    partners = ring_partners(plan, me)
    for p in partners:
        pl.semaphore_signal(barrier, inc=1, device_id=(p,), device_id_type=MESH)
    pl.semaphore_wait(barrier, len(partners))
    scatter = Scatter(plan, bit, other, send, recv)
    parts = []
    for i, (src, at, wide, split, turn) in enumerate([
        (g_small, 0, SMALL, False, 0), (g_in, 0, width, True, 0), (g_in, width, width, True, 1), (g_in, 2 * width, width, True, 2),
        (g_out, 0, width, True, 0), (g_up, 0, width, True, 1), (g_down, 0, width, True, 2),
    ]):
        parts.append(dict(i=i, src=src, slots=slots[i], at=at, width=wide, split=split, turn=turn,
                          sum=sums[i], last=lasts[i - 1] if split else None))
    for part in parts:
        scatter.start(part, 0)
    for phase in range(plan.chip_bits + 2):
        for part in parts:
            if phase < scatter.phases(part):
                scatter.advance(part, phase)
    outs = [o_small, o_in, o_in, o_in, o_out, o_up, o_down]
    for part, out in zip(parts, outs):
        scatter.finish(part, out)
    total = sum(jnp.sum(o[...] * o[...]) for o in (o_small, o_in, o_out, o_up, o_down))
    o_norm[...] = jnp.sqrt(norm_exchange(plan, me, bit, total, mine, boxes, nsend, nrecv))


def scatter_call(plan, grads, width):
    g_in, g_out, g_up, g_down, g_small = grads
    rows = g_in.shape[0] // plan.count
    vm = pl.BlockSpec(memory_space=pltpu.VMEM)
    shaped = [g.reshape(plan.dims + (2 * rows, g.shape[-1])) for g in grads]
    slots = lambda c: [pltpu.VMEM(plan.dims[j:] + (2 * rows, c), BF) for j in range(plan.chip_bits + 1)]
    half = width // 2
    scratch = slots(SMALL)
    for _ in range(6):
        scratch += slots(half)
    scratch += [pltpu.VMEM((2 * rows, SMALL), F32)] + [pltpu.VMEM((2 * rows, half), F32)] * 6
    scratch += [pltpu.VMEM((rows, half), F32)] * 6
    scratch += [pltpu.SemaphoreType.DMA((7, plan.chip_bits + 2))] * 2
    low = 1 << min(3, plan.bits)
    boxes = low - 1 + plan.count // low - 1
    scratch += [pltpu.VMEM((8, LANES), F32), pltpu.VMEM((boxes, 8, LANES), F32)]
    scratch += [pltpu.SemaphoreType.DMA((boxes,))] * 2
    shard = lambda c: jax.ShapeDtypeStruct((rows, c), F32)
    return pl.pallas_call(
        functools.partial(scatter_kernel, plan=plan, width=width),
        in_specs=[vm] * 5,
        out_specs=[vm] * 6,
        out_shape=[shard(3 * width), shard(width), shard(width), shard(width), shard(SMALL),
                   jax.ShapeDtypeStruct((8, LANES), F32)],
        scratch_shapes=scratch,
        compiler_params=pltpu.CompilerParams(
            collective_id=1, has_side_effects=True, vmem_limit_bytes=VMEM_LIMIT
        ),
        name="scatter",
    )(*shaped)


def update_kernel(
    steps, rates, norm, g_in, g_out, g_up, g_down, g_small, *refs,
):
    states, outs, norm_o = refs[:18], refs[18:42], refs[42]
    norm_o[0, 0] = norm[0, 0]
    total = norm[0:1, 0:1]
    factor = jnp.minimum(1.0, CLIP_LIMIT / (total + NORM_EPS))
    t = jnp.full((1, 1), steps[0].astype(F32), F32)
    rate = rates[0]
    fix_one = 1.0 / (1.0 - jnp.exp(t * math.log(BETA_ONE)))
    fix_two = 1.0 / (1.0 - jnp.exp(t * math.log(BETA_TWO)))
    small = g_small[...]
    turned = jnp.concatenate([small, jnp.zeros((LANES - small.shape[0], SMALL), F32)], 0).T
    vec = turned[32:43, : small.shape[0]]
    vec = jnp.concatenate([vec[2:, :], vec[:2, :]], 0)
    grads = (g_in[...], g_out[...], g_up[...], g_down[...], small[:, :32], vec)
    for i, g in enumerate(grads):
        master, first, second = (states[3 * i + j][...] for j in range(3))
        g = g * factor
        first = BETA_ONE * first + (1.0 - BETA_ONE) * g
        second = BETA_TWO * second + (1.0 - BETA_TWO) * g * g
        change = first * fix_one / (jnp.sqrt(second * fix_two) + ADAM_EPS)
        if i < 5:
            change = change + DECAY_RATE * master
        for j, v in enumerate((g, first, second, master - rate * change)):
            outs[4 * i + j][...] = v


def update_call(step_count, learn_rate, norm, grads, states):
    vm, sm = pl.BlockSpec(memory_space=pltpu.VMEM), pl.BlockSpec(memory_space=pltpu.SMEM)
    shapes = [jax.ShapeDtypeStruct(states[3 * i].shape, F32) for i in range(6) for _ in range(4)]
    return pl.pallas_call(
        update_kernel,
        in_specs=[sm, sm] + [vm] * 24,
        out_specs=[vm] * 24 + [sm],
        out_shape=shapes + [jax.ShapeDtypeStruct((1, 1), F32)],
        compiler_params=pltpu.CompilerParams(vmem_limit_bytes=VMEM_LIMIT),
        name="update",
    )(step_count.reshape(1), learn_rate.reshape(1), norm, *grads, *states)


def body(
    count,
    tokens, eigvecs, counts, endpoints, cotangent,
    attend_in, attend_in_first, attend_in_second,
    attend_out, attend_out_first, attend_out_second,
    feed_up, feed_up_first, feed_up_second,
    feed_down, feed_down_first, feed_down_second,
    label_in, label_in_first, label_in_second,
    vectors, vectors_first, vectors_second,
    step_count, learn_rate,
):
    shard, width = feed_up.shape
    small_shard = jnp.concatenate(
        [label_in.T, vectors[9:].T, vectors[:9].T, jnp.zeros((shard, SMALL - 43), F32)], 1
    )
    shards = (attend_in, attend_out.T, feed_up, feed_down.T, small_shard)
    paired = Plan.fits(count, shard)
    if paired:
        plan = Plan(count)
        weights = gather_call(plan, shards, width)
    else:
        weights = [lax.all_gather(v.astype(BF), "dp", axis=0, tiled=True) for v in shards]
    out, tg, *grads = layer(
        tokens, jnp.swapaxes(eigvecs, 1, 2), counts.T, jnp.swapaxes(endpoints, 1, 2), cotangent, *weights, MOLS_STEP,
    )
    if paired:
        *sums, norm = scatter_call(plan, grads, width)
    else:
        sums = [lax.psum_scatter(v.astype(F32), "dp", scatter_dimension=0, tiled=True) for v in grads]
        squares = lax.psum(sum(jnp.sum(v * v) for v in sums), "dp")
        norm = jnp.full((8, LANES), jnp.sqrt(squares), F32)
    states = (
        attend_in, attend_in_first, attend_in_second,
        attend_out.T, attend_out_first.T, attend_out_second.T,
        feed_up, feed_up_first, feed_up_second,
        feed_down.T, feed_down_first.T, feed_down_second.T,
        label_in.T, label_in_first.T, label_in_second.T,
        vectors, vectors_first, vectors_second,
    )
    *new, norm = update_call(step_count, learn_rate, norm, sums, states)
    new = [v.T if i // 4 in (1, 3, 4) else v for i, v in enumerate(new)]
    return (out, tg, norm.reshape(()), *new)


MOLS_STEP = 2


def solution(mesh):
    rows, cols = P("dp", None), P(None, "dp")
    state = (rows,) * 3 + (cols,) * 3 + (rows,) * 3 + (cols,) * 9
    placed = (rows, P("dp", None, None), rows, P("dp", None, None), rows) + state + (P(), P())
    results = (rows,) * 4 + (cols,) * 4 + (rows,) * 4 + (cols,) * 12
    return jax.shard_map(
        functools.partial(body, mesh.shape["dp"]),
        mesh=mesh, in_specs=placed, out_specs=(rows, rows, P()) + results, check_vma=False,
    )
```

```python
import functools
import math

import jax
import jax.numpy as jnp
from jax import lax
from jax.experimental import pallas as pl
from jax.experimental.pallas import tpu as pltpu
from jax.sharding import PartitionSpec as P

HEADS = 32
EPS_NORM = 1e-05
MASK_FILL = -1e30
SQRT_HALF = 0.7071067811865476
INV_SQRT_TWO_PI = 0.3989422804014327
BETA_ONE = 0.9
BETA_TWO = 0.999
ADAM_EPS = 1e-08
DECAY_RATE = 0.01
CLIP_LIMIT = 1.0
NORM_EPS = 1e-06
LOG2E = 1.4426950408889634

BF = jnp.bfloat16
F32 = jnp.float32
MESH = pl.DeviceIdType.MESH
LANES = 128
VMEM_LIMIT = 60 << 20

SMALL = 128
NODE, EDGE = 32, 33
GAIN1, SHIFT1, QBIAS, VBIAS, OBIAS, GAIN2, SHIFT2, UBIAS, DBIAS = range(34, 43)


def nn(a, b):
    return lax.dot_general(a, b, (((1,), (0,)), ((), ())), preferred_element_type=F32)


def nt(a, b):
    return lax.dot_general(a, b, (((1,), (1,)), ((), ())), preferred_element_type=F32)


def tn(a, b):
    return lax.dot_general(a, b, (((0,), (0,)), ((), ())), preferred_element_type=F32)


def layer_stats(values):
    centred = values - jnp.mean(values, -1, keepdims=True)
    recip_std = lax.rsqrt(jnp.mean(centred * centred, -1, keepdims=True) + EPS_NORM)
    return centred * recip_std, recip_std


def norm_back(grad_out, normed, recip_std, gain_row):
    scaled = grad_out * gain_row
    return recip_std * (
        scaled
        - jnp.mean(scaled, -1, keepdims=True)
        - normed * jnp.mean(scaled * normed, -1, keepdims=True)
    )


class Heads:
    def __init__(self, width):
        self.dim = width // HEADS
        span = 1
        while (span * self.dim) % LANES:
            span *= 2
        self.block = span
        self.tiles = span * self.dim // LANES
        self.blocks = HEADS // span

    def first(self, head):
        return head * self.dim // LANES

    def last(self, head):
        return ((head + 1) * self.dim - 1) // LANES

    def heads_of(self, tile):
        return [h for h in range(self.block) if self.first(h) <= tile <= self.last(h)]

    def slot(self, tile, head):
        return sum(len(self.heads_of(t)) for t in range(tile)) + head - self.heads_of(tile)[0]

    def slots(self):
        return sum(len(self.heads_of(t)) for t in range(self.tiles))

    def mask(self, tile, head):
        lane = lax.broadcasted_iota(jnp.int32, (1, LANES), 1) + tile * LANES
        inside = jnp.logical_and(lane >= head * self.dim, lane < (head + 1) * self.dim)
        return inside.astype(F32).astype(BF)


def masked(value, mask):
    rows = value.shape[0]
    return (value.reshape(rows // 16, 16, LANES) * mask[None]).reshape(rows, LANES)


def set_masks(hd, masks):
    for t in range(hd.tiles):
        for h in hd.heads_of(t):
            masks[hd.slot(t, h)] = jnp.broadcast_to(hd.mask(t, h), (16, LANES))


def across(parts):
    return parts[0] if len(parts) == 1 else jnp.concatenate(parts, 1)


def pair_rows(hd, masks, tiles_of, pair):
    h0, h1 = 2 * pair, 2 * pair + 1
    lo, hi = hd.first(h0), hd.last(h1)
    rows = []
    for h in (h0, h1):
        parts = []
        for t in range(lo, hi + 1):
            if hd.first(h) <= t <= hd.last(h):
                parts.append(masked(tiles_of[t], masks[hd.slot(t, h)]))
            else:
                parts.append(jnp.zeros_like(tiles_of[t]))
        rows.append(across(parts))
    return jnp.concatenate(rows, 0)


def pair_full(hd, tiles_of, pair):
    return across([tiles_of[t] for t in range(hd.first(2 * pair), hd.last(2 * pair + 1) + 1)])


def tile_rows(hd, masks, tile_value, tile):
    return jnp.concatenate([masked(tile_value, masks[hd.slot(tile, h)]) for h in hd.heads_of(tile)], 0)


class Plan:
    def __init__(self, count):
        self.count = count
        self.bits = count.bit_length() - 1
        self.chip_bits = self.bits - 1
        self.dims = (2,) * self.chip_bits
        near = list(range(1, min(4, self.bits)))
        self.far = list(range(self.bits - 1, near[-1], -1))
        self.turns = [near[i:] + near[:i] for i in range(len(near))]

    def order(self, part):
        return self.far + self.turns[part % len(self.turns)]

    @staticmethod
    def fits(count, rows):
        return count >= 16 and count & (count - 1) == 0 and rows % 8 == 0


def my_place(plan):
    me = lax.axis_index("dp")
    bit = [lax.rem(lax.div(me, jnp.int32(1 << b)), jnp.int32(2)) for b in range(plan.bits)]
    other = [me + (1 - 2 * bit[b]) * (1 << b) for b in range(plan.bits)]
    return me, bit, other


def greet(plan, other):
    barrier = pltpu.get_barrier_semaphore()
    for b in range(plan.bits):
        pl.semaphore_signal(barrier, inc=1, device_id=(other[b],), device_id_type=MESH)
    pl.semaphore_wait(barrier, plan.bits)


class Gather:
    def __init__(self, plan, bit, other, send, recv):
        self.plan, self.bit, self.other, self.send, self.recv = plan, bit, other, send, recv

    def cols(self, part, mine):
        buf, src, stage, at, width = part["buf"], part["src"], part["stage"], part["at"], part["width"]
        if not part["split"]:
            return pl.ds(at, width)
        half = width // 2
        which = self.bit[0] if mine else 1 - self.bit[0]
        return pl.ds(pl.multiple_of(at + which * half, LANES), half)

    def copy(self, part, phase):
        plan, i = self.plan, part["i"]
        if phase == 0:
            cols = self.cols(part, False)
            src, dst, to = part["src"].at[:, cols], part["stage"], self.other[0]
        elif phase <= plan.chip_bits:
            order = plan.order(part["turn"])
            done, b = order[: phase - 1], order[phase - 1]
            idx = tuple(
                slice(None) if bb in done else self.bit[bb] for bb in range(plan.bits - 1, 0, -1)
            )
            ref = part["buf"].at[idx + (slice(None), self.cols(part, True))]
            src, dst, to = ref, ref, self.other[b]
        else:
            ref = part["buf"].at[(slice(None),) * (plan.chip_bits + 1) + (self.cols(part, True),)]
            src, dst, to = ref, ref, self.other[0]
        return pltpu.make_async_remote_copy(
            src_ref=src, dst_ref=dst, send_sem=self.send.at[i, phase], recv_sem=self.recv.at[i, phase],
            device_id=(to,), device_id_type=MESH,
        )

    def phases(self, part):
        return self.plan.chip_bits + (2 if part["split"] else 1)

    def start(self, part, phase):
        self.copy(part, phase).start()

    def wait(self, part, phase):
        self.copy(part, phase).wait()
        if phase == 0:
            cols = self.cols(part, True)
            own, got = part["src"][:, cols], part["stage"][...]
            lower = self.bit[0] == 0
            rows = jnp.concatenate([jnp.where(lower, own, got), jnp.where(lower, got, own)], 0)
            idx = tuple(self.bit[bb] for bb in range(self.plan.bits - 1, 0, -1))
            part["buf"][idx + (slice(None), cols)] = rows.astype(BF)

    def advance(self, part, phase):
        self.wait(part, phase)
        if phase + 1 < self.phases(part):
            self.start(part, phase + 1)


class Scatter:
    def __init__(self, plan, bit, other, send, recv):
        self.plan, self.bit, self.other, self.send, self.recv = plan, bit, other, send, recv

    def cols(self, part, mine):
        half = part["width"] // 2
        which = self.bit[0] if mine else 1 - self.bit[0]
        return pl.ds(pl.multiple_of(part["at"] + which * half, LANES), half)

    def order(self, part):
        return self.plan.order(part["turn"])[::-1]

    def index(self, part, phase, mine):
        done, b = self.order(part)[: phase - 1], self.order(part)[phase - 1]
        idx = []
        for bb in range(self.plan.bits - 1, 0, -1):
            if bb in done:
                continue
            idx.append((self.bit[b] if mine else 1 - self.bit[b]) if bb == b else slice(None))
        return tuple(idx)

    def rows(self, which):
        r = self.plan_rows
        return pl.ds(pl.multiple_of(which * r, 8), r)

    def copy(self, part, phase):
        plan, i = self.plan, part["i"]
        every = (slice(None),) * (plan.chip_bits + 1)
        if phase == 0:
            if part["split"]:
                src = part["src"].at[every + (self.cols(part, False),)]
            else:
                src = part["src"]
            dst, to = part["slots"][0], self.other[0]
        elif phase <= plan.chip_bits:
            src = part["slots"][phase - 1].at[self.index(part, phase, False)]
            dst, to = part["slots"][phase], self.other[self.order(part)[phase - 1]]
        else:
            r = part["sum"].shape[0] // 2
            src = part["sum"].at[pl.ds(pl.multiple_of((1 - self.bit[0]) * r, 8), r)]
            dst, to = part["last"], self.other[0]
        return pltpu.make_async_remote_copy(
            src_ref=src, dst_ref=dst, send_sem=self.send.at[i, phase], recv_sem=self.recv.at[i, phase],
            device_id=(to,), device_id_type=MESH,
        )

    def phases(self, part):
        return self.plan.chip_bits + (2 if part["split"] else 1)

    def start(self, part, phase):
        self.copy(part, phase).start()

    def wait(self, part, phase):
        plan = self.plan
        self.copy(part, phase).wait()
        every = (slice(None),) * (plan.chip_bits + 1)
        if phase > plan.chip_bits:
            return
        slot = part["slots"][phase]
        if phase == 0:
            if part["split"]:
                mine = part["src"][every + (self.cols(part, True),)]
            else:
                mine = part["src"][...]
        else:
            mine = part["slots"][phase - 1][self.index(part, phase, True)]
        total = mine.astype(F32) + slot[...].astype(F32)
        if phase == plan.chip_bits:
            part["sum"][...] = total
        else:
            slot[...] = total.astype(BF)

    def advance(self, part, phase):
        self.wait(part, phase)
        if phase + 1 < self.phases(part):
            self.start(part, phase + 1)

    def finish(self, part, out):
        r = part["sum"].shape[0] // 2
        own = part["sum"][pl.ds(pl.multiple_of(self.bit[0] * r, 8), r), :]
        if not part["split"]:
            out[...] = own
            return
        half = part["width"] // 2
        out[:, self.cols(part, True)] = own
        out[:, self.cols(part, False)] = part["last"][...]


def norm_exchange(plan, me, bit, squares, mine, boxes, send, recv):
    low = 1 << min(3, plan.bits)
    value = jnp.full((8, LANES), squares, F32)
    base = 0
    for span, stride in ((low, 1), (plan.count // low, low)):
        if span == 1:
            continue
        place = lax.rem(lax.div(me, jnp.int32(stride)), jnp.int32(span))
        mine[...] = value
        copies = []
        for d in range(1, span):
            to_place = lax.rem(place + d, jnp.int32(span))
            to = me + (to_place - place) * stride
            copies.append(pltpu.make_async_remote_copy(
                src_ref=mine, dst_ref=boxes.at[base + d - 1], send_sem=send.at[base + d - 1],
                recv_sem=recv.at[base + d - 1], device_id=(to,), device_id_type=MESH,
            ))
        for c in copies:
            c.start()
        for c in copies:
            c.wait()
        for d in range(1, span):
            value = value + boxes[base + d - 1]
        base += span - 1
    return value


def ring_partners(plan, me):
    low = 1 << min(3, plan.bits)
    found = []
    for span, stride in ((low, 1), (plan.count // low, low)):
        place = lax.rem(lax.div(me, jnp.int32(stride)), jnp.int32(span))
        for d in range(1, span):
            found.append(me + (lax.rem(place + d, jnp.int32(span)) - place) * stride)
    return found


def mat(ref, *cols):
    value = ref[(slice(None),) * (len(ref.shape) - 1) + cols] if cols else ref[...]
    return value.reshape(-1, value.shape[-1])


def front_kernel(*refs, plan, hd, mols, wide, seq, steps, steps2):
    refs = list(refs)
    take = lambda k: [refs.pop(0) for _ in range(k)]
    counts, tokens, eig, ends, cot = take(5)
    shards = take(5)
    out_o, proj_o, lse_o, dmid_o, dmix_o, labt_o, gout_o, gup_o, gdown_o, gvec_o, smallt_o, emb_o, inp_o, win_o = take(14)
    w_in, w_out, w_up, w_down, small = take(5)
    stages = take(7)
    small_t, masks, tok_s, emb_s, inp_s, mixed_s, p_buf, acc_out, acc_up, acc_down, acc_vec = take(11)
    send, recv, keep = take(3)
    s_in, s_out, s_up, s_down, s_small = shards
    step = pl.program_id(0)
    width = w_out.shape[-1]
    across_tiles = width // LANES
    score = hd.dim ** -0.5
    rows_all = mols * seq
    me, bit, other = my_place(plan)
    gather = Gather(plan, bit, other, send, recv)
    make = lambda i, src, buf, at, wide, split, t: dict(
        i=i, src=src, buf=buf, stage=stages[i], at=at, width=wide, split=split, turn=t
    )
    early = [
        make(0, s_small, small, 0, SMALL, False, 0),
        make(1, s_in, w_in, 0, width, True, 0),
        make(2, s_in, w_in, width, width, True, 1),
        make(3, s_in, w_in, 2 * width, width, True, 2),
    ]
    late = [
        make(4, s_out, w_out, 0, width, True, 0),
        make(5, s_up, w_up, 0, width, True, 1),
        make(6, s_down, w_down, 0, width, True, 2),
    ]
    final = plan.chip_bits + 1
    kept = [pltpu.make_async_copy(a, b, keep.at[i]) for i, (a, b) in enumerate(((w_in, win_o), (emb_s, emb_o), (inp_s, inp_o)))]
    get_tokens = pltpu.make_async_copy(tokens, tok_s, keep.at[3])

    row = lambda i: small_t[i : i + 1, :]

    def embed(group, carry):
        iota0 = lax.broadcasted_iota(jnp.int32, (seq, seq), 0)
        iota1 = lax.broadcasted_iota(jnp.int32, (seq, seq), 1)
        token_row = lax.broadcasted_iota(jnp.int32, (1, seq), 1)
        kind_row = lax.broadcasted_iota(jnp.int32, (16, seq), 0)
        one = lambda c: c.astype(F32).astype(BF)
        label_rows = []
        for g in range(mols):
            m = group * mols + g
            nodes = counts[0, m]
            live = nodes + counts[1, m]
            eig_f = eig[m]
            shift = one(jnp.logical_and(iota1 - iota0 == nodes, iota1 < live))
            picks = jnp.concatenate([one(iota0 == ends[m, end : end + 1, :]) for end in range(2)], 1)
            edge_lab = nn(eig_f.astype(BF), picks).astype(BF)
            moved = nn(jnp.concatenate([edge_lab[:, :seq], edge_lab[:, seq:]], 0), shift)
            at_node = token_row < nodes
            is_node = at_node.astype(F32)
            is_edge = jnp.logical_and(token_row >= nodes, token_row < live).astype(F32)
            kind = jnp.where(kind_row == 0, is_node, jnp.where(kind_row == 1, is_edge, 0.0))
            lab = jnp.concatenate(
                [jnp.where(at_node, eig_f, moved[:16]), jnp.where(at_node, eig_f, moved[16:]), kind], 0
            )
            labt_o[m] = lab.astype(BF)
            pad = jnp.zeros((SMALL - lab.shape[0], seq), F32)
            label_rows.append(jnp.concatenate([lab, pad], 0).T.astype(BF))
        labels = jnp.concatenate(label_rows, 0)
        here = pl.ds(pl.multiple_of(group * rows_all, rows_all), rows_all)
        embedded = tok_s[here, :].astype(F32) + nn(labels, small_t[...].astype(BF))
        emb_s[here, :] = embedded
        normed, _ = layer_stats(embedded)
        value = (normed * row(GAIN1) + row(SHIFT1)).astype(BF)
        for t in range(across_tiles):
            inp_s[t, here, :] = value[:, t * LANES : (t + 1) * LANES]
        return carry

    @pl.when(step == 0)
    def _():
        get_tokens.start()
        greet(plan, other)
        for part in early + late:
            gather.start(part, 0)
        set_masks(hd, masks)
        acc_out[...] = jnp.zeros_like(acc_out)
        acc_up[...] = jnp.zeros_like(acc_up)
        acc_down[...] = jnp.zeros_like(acc_down)
        acc_vec[...] = jnp.zeros_like(acc_vec)
        for phase in range(final):
            for part in early:
                if part["split"] and phase == final - 1:
                    continue
                gather.advance(part, phase)
        small_t[...] = mat(small).astype(F32).T
        smallt_o[...] = small_t[...]
        get_tokens.wait()
        cut = (steps + 1) // 2
        lax.fori_loop(0, cut, embed, 0)
        for part in early[1:]:
            gather.advance(part, final - 1)
        lax.fori_loop(cut, steps, embed, 0)
        for part in early[1:]:
            gather.advance(part, final)
        for part in late:
            gather.advance(part, 0)
        for copy in kept:
            copy.start()

    @pl.when(step < steps)
    def _():
        here = pl.ds(pl.multiple_of(step * rows_all, rows_all), rows_all)
        input_one = across([inp_s[t, here, :] for t in range(across_tiles)])
        for part in range(3):
            value = nn(input_one, mat(w_in, slice(part * width, (part + 1) * width)))
            if part == 0:
                value = value + row(QBIAS)
            if part == 2:
                value = value + row(VBIAS)
            value = value.astype(BF)
            for t in range(across_tiles):
                proj_o[part * across_tiles + t] = value[:, t * LANES : (t + 1) * LANES]

        for m in range(mols):
            nodes = counts[0, step * mols + m]
            live = nodes + counts[1, step * mols + m]
            key_live = lax.broadcasted_iota(jnp.int32, (seq, 2 * seq), 0) < live
            rows = slice(m * seq, (m + 1) * seq)
            for b in range(hd.blocks):
                get = lambda part: [proj_o[part * across_tiles + b * hd.tiles + t, rows, :] for t in range(hd.tiles)]
                q, k, v = get(0), get(1), get(2)
                for pair in range(hd.block // 2):
                    scores = nt(pair_full(hd, k, pair), pair_rows(hd, masks, q, pair))
                    scores = jnp.where(key_live, scores, MASK_FILL)
                    top = jnp.max(scores, 0, keepdims=True)
                    ex = jnp.exp2((scores - top) * (score * LOG2E))
                    total = jnp.sum(ex, 0, keepdims=True)
                    shares = (ex * (1.0 / total)).astype(BF)
                    at = b * (hd.block // 2) + pair
                    lse_o[m, at : at + 1, :] = top + jnp.log2(total) * (1.0 / (score * LOG2E))
                    for i in range(2):
                        p_buf[b * hd.block + 2 * pair + i] = shares[:, i * seq : (i + 1) * seq].T
                for t in range(hd.tiles):
                    hs = hd.heads_of(t)
                    mixed = nn(across([p_buf[b * hd.block + h] for h in hs]), tile_rows(hd, masks, v[t], t))
                    put = pl.ds(pl.multiple_of(step * rows_all + m * seq, seq), seq)
                    mixed_s[b * hd.tiles + t, put, :] = mixed.astype(BF)

    for phase in range(1, final + 1):
        @pl.when(step == min((1, 2, 4, 6)[min(phase, 4) - 1] + max(phase - 4, 0), steps - 1))
        def _():
            for part in late:
                gather.advance(part, phase)

    @pl.when(step >= steps)
    def _():
        here = pl.ds(pl.multiple_of((step - steps) * wide, wide), wide)
        mixed = across([mixed_s[t, here, :] for t in range(across_tiles)])
        middle = emb_s[here, :] + (nt(mixed, mat(w_out)) + row(OBIAS))
        normed2, recip2 = layer_stats(middle)
        input_two = (normed2 * row(GAIN2) + row(SHIFT2)).astype(BF)
        pre = nn(input_two, mat(w_up)) + row(UBIAS)
        half_erf = 0.5 * (1.0 + lax.erf(pre * SQRT_HALF))
        act = (pre * half_erf).astype(BF)
        slope = half_erf + pre * jnp.exp(-0.5 * pre * pre) * INV_SQRT_TWO_PI
        out_o[...] = (middle + (nt(act, mat(w_down)) + row(DBIAS))).astype(BF)
        back = cot[...]
        back_f = back.astype(F32)
        d_pre = (nn(back, mat(w_down)) * slope).astype(BF)
        acc_down[...] += tn(back, act)
        acc_up[...] += tn(input_two, d_pre)
        d_in2 = nt(d_pre, mat(w_up))
        d_mid = back_f + norm_back(d_in2, normed2, recip2, row(GAIN2))
        dmid_o[...] = d_mid
        branch = d_mid.astype(BF)
        acc_out[...] += tn(branch, mixed)
        d_mixed = nn(branch, mat(w_out)).astype(BF)
        for t in range(across_tiles):
            dmix_o[t] = d_mixed[:, t * LANES : (t + 1) * LANES]
        add = lambda v: jnp.sum(v, 0, keepdims=True)
        sums = {
            OBIAS: add(branch.astype(F32)),
            GAIN2: add(d_in2 * normed2),
            SHIFT2: add(d_in2),
            UBIAS: add(d_pre.astype(F32)),
            DBIAS: add(back_f),
        }
        for i, v in sums.items():
            acc_vec[i - 34 : i - 33, :] += v

    @pl.when(step == steps + steps2 - 1)
    def _():
        for acc, out in ((acc_out, gout_o), (acc_up, gup_o), (acc_down, gdown_o)):
            out[...] = acc[...].astype(BF)
        gvec_o[...] = acc_vec[...]
        for copy in kept:
            copy.wait()


class ShareSmall:
    def __init__(self, plan, me, src, boxes, part, boxes2, send, recv):
        self.src, self.boxes, self.part, self.boxes2 = src, boxes, part, boxes2
        low = src.shape[1]
        high = plan.count // low
        self.place, self.level = lax.rem(me, jnp.int32(low)), lax.div(me, jnp.int32(low))
        self.one, self.two = [], []
        for d in range(1, low):
            to = lax.rem(self.place + d, jnp.int32(low))
            self.one.append(pltpu.make_async_remote_copy(
                src_ref=src.at[:, to], dst_ref=boxes.at[d - 1], send_sem=send.at[d - 1], recv_sem=recv.at[d - 1],
                device_id=(me + to - self.place,), device_id_type=MESH,
            ))
        for d in range(1, high):
            to = lax.rem(self.level + d, jnp.int32(high))
            at = low - 2 + d
            self.two.append(pltpu.make_async_remote_copy(
                src_ref=part.at[to], dst_ref=boxes2.at[d - 1], send_sem=send.at[at], recv_sem=recv.at[at],
                device_id=(me + (to - self.level) * low,), device_id_type=MESH,
            ))

    def begin(self):
        for c in self.one:
            c.start()

    def middle(self):
        total = self.src[:, self.place]
        for d, c in enumerate(self.one):
            c.wait()
            total = total + self.boxes[d]
        self.part[...] = total
        for c in self.two:
            c.start()

    def end(self):
        total = self.part[self.level]
        for d, c in enumerate(self.two):
            c.wait()
            total = total + self.boxes2[d]
        return total


def back_kernel(*refs, plan, hd, mols, wide, seq, steps, steps2):
    refs = list(refs)
    take = lambda k: [refs.pop(0) for _ in range(k)]
    counts, proj, lse, inp, emb, dmid, dmix, labt, w_in, small_t, gvec, g_out, g_up, g_down = take(14)
    tg_o, o_in, o_out, o_up, o_down, o_small, o_norm = take(7)
    masks, pt_buf, dst_buf, ds_buf, dproj_s, acc_in, g_in, acc_vec, acc_lab = take(9)
    k = plan.chip_bits + 1
    slots = [take(k) for _ in range(6)]
    part_sums, lasts = take(6), take(6)
    send, recv = take(2)
    small_s, small_box, small_part, small_box2, ssend, srecv = take(6)
    mine, boxes, nsend, nrecv = take(4)
    step = pl.program_id(0)
    width = g_out.shape[-1]
    across_tiles = width // LANES
    score = hd.dim ** -0.5
    rows_all = mols * seq
    me, bit, other = my_place(plan)
    scatter = Scatter(plan, bit, other, send, recv)
    parts = []
    for i, (src, at, t) in enumerate([
        (g_in, 0, 0), (g_in, width, 1), (g_in, 2 * width, 2), (g_out, 0, 0), (g_up, 0, 1), (g_down, 0, 2),
    ]):
        parts.append(dict(i=i, src=src, slots=slots[i], at=at, width=width, split=True, turn=t,
                          sum=part_sums[i], last=lasts[i]))
    late, early = parts[:3], parts[3:]
    final = plan.chip_bits + 1

    @pl.when(step == 0)
    def _():
        barrier = pltpu.get_barrier_semaphore()
        partners = ring_partners(plan, me)
        for p in partners:
            pl.semaphore_signal(barrier, inc=1, device_id=(p,), device_id_type=MESH)
        pl.semaphore_wait(barrier, len(partners))
        for part in early:
            scatter.start(part, 0)
        set_masks(hd, masks)
        acc_in[...] = jnp.zeros_like(acc_in)
        acc_vec[...] = gvec[...]
        acc_lab[...] = jnp.zeros_like(acc_lab)

    row = lambda i: small_t[i : i + 1, :]

    @pl.when(step < steps)
    def _():
        here = pl.ds(pl.multiple_of(step * rows_all, rows_all), rows_all)
        for m in range(mols):
            nodes = counts[0, step * mols + m]
            live = nodes + counts[1, step * mols + m]
            key_live = lax.broadcasted_iota(jnp.int32, (seq, 2 * seq), 0) < live
            rows = slice(m * seq, (m + 1) * seq)
            put = pl.ds(pl.multiple_of(step * rows_all + m * seq, seq), seq)
            for b in range(hd.blocks):
                get = lambda ref, part: [ref[part * across_tiles + b * hd.tiles + t, rows, :] for t in range(hd.tiles)]
                q, k, v, do = get(proj, 0), get(proj, 1), get(proj, 2), get(dmix, 0)
                for pair in range(hd.block // 2):
                    scores = nt(pair_full(hd, k, pair), pair_rows(hd, masks, q, pair))
                    scores = jnp.where(key_live, scores, MASK_FILL)
                    at = b * (hd.block // 2) + pair
                    p = jnp.exp2((scores - lse[m, at : at + 1, :]) * (score * LOG2E))
                    dp = nt(pair_full(hd, v, pair), pair_rows(hd, masks, do, pair))
                    inner = jnp.sum(p * dp, 0, keepdims=True)
                    ds = (p * (dp - inner)).astype(BF)
                    p = p.astype(BF)
                    for i in range(2):
                        h = b * hd.block + 2 * pair + i
                        pt_buf[h] = p[:, i * seq : (i + 1) * seq]
                        dst_buf[h] = ds[:, i * seq : (i + 1) * seq]
                        ds_buf[h] = ds[:, i * seq : (i + 1) * seq].T
                for t in range(hd.tiles):
                    hs = [b * hd.block + h for h in hd.heads_of(t)]
                    at = b * hd.tiles + t
                    d_v = nn(across([pt_buf[h] for h in hs]), tile_rows(hd, masks, do[t], t))
                    d_k = nn(across([dst_buf[h] for h in hs]), tile_rows(hd, masks, q[t], t)) * score
                    d_q = nn(across([ds_buf[h] for h in hs]), tile_rows(hd, masks, k[t], t)) * score
                    dproj_s[at, put, :] = d_q.astype(BF)
                    dproj_s[across_tiles + at, put, :] = d_k.astype(BF)
                    dproj_s[2 * across_tiles + at, put, :] = d_v.astype(BF)
        input_one = across([inp[t] for t in range(across_tiles)])
        d_proj = across([dproj_s[t, here, :] for t in range(3 * across_tiles)])
        acc_in[...] += tn(input_one, d_proj)
        add = lambda v: jnp.sum(v, 0, keepdims=True)
        acc_vec[QBIAS - 34 : QBIAS - 33, :] += add(d_proj[:, :width].astype(F32))
        acc_vec[VBIAS - 34 : VBIAS - 33, :] += add(d_proj[:, 2 * width :].astype(F32))

    for phase in range(final + 1):
        @pl.when(step == min((0, 2, 3, 4)[min(phase, 3)] + 2 * max(phase - 3, 0), steps - 1))
        def _():
            for part in early:
                scatter.advance(part, phase)

    @pl.when(step == steps - 1)
    def _():
        for part in late:
            cols = slice(part["at"], part["at"] + width)
            g_in[(slice(None),) * (plan.chip_bits + 1) + (cols,)] = acc_in[:, cols].astype(BF).reshape(
                g_in.shape[:-1] + (width,)
            )
            scatter.start(part, 0)

    @pl.when(step >= steps)
    def _():
        here = pl.ds(pl.multiple_of((step - steps) * wide, wide), wide)
        normed, recip = layer_stats(emb[...])
        d_proj = across([dproj_s[t, here, :] for t in range(3 * across_tiles)])
        d_in1 = nt(d_proj, mat(w_in))
        tg = dmid[...] + norm_back(d_in1, normed, recip, row(GAIN1))
        tg_o[...] = tg
        tg_hi = tg.astype(BF)
        tg_lo = (tg - tg_hi.astype(F32)).astype(BF)
        lab = jnp.concatenate([labt[m] for m in range(wide // seq)], 1)
        acc_lab[...] += nn(lab, tg_hi)
        acc_lab[32:48, :] += nn(lab[32:48, :], tg_lo)
        add = lambda v: jnp.sum(v, 0, keepdims=True)
        acc_vec[GAIN1 - 34 : GAIN1 - 33, :] += add(d_in1 * normed)
        acc_vec[SHIFT1 - 34 : SHIFT1 - 33, :] += add(d_in1)

    for phase in range(min(final, steps2 - 1)):
        @pl.when(step == steps + phase)
        def _():
            for part in late:
                scatter.advance(part, phase)

    @pl.when(step == steps + steps2 - 1)
    def _():
        full = jnp.concatenate(
            [acc_lab[0:32, :], acc_lab[32:34, :], acc_vec[0:9, :], jnp.zeros((SMALL - 43, width), F32)], 0
        )
        small_s[...] = full.T.reshape(small_s.shape)
        share = ShareSmall(plan, me, small_s, small_box, small_part, small_box2, ssend, srecv)
        share.begin()
        for phase in range(min(final, steps2 - 1), final + 1):
            for part in late:
                scatter.advance(part, phase)
            if phase == final - 1:
                share.middle()
        o_small[...] = share.end()
        for part, out in zip(parts, (o_in, o_in, o_in, o_out, o_up, o_down)):
            scatter.finish(part, out)
        total = sum(jnp.sum(o[...] * o[...]) for o in (o_small, o_in, o_out, o_up, o_down))
        o_norm[...] = jnp.sqrt(norm_exchange(plan, me, bit, total, mine, boxes, nsend, nrecv))


def paired_layer(plan, tokens, eig_t, counts_t, ends_t, cot, shards, mols_step):
    count, width = tokens.shape
    mols_all, lap, seq = eig_t.shape
    shard = shards[0].shape[0]
    hd = Heads(width)
    steps = mols_all // mols_step
    rows = mols_step * seq
    wide = min(WIDE, count)
    steps2 = count // wide
    across_tiles = width // LANES
    last = steps - 1
    first = lambda i: lax.min(i, last)
    second = lambda i: lax.max(i - steps, 0)
    tok2 = lambda w: pl.BlockSpec((wide, w), lambda i: (second(i), 0))
    mol = lambda a, b: pl.BlockSpec((mols_step, a, b), lambda i: (first(i), 0, 0))
    tiled = lambda n: pl.BlockSpec((n, rows, LANES), lambda i: (0, first(i), 0))
    tiled2 = lambda n: pl.BlockSpec((n, wide, LANES), lambda i: (0, second(i), 0))
    sizes = dict(plan=plan, hd=hd, mols=mols_step, wide=wide, seq=seq, steps=steps, steps2=steps2)
    vm, sm, hbm = (pl.BlockSpec(memory_space=m) for m in (pltpu.VMEM, pltpu.SMEM, pl.ANY))
    sq = (width, width)
    buf = lambda c: plan.dims + (2 * shard, c)
    f32 = lambda *shape: jax.ShapeDtypeStruct(shape, F32)
    bf = lambda *shape: jax.ShapeDtypeStruct(shape, BF)
    params = lambda cid: pltpu.CompilerParams(
        vmem_limit_bytes=VMEM_LIMIT, dimension_semantics=("arbitrary",), collective_id=cid,
        has_side_effects=True,
    )
    half = width // 2
    out, proj, lse, dmid, dmix, labt, g_out, g_up, g_down, g_vec, small_t, emb, inp, w_in = pl.pallas_call(
        functools.partial(front_kernel, **sizes),
        grid=(steps + steps2,),
        in_specs=[sm, hbm, vm, vm, tok2(width)] + [vm] * 5,
        out_specs=[tok2(width), tiled(3 * across_tiles), mol(HEADS // 2, 2 * seq), tok2(width), tiled2(across_tiles)]
        + [vm] * 6 + [hbm] * 3,
        out_shape=[bf(count, width), bf(3 * across_tiles, count, LANES), f32(mols_all, HEADS // 2, 2 * seq),
                   f32(count, width), bf(across_tiles, count, LANES), bf(mols_all, 48, seq),
                   bf(*sq), bf(*sq), bf(*sq), f32(16, width), f32(SMALL, width),
                   f32(count, width), bf(across_tiles, count, LANES), bf(*buf(3 * width))],
        scratch_shapes=[pltpu.VMEM(buf(c), BF) for c in (3 * width, width, width, width, SMALL)]
        + [pltpu.VMEM((shard, SMALL), F32)] + [pltpu.VMEM((shard, half), F32)] * 6
        + [
            pltpu.VMEM((SMALL, width), F32),
            pltpu.VMEM((hd.slots(), 16, LANES), BF),
            pltpu.VMEM((count, width), BF),
            pltpu.VMEM((count, width), F32),
            pltpu.VMEM((across_tiles, count, LANES), BF),
            pltpu.VMEM((across_tiles, count, LANES), BF),
            pltpu.VMEM((HEADS, seq, seq), BF),
            pltpu.VMEM(sq, F32), pltpu.VMEM(sq, F32), pltpu.VMEM(sq, F32),
            pltpu.VMEM((16, width), F32),
        ]
        + [pltpu.SemaphoreType.DMA((7, plan.chip_bits + 2))] * 2 + [pltpu.SemaphoreType.DMA((4,))],
        compiler_params=params(0),
        name="front",
    )(counts_t, tokens, eig_t, ends_t, cot, *shards)

    low = 1 << min(3, plan.bits)
    high = plan.count // low
    boxes = low - 1 + high - 1
    slots = [pltpu.VMEM(plan.dims[j:] + (2 * shard, half), BF) for j in range(plan.chip_bits + 1)]
    shaped = [g.reshape(buf(width)) for g in (g_out, g_up, g_down)]
    tg, *sums, norm = pl.pallas_call(
        functools.partial(back_kernel, **sizes),
        grid=(steps + steps2,),
        in_specs=[sm, tiled(3 * across_tiles), mol(HEADS // 2, 2 * seq), tiled(across_tiles), tok2(width), tok2(width),
                  tiled(across_tiles), pl.BlockSpec((wide // seq, 48, seq), lambda i: (second(i), 0, 0))] + [vm] * 6,
        out_specs=[tok2(width)] + [vm] * 6,
        out_shape=[f32(count, width), f32(shard, 3 * width), f32(shard, width), f32(shard, width), f32(shard, width),
                   f32(shard, SMALL), f32(8, LANES)],
        scratch_shapes=[
            pltpu.VMEM((hd.slots(), 16, LANES), BF),
            pltpu.VMEM((HEADS, seq, seq), BF),
            pltpu.VMEM((HEADS, seq, seq), BF),
            pltpu.VMEM((HEADS, seq, seq), BF),
            pltpu.VMEM((3 * across_tiles, count, LANES), BF),
            pltpu.VMEM((width, 3 * width), F32),
            pltpu.VMEM(buf(3 * width), BF),
            pltpu.VMEM((16, width), F32),
            pltpu.VMEM((48, width), F32),
        ]
        + slots * 6
        + [pltpu.VMEM((2 * shard, half), F32)] * 6 + [pltpu.VMEM((shard, half), F32)] * 6
        + [pltpu.SemaphoreType.DMA((6, plan.chip_bits + 2))] * 2
        + [
            pltpu.VMEM((high, low, shard, SMALL), F32),
            pltpu.VMEM((low - 1, high, shard, SMALL), F32),
            pltpu.VMEM((high, shard, SMALL), F32),
            pltpu.VMEM((max(high - 1, 1), shard, SMALL), F32),
        ]
        + [pltpu.SemaphoreType.DMA((boxes,))] * 2
        + [pltpu.VMEM((8, LANES), F32), pltpu.VMEM((boxes, 8, LANES), F32)]
        + [pltpu.SemaphoreType.DMA((boxes,))] * 2,
        compiler_params=params(1),
        name="back",
    )(counts_t, proj, lse, inp, emb, dmid, dmix, labt, w_in, small_t, g_vec, *shaped)
    return out, tg, sums, norm


def plain_front_kernel(
    counts, tokens, eig, ends, cot, w_in, w_out, w_up, w_down, small,
    out_o, proj_o, lse_o, emb_o, dmid_o, dmix_o, labt_o, gout_o, gup_o, gdown_o, gvec_o,
    small_t, masks, mixed_s, p_buf, acc_out, acc_up, acc_down, acc_vec,
    *, hd, mols, seq, steps,
):
    step = pl.program_id(0)
    width = w_in.shape[0]
    across_tiles = width // LANES
    score = hd.dim ** -0.5

    @pl.when(step == 0)
    def _():
        small_t[...] = small[...].astype(F32).T
        set_masks(hd, masks)
        acc_out[...] = jnp.zeros_like(acc_out)
        acc_up[...] = jnp.zeros_like(acc_up)
        acc_down[...] = jnp.zeros_like(acc_down)
        acc_vec[...] = jnp.zeros_like(acc_vec)

    row = lambda i: small_t[i : i + 1, :]
    iota0 = lax.broadcasted_iota(jnp.int32, (seq, seq), 0)
    iota1 = lax.broadcasted_iota(jnp.int32, (seq, seq), 1)
    token_row = lax.broadcasted_iota(jnp.int32, (1, seq), 1)
    one = lambda c: c.astype(F32).astype(BF)
    label_rows = []
    for m in range(mols):
        nodes = counts[0, step * mols + m]
        live = nodes + counts[1, step * mols + m]
        eig_f = eig[m]
        eig_low = eig_f.astype(BF)
        shift = one(jnp.logical_and(iota1 - iota0 == nodes, iota1 < live))
        halves = []
        for end in range(2):
            pick = one(iota0 == ends[m, end : end + 1, :])
            edge_lab = nn(eig_low, pick).astype(BF)
            moved = nn(edge_lab, shift)
            halves.append(jnp.where(token_row < nodes, eig_f, moved))
        is_node = (token_row < nodes).astype(F32)
        is_edge = jnp.logical_and(token_row >= nodes, token_row < live).astype(F32)
        kind = jnp.where(lax.broadcasted_iota(jnp.int32, (16, seq), 0) == 0, is_node,
                         jnp.where(lax.broadcasted_iota(jnp.int32, (16, seq), 0) == 1, is_edge, 0.0))
        lab = jnp.concatenate(halves + [kind], 0)
        labt_o[m] = lab.astype(BF)
        pad = jnp.zeros((SMALL - lab.shape[0], seq), F32)
        label_rows.append(jnp.concatenate([lab, pad], 0).T.astype(BF))
    labels = jnp.concatenate(label_rows, 0)
    embedded = tokens[...].astype(F32) + nn(labels, small_t[...].astype(BF))
    emb_o[...] = embedded
    normed, recip = layer_stats(embedded)
    input_one = (normed * row(GAIN1) + row(SHIFT1)).astype(BF)
    for part in range(3):
        cols = slice(part * width, (part + 1) * width)
        value = nn(input_one, w_in[:, cols])
        if part == 0:
            value = value + row(QBIAS)
        if part == 2:
            value = value + row(VBIAS)
        value = value.astype(BF)
        for t in range(across_tiles):
            proj_o[part * across_tiles + t] = value[:, t * LANES : (t + 1) * LANES]

    for m in range(mols):
        nodes = counts[0, step * mols + m]
        live = nodes + counts[1, step * mols + m]
        key_live = lax.broadcasted_iota(jnp.int32, (seq, 2 * seq), 0) < live
        rows = slice(m * seq, (m + 1) * seq)
        for b in range(hd.blocks):
            base = b * hd.tiles * LANES
            get = lambda part: [proj_o[part * across_tiles + b * hd.tiles + t, rows, :] for t in range(hd.tiles)]
            q, k, v = get(0), get(1), get(2)
            for pair in range(hd.block // 2):
                scores = nt(pair_full(hd, k, pair), pair_rows(hd, masks, q, pair))
                scores = jnp.where(key_live, scores, MASK_FILL)
                top = jnp.max(scores, 0, keepdims=True)
                ex = jnp.exp2((scores - top) * (score * LOG2E))
                total = jnp.sum(ex, 0, keepdims=True)
                shares = (ex * (1.0 / total)).astype(BF)
                lse_o[m, b * (hd.block // 2) + pair : b * (hd.block // 2) + pair + 1, :] = (
                    top + jnp.log2(total) * (1.0 / (score * LOG2E))
                )
                for i in range(2):
                    h = 2 * pair + i
                    p_buf[b * hd.block + h] = shares[:, i * seq : (i + 1) * seq].T
            for t in range(hd.tiles):
                hs = hd.heads_of(t)
                mixed = nn(across([p_buf[b * hd.block + h] for h in hs]), tile_rows(hd, masks, v[t], t))
                mixed_s[b * hd.tiles + t, rows, :] = mixed.astype(BF)

    mixed = across([mixed_s[t] for t in range(across_tiles)])
    middle = embedded + (nt(mixed, w_out[...]) + row(OBIAS))
    normed2, recip2 = layer_stats(middle)
    input_two = (normed2 * row(GAIN2) + row(SHIFT2)).astype(BF)
    pre = nn(input_two, w_up[...]) + row(UBIAS)
    half_erf = 0.5 * (1.0 + lax.erf(pre * SQRT_HALF))
    act = (pre * half_erf).astype(BF)
    slope = half_erf + pre * jnp.exp(-0.5 * pre * pre) * INV_SQRT_TWO_PI
    out_o[...] = (middle + (nt(act, w_down[...]) + row(DBIAS))).astype(BF)
    back = cot[...]
    back_f = back.astype(F32)
    d_pre_f = nn(back, w_down[...]) * slope
    d_pre = d_pre_f.astype(BF)
    acc_down[...] += tn(back, act)
    acc_up[...] += tn(input_two, d_pre)
    d_in2 = nt(d_pre, w_up[...])
    d_mid = back_f + norm_back(d_in2, normed2, recip2, row(GAIN2))
    dmid_o[...] = d_mid
    branch = d_mid.astype(BF)
    acc_out[...] += tn(branch, mixed)
    d_mixed = nn(branch, w_out[...]).astype(BF)
    for t in range(across_tiles):
        dmix_o[t] = d_mixed[:, t * LANES : (t + 1) * LANES]
    add = lambda v: jnp.sum(v, 0, keepdims=True)
    sums = {
        OBIAS: add(branch.astype(F32)),
        GAIN2: add(d_in2 * normed2),
        SHIFT2: add(d_in2),
        UBIAS: add(d_pre.astype(F32)),
        DBIAS: add(back_f),
    }
    for i, v in sums.items():
        acc_vec[i - 34 : i - 33, :] += v

    @pl.when(step == steps - 1)
    def _():
        gout_o[...] = acc_out[...].astype(BF)
        gup_o[...] = acc_up[...].astype(BF)
        gdown_o[...] = acc_down[...].astype(BF)
        gvec_o[...] = acc_vec[...]


def plain_back_kernel(
    counts, proj, lse, emb, dmid, dmix, labt, w_in, small, gvec,
    tg_o, gin_o, gsmall_o,
    small_t, masks, pt_buf, dst_buf, ds_buf, dproj_s, acc_in, acc_vec, acc_lab,
    *, hd, mols, seq, steps,
):
    step = pl.program_id(0)
    width = w_in.shape[0]
    across_tiles = width // LANES
    score = hd.dim ** -0.5

    @pl.when(step == 0)
    def _():
        small_t[...] = small[...].astype(F32).T
        set_masks(hd, masks)
        acc_in[...] = jnp.zeros_like(acc_in)
        acc_vec[...] = gvec[...]
        acc_lab[...] = jnp.zeros_like(acc_lab)

    row = lambda i: small_t[i : i + 1, :]
    for m in range(mols):
        nodes = counts[0, step * mols + m]
        live = nodes + counts[1, step * mols + m]
        key_live = lax.broadcasted_iota(jnp.int32, (seq, 2 * seq), 0) < live
        rows = slice(m * seq, (m + 1) * seq)
        for b in range(hd.blocks):
            base = b * hd.tiles * LANES
            get = lambda ref, part: [ref[part * across_tiles + b * hd.tiles + t, rows, :] for t in range(hd.tiles)]
            q, k, v, do = get(proj, 0), get(proj, 1), get(proj, 2), get(dmix, 0)
            for pair in range(hd.block // 2):
                scores = nt(pair_full(hd, k, pair), pair_rows(hd, masks, q, pair))
                scores = jnp.where(key_live, scores, MASK_FILL)
                at = b * (hd.block // 2) + pair
                p = jnp.exp2((scores - lse[m, at : at + 1, :]) * (score * LOG2E))
                dp = nt(pair_full(hd, v, pair), pair_rows(hd, masks, do, pair))
                inner = jnp.sum(p * dp, 0, keepdims=True)
                ds = (p * (dp - inner)).astype(BF)
                p = p.astype(BF)
                for i in range(2):
                    h = b * hd.block + 2 * pair + i
                    pt_buf[h] = p[:, i * seq : (i + 1) * seq]
                    dst_buf[h] = ds[:, i * seq : (i + 1) * seq]
                    ds_buf[h] = ds[:, i * seq : (i + 1) * seq].T
            for t in range(hd.tiles):
                hs = [b * hd.block + h for h in hd.heads_of(t)]
                at = b * hd.tiles + t
                d_v = nn(across([pt_buf[h] for h in hs]), tile_rows(hd, masks, do[t], t))
                d_k = nn(across([dst_buf[h] for h in hs]), tile_rows(hd, masks, q[t], t)) * score
                d_q = nn(across([ds_buf[h] for h in hs]), tile_rows(hd, masks, k[t], t)) * score
                dproj_s[at, rows, :] = d_q.astype(BF)
                dproj_s[across_tiles + at, rows, :] = d_k.astype(BF)
                dproj_s[2 * across_tiles + at, rows, :] = d_v.astype(BF)

    normed, recip = layer_stats(emb[...])
    input_one = (normed * row(GAIN1) + row(SHIFT1)).astype(BF)
    d_proj = across([dproj_s[t] for t in range(3 * across_tiles)])
    acc_in[...] += tn(input_one, d_proj)
    d_in1 = nt(d_proj, w_in[...])
    tg = dmid[...] + norm_back(d_in1, normed, recip, row(GAIN1))
    tg_o[...] = tg
    tg_hi = tg.astype(BF)
    tg_lo = (tg - tg_hi.astype(F32)).astype(BF)
    lab = jnp.concatenate([labt[m] for m in range(mols)], 1)
    acc_lab[...] += nn(lab, tg_hi)
    acc_lab[32:48, :] += nn(lab[32:48, :], tg_lo)
    add = lambda v: jnp.sum(v, 0, keepdims=True)
    sums = {
        GAIN1: add(d_in1 * normed),
        SHIFT1: add(d_in1),
        QBIAS: add(d_proj[:, :width].astype(F32)),
        VBIAS: add(d_proj[:, 2 * width :].astype(F32)),
    }
    for i, v in sums.items():
        acc_vec[i - 34 : i - 33, :] += v

    @pl.when(step == steps - 1)
    def _():
        gin_o[...] = acc_in[...].astype(BF)
        full = jnp.concatenate(
            [acc_lab[0:32, :], acc_lab[32:34, :], acc_vec[0:9, :], jnp.zeros((SMALL - 43, width), F32)], 0
        )
        gsmall_o[...] = full.T.astype(BF)


def whole(shape):
    return pl.BlockSpec(shape, lambda *_: (0,) * len(shape), pipeline_mode=pl.Buffered(1))


def out_whole(shape):
    return pl.BlockSpec(shape, lambda *_: (0,) * len(shape))


def plain_layer(tokens, eig_t, counts_t, ends_t, cot, w_in, w_out, w_up, w_down, small, mols_step):
    count, width = tokens.shape
    mols_all, lap, seq = eig_t.shape
    hd = Heads(width)
    steps = mols_all // mols_step
    rows = mols_step * seq
    tok = lambda w: pl.BlockSpec((rows, w), lambda i, *_: (i, 0))
    tiled = lambda n: pl.BlockSpec((n, rows, LANES), lambda i, *_: (0, i, 0))
    across_tiles = width // LANES
    mol = lambda a, b: pl.BlockSpec((mols_step, a, b), lambda i, *_: (i, 0, 0))
    params = pltpu.CompilerParams(vmem_limit_bytes=VMEM_LIMIT, dimension_semantics=("arbitrary",))
    sq = (width, width)
    front = pl.pallas_call(
        functools.partial(plain_front_kernel, hd=hd, mols=mols_step, seq=seq, steps=steps),
        grid_spec=pltpu.PrefetchScalarGridSpec(
            num_scalar_prefetch=1,
            grid=(steps,),
            in_specs=[tok(width), mol(lap, seq), mol(2, seq), tok(width), whole((width, 3 * width)),
                      whole(sq), whole(sq), whole(sq), whole((width, SMALL))],
            out_specs=[tok(width), tiled(3 * across_tiles), mol(HEADS // 2, 2 * seq), tok(width), tok(width), tiled(across_tiles),
                       mol(48, seq), out_whole(sq), out_whole(sq), out_whole(sq), out_whole((16, width))],
            scratch_shapes=[
                pltpu.VMEM((SMALL, width), F32),
                pltpu.VMEM((hd.slots(), 16, LANES), BF),
                pltpu.VMEM((across_tiles, rows, LANES), BF),
                pltpu.VMEM((HEADS, seq, seq), BF),
                pltpu.VMEM(sq, F32), pltpu.VMEM(sq, F32), pltpu.VMEM(sq, F32),
                pltpu.VMEM((16, width), F32),
            ],
        ),
        out_shape=[
            jax.ShapeDtypeStruct((count, width), BF),
            jax.ShapeDtypeStruct((3 * across_tiles, count, LANES), BF),
            jax.ShapeDtypeStruct((mols_all, HEADS // 2, 2 * seq), F32),
            jax.ShapeDtypeStruct((count, width), F32),
            jax.ShapeDtypeStruct((count, width), F32),
            jax.ShapeDtypeStruct((across_tiles, count, LANES), BF),
            jax.ShapeDtypeStruct((mols_all, 48, seq), BF),
            jax.ShapeDtypeStruct(sq, BF),
            jax.ShapeDtypeStruct(sq, BF),
            jax.ShapeDtypeStruct(sq, BF),
            jax.ShapeDtypeStruct((16, width), F32),
        ],
        compiler_params=params,
        name="plain_front",
    )(counts_t, tokens, eig_t, ends_t, cot, w_in, w_out, w_up, w_down, small)
    out, proj, lse, emb, dmid, dmix, labt, g_out, g_up, g_down, g_vec = front
    tg, g_in, g_small = pl.pallas_call(
        functools.partial(plain_back_kernel, hd=hd, mols=mols_step, seq=seq, steps=steps),
        grid_spec=pltpu.PrefetchScalarGridSpec(
            num_scalar_prefetch=1,
            grid=(steps,),
            in_specs=[tiled(3 * across_tiles), mol(HEADS // 2, 2 * seq), tok(width), tok(width), tiled(across_tiles), mol(48, seq),
                      whole((width, 3 * width)), whole((width, SMALL)), whole((16, width))],
            out_specs=[tok(width), out_whole((width, 3 * width)), out_whole((width, SMALL))],
            scratch_shapes=[
                pltpu.VMEM((SMALL, width), F32),
                pltpu.VMEM((hd.slots(), 16, LANES), BF),
                pltpu.VMEM((HEADS, seq, seq), BF),
                pltpu.VMEM((HEADS, seq, seq), BF),
                pltpu.VMEM((HEADS, seq, seq), BF),
                pltpu.VMEM((3 * across_tiles, rows, LANES), BF),
                pltpu.VMEM((width, 3 * width), F32),
                pltpu.VMEM((16, width), F32),
                pltpu.VMEM((48, width), F32),
            ],
        ),
        out_shape=[
            jax.ShapeDtypeStruct((count, width), F32),
            jax.ShapeDtypeStruct((width, 3 * width), BF),
            jax.ShapeDtypeStruct((width, SMALL), BF),
        ],
        compiler_params=params,
        name="plain_back",
    )(counts_t, proj, lse, emb, dmid, dmix, labt, w_in, small, g_vec)
    return out, tg, g_in, g_out, g_up, g_down, g_small


def update_kernel(
    steps, rates, large_a, large_b, norm, g_in, g_out, g_up, g_down, g_small, *refs,
):
    states, outs, norm_o = refs[:18], refs[18:42], refs[42]
    moves = []
    for i, (source, target, stay) in enumerate(((large_b, refs[44], refs[46]), (large_a, refs[43], refs[45]))):
        size = source.shape[0] // MOVES
        for j in range(MOVES):
            part = pl.ds(j * size, size)
            moves.append((
                pltpu.make_async_copy(source.at[part], stay.at[part], refs[47].at[2 * (MOVES * i + j)]),
                pltpu.make_async_copy(stay.at[part], target.at[part], refs[47].at[2 * (MOVES * i + j) + 1]),
            ))
    for load, _ in moves:
        load.start()
    for load, store in moves:
        load.wait()
        store.start()
    norm_o[0, 0] = norm[0, 0]
    total = norm[0:1, 0:1]
    factor = jnp.minimum(1.0, CLIP_LIMIT / (total + NORM_EPS))
    t = jnp.full((1, 1), steps[0].astype(F32), F32)
    rate = rates[0]
    fix_one = 1.0 / (1.0 - jnp.exp(t * math.log(BETA_ONE)))
    fix_two = 1.0 / (1.0 - jnp.exp(t * math.log(BETA_TWO)))
    small = g_small[...]
    turned = jnp.concatenate([small, jnp.zeros((LANES - small.shape[0], SMALL), F32)], 0).T
    vec = turned[32:43, : small.shape[0]]
    vec = jnp.concatenate([vec[2:, :], vec[:2, :]], 0)
    grads = (g_in[...], g_out[...], g_up[...], g_down[...], small[:, :32], vec)
    for i, g in enumerate(grads):
        master, first, second = (states[3 * i + j][...] for j in range(3))
        g = g * factor
        first = BETA_ONE * first + (1.0 - BETA_ONE) * g
        second = BETA_TWO * second + (1.0 - BETA_TWO) * g * g
        change = first * fix_one / (jnp.sqrt(second * fix_two) + ADAM_EPS)
        if i < 5:
            change = change + DECAY_RATE * master
        for j, v in enumerate((g, first, second, master - rate * change)):
            outs[4 * i + j][...] = v
    for _, store in moves:
        store.wait()


def update_call(step_count, learn_rate, large, norm, grads, states):
    vm, sm, hbm = (pl.BlockSpec(memory_space=m) for m in (pltpu.VMEM, pltpu.SMEM, pl.ANY))
    shapes = [jax.ShapeDtypeStruct(states[3 * i].shape, F32) for i in range(6) for _ in range(4)]
    return pl.pallas_call(
        update_kernel,
        in_specs=[sm, sm, hbm, hbm] + [vm] * 24,
        out_specs=[vm] * 24 + [sm, hbm, hbm],
        out_shape=shapes + [jax.ShapeDtypeStruct((1, 1), F32)] + [jax.ShapeDtypeStruct(v.shape, v.dtype) for v in large],
        scratch_shapes=[pltpu.VMEM(v.shape, v.dtype) for v in large] + [pltpu.SemaphoreType.DMA((4 * MOVES,))],
        compiler_params=pltpu.CompilerParams(vmem_limit_bytes=VMEM_LIMIT),
        name="update",
    )(step_count.reshape(1), learn_rate.reshape(1), *large, norm, *grads, *states)


def body(
    count,
    tokens, eigvecs, counts, endpoints, cotangent,
    attend_in, attend_in_first, attend_in_second,
    attend_out, attend_out_first, attend_out_second,
    feed_up, feed_up_first, feed_up_second,
    feed_down, feed_down_first, feed_down_second,
    label_in, label_in_first, label_in_second,
    vectors, vectors_first, vectors_second,
    step_count, learn_rate,
):
    shard, width = feed_up.shape
    small_shard = jnp.concatenate(
        [label_in.T, vectors[9:].T, vectors[:9].T, jnp.zeros((shard, SMALL - 43), F32)], 1
    )
    shards = (attend_in, attend_out.T, feed_up, feed_down.T, small_shard)
    arrays = (tokens, jnp.swapaxes(eigvecs, 1, 2), counts.T, jnp.swapaxes(endpoints, 1, 2), cotangent)
    if Plan.fits(count, shard):
        out, tg, sums, norm = paired_layer(Plan(count), *arrays, shards, MOLS_STEP)
    else:
        weights = [lax.all_gather(v.astype(BF), "dp", axis=0, tiled=True) for v in shards]
        out, tg, *grads = plain_layer(*arrays, *weights, MOLS_STEP)
        sums = [lax.psum_scatter(v.astype(F32), "dp", scatter_dimension=0, tiled=True) for v in grads]
        squares = lax.psum(sum(jnp.sum(v * v) for v in sums), "dp")
        norm = jnp.full((8, LANES), jnp.sqrt(squares), F32)
    states = (
        attend_in, attend_in_first, attend_in_second,
        attend_out.T, attend_out_first.T, attend_out_second.T,
        feed_up, feed_up_first, feed_up_second,
        feed_down.T, feed_down_first.T, feed_down_second.T,
        label_in.T, label_in_first.T, label_in_second.T,
        vectors, vectors_first, vectors_second,
    )
    *new, norm, out, tg = update_call(step_count, learn_rate, (out, tg), norm, sums, states)
    new = [v.T if i // 4 in (1, 3, 4) else v for i, v in enumerate(new)]
    return (out, tg, norm.reshape(()), *new)


MOLS_STEP = 2
WIDE = 512
MOVES = 8


def solution(mesh):
    rows, cols = P("dp", None), P(None, "dp")
    state = (rows,) * 3 + (cols,) * 3 + (rows,) * 3 + (cols,) * 9
    placed = (rows, P("dp", None, None), rows, P("dp", None, None), rows) + state + (P(), P())
    results = (rows,) * 4 + (cols,) * 4 + (rows,) * 4 + (cols,) * 12
    return jax.shard_map(
        functools.partial(body, mesh.shape["dp"]),
        mesh=mesh, in_specs=placed, out_specs=(rows, rows, P()) + results, check_vma=False,
    )
```

```python
import functools
import math

import jax
import jax.numpy as jnp
from jax import lax
from jax.experimental import pallas as pl
from jax.experimental.pallas import tpu as pltpu
from jax.sharding import PartitionSpec as P

HEADS = 32
EPS_NORM = 1e-05
MASK_FILL = -1e30
SQRT_HALF = 0.7071067811865476
INV_SQRT_TWO_PI = 0.3989422804014327
BETA_ONE = 0.9
BETA_TWO = 0.999
ADAM_EPS = 1e-08
DECAY_RATE = 0.01
CLIP_LIMIT = 1.0
NORM_EPS = 1e-06
LOG2E = 1.4426950408889634

BF = jnp.bfloat16
F32 = jnp.float32
MESH = pl.DeviceIdType.MESH
LANES = 128
VMEM_LIMIT = 60 << 20

SMALL = 128
NODE, EDGE = 32, 33
GAIN1, SHIFT1, QBIAS, VBIAS, OBIAS, GAIN2, SHIFT2, UBIAS, DBIAS = range(34, 43)


def nn(a, b):
    return lax.dot_general(a, b, (((1,), (0,)), ((), ())), preferred_element_type=F32)


def nt(a, b):
    return lax.dot_general(a, b, (((1,), (1,)), ((), ())), preferred_element_type=F32)


def tn(a, b):
    return lax.dot_general(a, b, (((0,), (0,)), ((), ())), preferred_element_type=F32)


def layer_stats(values):
    centred = values - jnp.mean(values, -1, keepdims=True)
    recip_std = lax.rsqrt(jnp.mean(centred * centred, -1, keepdims=True) + EPS_NORM)
    return centred * recip_std, recip_std


def norm_back(grad_out, normed, recip_std, gain_row):
    scaled = grad_out * gain_row
    return recip_std * (
        scaled
        - jnp.mean(scaled, -1, keepdims=True)
        - normed * jnp.mean(scaled * normed, -1, keepdims=True)
    )


class Heads:
    def __init__(self, width):
        self.dim = width // HEADS
        span = 1
        while (span * self.dim) % LANES:
            span *= 2
        self.block = span
        self.tiles = span * self.dim // LANES
        self.blocks = HEADS // span

    def first(self, head):
        return head * self.dim // LANES

    def last(self, head):
        return ((head + 1) * self.dim - 1) // LANES

    def heads_of(self, tile):
        return [h for h in range(self.block) if self.first(h) <= tile <= self.last(h)]

    def slot(self, tile, head):
        return sum(len(self.heads_of(t)) for t in range(tile)) + head - self.heads_of(tile)[0]

    def slots(self):
        return sum(len(self.heads_of(t)) for t in range(self.tiles))

    def mask(self, tile, head):
        lane = lax.broadcasted_iota(jnp.int32, (1, LANES), 1) + tile * LANES
        inside = jnp.logical_and(lane >= head * self.dim, lane < (head + 1) * self.dim)
        return inside.astype(F32).astype(BF)


def masked(value, mask):
    rows = value.shape[0]
    return (value.reshape(rows // 16, 16, LANES) * mask[None]).reshape(rows, LANES)


def dense(value):
    return value.astype(F32).astype(BF)


def set_masks(hd, masks):
    for t in range(hd.tiles):
        for h in hd.heads_of(t):
            masks[hd.slot(t, h)] = jnp.broadcast_to(hd.mask(t, h), (16, LANES))


def across(parts):
    return parts[0] if len(parts) == 1 else jnp.concatenate(parts, 1)


def pair_rows(hd, masks, tiles_of, pair):
    h0, h1 = 2 * pair, 2 * pair + 1
    lo, hi = hd.first(h0), hd.last(h1)
    rows = []
    for h in (h0, h1):
        parts = []
        for t in range(lo, hi + 1):
            if hd.first(h) <= t <= hd.last(h):
                parts.append(masked(tiles_of[t], masks[hd.slot(t, h)]))
            else:
                parts.append(jnp.zeros_like(tiles_of[t]))
        rows.append(across(parts))
    return jnp.concatenate(rows, 0)


def pair_full(hd, tiles_of, pair):
    return across([tiles_of[t] for t in range(hd.first(2 * pair), hd.last(2 * pair + 1) + 1)])


def tile_rows(hd, masks, tile_value, tile):
    return jnp.concatenate([masked(tile_value, masks[hd.slot(tile, h)]) for h in hd.heads_of(tile)], 0)


def units(width):
    unit = 2 * LANES
    return [(at, unit) for at in range(0, width, unit)]


class Plan:
    def __init__(self, count):
        self.count = count
        self.bits = count.bit_length() - 1
        self.chip_bits = self.bits - 1
        self.dims = (2,) * self.chip_bits
        near = list(range(1, min(4, self.bits)))
        self.far = list(range(self.bits - 1, near[-1], -1))
        self.turns = [near[i:] + near[:i] for i in range(len(near))]

    def order(self, part):
        return self.far + self.turns[part % len(self.turns)]

    @staticmethod
    def fits(count, rows):
        return count >= 16 and count & (count - 1) == 0 and rows % 8 == 0


def my_place(plan):
    me = lax.axis_index("dp")
    bit = [lax.rem(lax.div(me, jnp.int32(1 << b)), jnp.int32(2)) for b in range(plan.bits)]
    other = [me + (1 - 2 * bit[b]) * (1 << b) for b in range(plan.bits)]
    return me, bit, other


def greet(plan, other):
    barrier = pltpu.get_barrier_semaphore()
    for b in range(plan.bits):
        pl.semaphore_signal(barrier, inc=1, device_id=(other[b],), device_id_type=MESH)
    pl.semaphore_wait(barrier, plan.bits)


class Gather:
    def __init__(self, plan, bit, other, send, recv):
        self.plan, self.bit, self.other, self.send, self.recv = plan, bit, other, send, recv

    def cols(self, part, mine):
        buf, src, stage, at, width = part["buf"], part["src"], part["stage"], part["at"], part["width"]
        if not part["split"]:
            return pl.ds(at, width)
        half = width // 2
        which = self.bit[0] if mine else 1 - self.bit[0]
        return pl.ds(pl.multiple_of(at + which * half, LANES), half)

    def copy(self, part, phase):
        plan, i = self.plan, part["i"]
        if phase == 0:
            cols = self.cols(part, False)
            src, dst, to = part["src"].at[:, cols], part["stage"], self.other[0]
        elif phase <= plan.chip_bits:
            order = plan.order(part["turn"])
            done, b = order[: phase - 1], order[phase - 1]
            idx = tuple(
                slice(None) if bb in done else self.bit[bb] for bb in range(plan.bits - 1, 0, -1)
            )
            ref = part["buf"].at[idx + (slice(None), self.cols(part, True))]
            src, dst, to = ref, ref, self.other[b]
        else:
            ref = part["buf"].at[(slice(None),) * (plan.chip_bits + 1) + (self.cols(part, True),)]
            src, dst, to = ref, ref, self.other[0]
        return pltpu.make_async_remote_copy(
            src_ref=src, dst_ref=dst, send_sem=self.send.at[i, phase], recv_sem=self.recv.at[i, phase],
            device_id=(to,), device_id_type=MESH,
        )

    def phases(self, part):
        return self.plan.chip_bits + (2 if part["split"] else 1)

    def start(self, part, phase):
        self.copy(part, phase).start()

    def wait(self, part, phase):
        self.copy(part, phase).wait()
        if phase == 0:
            cols = self.cols(part, True)
            own, got = part["src"][:, cols], part["stage"][...]
            lower = self.bit[0] == 0
            rows = jnp.concatenate([jnp.where(lower, own, got), jnp.where(lower, got, own)], 0)
            idx = tuple(self.bit[bb] for bb in range(self.plan.bits - 1, 0, -1))
            part["buf"][idx + (slice(None), cols)] = rows.astype(BF)

    def advance(self, part, phase):
        self.wait(part, phase)
        if phase + 1 < self.phases(part):
            self.start(part, phase + 1)


class Scatter:
    def __init__(self, plan, bit, other, send, recv):
        self.plan, self.bit, self.other, self.send, self.recv = plan, bit, other, send, recv

    def cols(self, part, mine):
        half = part["width"] // 2
        which = self.bit[0] if mine else 1 - self.bit[0]
        return pl.ds(pl.multiple_of(part["at"] + which * half, LANES), half)

    def order(self, part):
        return self.plan.order(part["turn"])[::-1]

    def index(self, part, phase, mine):
        done, b = self.order(part)[: phase - 1], self.order(part)[phase - 1]
        idx = []
        for bb in range(self.plan.bits - 1, 0, -1):
            if bb in done:
                continue
            idx.append((self.bit[b] if mine else 1 - self.bit[b]) if bb == b else slice(None))
        return tuple(idx)

    def rows(self, which):
        r = self.plan_rows
        return pl.ds(pl.multiple_of(which * r, 8), r)

    def copy(self, part, phase):
        plan, i = self.plan, part["i"]
        every = (slice(None),) * (plan.chip_bits + 1)
        if phase == 0:
            if part["split"]:
                src = part["src"].at[every + (self.cols(part, False),)]
            else:
                src = part["src"]
            dst, to = part["slots"][0], self.other[0]
        elif phase <= plan.chip_bits:
            src = part["slots"][phase - 1].at[self.index(part, phase, False)]
            dst, to = part["slots"][phase], self.other[self.order(part)[phase - 1]]
        else:
            r = part["sum"].shape[0] // 2
            src = part["sum"].at[pl.ds(pl.multiple_of((1 - self.bit[0]) * r, 8), r)]
            dst, to = part["last"], self.other[0]
        return pltpu.make_async_remote_copy(
            src_ref=src, dst_ref=dst, send_sem=self.send.at[i, phase], recv_sem=self.recv.at[i, phase],
            device_id=(to,), device_id_type=MESH,
        )

    def phases(self, part):
        return self.plan.chip_bits + (2 if part["split"] else 1)

    def start(self, part, phase):
        self.copy(part, phase).start()

    def wait(self, part, phase):
        plan = self.plan
        self.copy(part, phase).wait()
        every = (slice(None),) * (plan.chip_bits + 1)
        if phase > plan.chip_bits:
            return
        slot = part["slots"][phase]
        if phase == 0:
            if part["split"]:
                mine = part["src"][every + (self.cols(part, True),)]
            else:
                mine = part["src"][...]
        else:
            mine = part["slots"][phase - 1][self.index(part, phase, True)]
        if phase == plan.chip_bits:
            part["sum"][...] = mine.astype(F32) + slot[...].astype(F32)
        else:
            slot[...] = mine + slot[...]

    def advance(self, part, phase):
        self.wait(part, phase)
        if phase + 1 < self.phases(part):
            self.start(part, phase + 1)

    def finish(self, part, out):
        r = part["sum"].shape[0] // 2
        own = part["sum"][pl.ds(pl.multiple_of(self.bit[0] * r, 8), r), :]
        if not part["split"]:
            out[...] = own
            return
        half = part["width"] // 2
        out[:, self.cols(part, True)] = own
        out[:, self.cols(part, False)] = part["last"][...]


def norm_exchange(plan, me, squares, mine, boxes, send, recv):
    mine[...] = jnp.full((8, LANES), squares, F32)
    copies = []
    for d in range(1, plan.count):
        copies.append(pltpu.make_async_remote_copy(
            src_ref=mine, dst_ref=boxes.at[d - 1], send_sem=send.at[d - 1], recv_sem=recv.at[d - 1],
            device_id=(lax.rem(me + d, jnp.int32(plan.count)),), device_id_type=MESH,
        ))
    for c in copies:
        c.start()
    for c in copies:
        c.wait()
    return mine[...] + jnp.sum(boxes[...], 0)


def ring_partners(plan, me):
    return [lax.rem(me + d, jnp.int32(plan.count)) for d in range(1, plan.count)]


def mat(ref, *cols):
    value = ref[(slice(None),) * (len(ref.shape) - 1) + cols] if cols else ref[...]
    return value.reshape(-1, value.shape[-1])


def front_kernel(*refs, plan, hd, mols, wide, seq, steps, steps2):
    refs = list(refs)
    take = lambda k: [refs.pop(0) for _ in range(k)]
    counts, tokens, eig, ends, cot = take(5)
    s_in, s_out, s_up, s_down, label_t, vec = take(6)
    out_o, proj_o, lse_o, dmid_o, dmix_o, labt_o, gout_o, gup_o, gdown_o, gvec_o, smallt_o, emb_o, inp_o, win_o = take(14)
    w_in, w_out, w_up, w_down, small = take(5)
    stages = take(1 + 6 * len(units(hd.dim * HEADS)))
    small_t, masks, tok_s, emb_s, inp_s, mixed_s, p_buf, acc_out, acc_up, acc_down, acc_vec = take(11)
    send, recv, keep = take(3)
    s_small, vec_s = take(2)
    step = pl.program_id(0)
    width = w_out.shape[-1]
    across_tiles = width // LANES
    score = hd.dim ** -0.5
    rows_all = mols * seq
    me, bit, other = my_place(plan)
    gather = Gather(plan, bit, other, send, recv)
    make = lambda i, src, buf, at, wide, split, t: dict(
        i=i, src=src, buf=buf, stage=stages[i], at=at, width=wide, split=split, turn=t
    )
    early = [make(0, s_small, small, 0, SMALL, False, 0)]
    late = []
    for src, buf, group in ((s_in, w_in, early), (s_out, w_out, late), (s_up, w_up, late), (s_down, w_down, late)):
        for at, unit in units(buf.shape[-1]):
            n = len(early) + len(late)
            group.append(make(n, src, buf, at, unit, True, n))
    final = plan.chip_bits + 1
    kept = [pltpu.make_async_copy(a, b, keep.at[i]) for i, (a, b) in enumerate(((w_in, win_o), (emb_s, emb_o), (inp_s, inp_o)))]
    get_tokens = pltpu.make_async_copy(tokens, tok_s, keep.at[3])

    row = lambda i: small_t[i : i + 1, :]

    def embed(group, carry):
        iota0 = lax.broadcasted_iota(jnp.int32, (seq, seq), 0)
        iota1 = lax.broadcasted_iota(jnp.int32, (seq, seq), 1)
        token_row = lax.broadcasted_iota(jnp.int32, (1, seq), 1)
        kind_row = lax.broadcasted_iota(jnp.int32, (16, seq), 0)
        one = lambda c: c.astype(F32).astype(BF)
        label_rows = []
        for g in range(mols):
            m = group * mols + g
            nodes = counts[0, m]
            live = nodes + counts[1, m]
            eig_f = eig[m]
            shift = one(jnp.logical_and(iota1 - iota0 == nodes, iota1 < live))
            picks = jnp.concatenate([one(iota0 == ends[m, end : end + 1, :]) for end in range(2)], 1)
            edge_lab = nn(eig_f.astype(BF), picks).astype(BF)
            moved = nn(jnp.concatenate([edge_lab[:, :seq], edge_lab[:, seq:]], 0), shift)
            at_node = token_row < nodes
            is_node = at_node.astype(F32)
            is_edge = jnp.logical_and(token_row >= nodes, token_row < live).astype(F32)
            kind = jnp.where(kind_row == 0, is_node, jnp.where(kind_row == 1, is_edge, 0.0))
            lab = jnp.concatenate(
                [jnp.where(at_node, eig_f, moved[:16]), jnp.where(at_node, eig_f, moved[16:]), kind], 0
            )
            labt_o[m] = lab.astype(BF)
            pad = jnp.zeros((SMALL - lab.shape[0], seq), F32)
            label_rows.append(jnp.concatenate([lab, pad], 0).T.astype(BF))
        labels = jnp.concatenate(label_rows, 0)
        here = pl.ds(pl.multiple_of(group * rows_all, rows_all), rows_all)
        embedded = tok_s[here, :].astype(F32) + nn(labels, small_t[...].astype(BF))
        emb_s[here, :] = embedded
        normed, _ = layer_stats(embedded)
        value = (normed * row(GAIN1) + row(SHIFT1)).astype(BF)
        for t in range(across_tiles):
            inp_s[t, here, :] = value[:, t * LANES : (t + 1) * LANES]
        return carry

    @pl.when(step == 0)
    def _():
        get_tokens.start()
        vec_s[...] = jnp.zeros_like(vec_s)
        vec_s[32:34, : vec.shape[1]] = vec[9:11, :]
        vec_s[34:43, : vec.shape[1]] = vec[0:9, :]
        s_small[...] = vec_s[...].T[: s_small.shape[0], :]
        s_small[:, :32] = label_t[...]
        greet(plan, other)
        for part in early + late:
            gather.start(part, 0)
        set_masks(hd, masks)
        acc_out[...] = jnp.zeros_like(acc_out)
        acc_up[...] = jnp.zeros_like(acc_up)
        acc_down[...] = jnp.zeros_like(acc_down)
        acc_vec[...] = jnp.zeros_like(acc_vec)
        for phase in range(final):
            for part in early:
                if part["split"] and phase == final - 1:
                    continue
                gather.advance(part, phase)
        small_t[...] = mat(small).astype(F32).T
        smallt_o[...] = small_t[...]
        get_tokens.wait()
        cut = (steps + 1) // 2
        lax.fori_loop(0, cut, embed, 0)
        for part in early[1:]:
            gather.advance(part, final - 1)
        lax.fori_loop(cut, steps, embed, 0)
        for part in early[1:]:
            gather.advance(part, final)
        for part in late:
            gather.advance(part, 0)
        for copy in kept:
            copy.start()

    def attend(some):
        for m in some:
            nodes = counts[0, step * mols + m]
            live = nodes + counts[1, step * mols + m]
            key_live = lax.broadcasted_iota(jnp.int32, (seq, 2 * seq), 0) < live
            rows = slice(m * seq, (m + 1) * seq)
            for b in range(hd.blocks):
                get = lambda part: [proj_o[part * across_tiles + b * hd.tiles + t, rows, :] for t in range(hd.tiles)]
                q, k, v = [dense(x) for x in get(0)], get(1), [dense(x) for x in get(2)]
                for pair in range(hd.block // 2):
                    scores = nt(pair_full(hd, k, pair), pair_rows(hd, masks, q, pair))
                    scores = jnp.where(key_live, scores, MASK_FILL)
                    top = jnp.max(scores, 0, keepdims=True)
                    ex = jnp.exp2((scores - top) * (score * LOG2E))
                    total = jnp.sum(ex, 0, keepdims=True)
                    shares = (ex * (1.0 / total)).astype(BF)
                    at = b * (hd.block // 2) + pair
                    lse_o[m, at : at + 1, :] = top + jnp.log2(total) * (1.0 / (score * LOG2E))
                    for i in range(2):
                        p_buf[b * hd.block + 2 * pair + i] = shares[:, i * seq : (i + 1) * seq].T
                for t in range(hd.tiles):
                    hs = hd.heads_of(t)
                    mixed = nn(across([p_buf[b * hd.block + h] for h in hs]), tile_rows(hd, masks, v[t], t))
                    put = pl.ds(pl.multiple_of(step * rows_all + m * seq, seq), seq)
                    mixed_s[b * hd.tiles + t, put, :] = mixed.astype(BF)

    @pl.when(step < steps)
    def _():
        here = pl.ds(pl.multiple_of(step * rows_all, rows_all), rows_all)
        input_one = across([inp_s[t, here, :] for t in range(across_tiles)])
        for part in range(3):
            value = nn(input_one, mat(w_in, slice(part * width, (part + 1) * width)))
            if part == 0:
                value = value + row(QBIAS)
            if part == 2:
                value = value + row(VBIAS)
            value = value.astype(BF)
            for t in range(across_tiles):
                proj_o[part * across_tiles + t] = value[:, t * LANES : (t + 1) * LANES]
        attend(range(mols // 2))

    def pump(half):
        for phase in range(1, final + 1):
            slot = min(SLOTS_GATHER[min(phase, 4) - 1] + max(phase - 4, 0), 2 * steps - 1)
            if slot % 2 == half:
                @pl.when(step == slot // 2)
                def _():
                    for part in late:
                        gather.advance(part, phase)

    pump(0)

    @pl.when(step < steps)
    def _():
        attend(range(mols // 2, mols))

    pump(1)

    @pl.when(step >= steps)
    def _():
        here = pl.ds(pl.multiple_of((step - steps) * wide, wide), wide)
        mixed = across([mixed_s[t, here, :] for t in range(across_tiles)])
        middle = emb_s[here, :] + (nt(mixed, mat(w_out)) + row(OBIAS))
        normed2, recip2 = layer_stats(middle)
        input_two = (normed2 * row(GAIN2) + row(SHIFT2)).astype(BF)
        pre = nn(input_two, mat(w_up)) + row(UBIAS)
        half_erf = 0.5 * (1.0 + lax.erf(pre * SQRT_HALF))
        act = (pre * half_erf).astype(BF)
        slope = half_erf + pre * jnp.exp(-0.5 * pre * pre) * INV_SQRT_TWO_PI
        out_o[...] = (middle + (nt(act, mat(w_down)) + row(DBIAS))).astype(BF)
        back = cot[...]
        back_f = back.astype(F32)
        d_pre = (nn(back, mat(w_down)) * slope).astype(BF)
        acc_down[...] += tn(back, act)
        acc_up[...] += tn(input_two, d_pre)
        d_in2 = nt(d_pre, mat(w_up))
        d_mid = back_f + norm_back(d_in2, normed2, recip2, row(GAIN2))
        dmid_o[...] = d_mid
        branch = d_mid.astype(BF)
        acc_out[...] += tn(branch, mixed)
        d_mixed = nn(branch, mat(w_out)).astype(BF)
        for t in range(across_tiles):
            dmix_o[t] = d_mixed[:, t * LANES : (t + 1) * LANES]
        add = lambda v: jnp.sum(v, 0, keepdims=True)
        sums = {
            OBIAS: add(branch.astype(F32)),
            GAIN2: add(d_in2 * normed2),
            SHIFT2: add(d_in2),
            UBIAS: add(d_pre.astype(F32)),
            DBIAS: add(back_f),
        }
        for i, v in sums.items():
            acc_vec[i - 34 : i - 33, :] += v

    @pl.when(step == steps + steps2 - 1)
    def _():
        for acc, out in ((acc_out, gout_o), (acc_up, gup_o), (acc_down, gdown_o)):
            out[...] = acc[...].astype(BF)
        gvec_o[...] = acc_vec[...]
        for copy in kept:
            copy.wait()


class ShareSmall:
    def __init__(self, plan, me, src, boxes, part, boxes2, send, recv):
        self.src, self.boxes, self.part, self.boxes2 = src, boxes, part, boxes2
        low = src.shape[1]
        high = plan.count // low
        self.place, self.level = lax.rem(me, jnp.int32(low)), lax.div(me, jnp.int32(low))
        self.one, self.two = [], []
        for d in range(1, low):
            to = lax.rem(self.place + d, jnp.int32(low))
            self.one.append(pltpu.make_async_remote_copy(
                src_ref=src.at[:, to], dst_ref=boxes.at[d - 1], send_sem=send.at[d - 1], recv_sem=recv.at[d - 1],
                device_id=(me + to - self.place,), device_id_type=MESH,
            ))
        for d in range(1, high):
            to = lax.rem(self.level + d, jnp.int32(high))
            at = low - 2 + d
            self.two.append(pltpu.make_async_remote_copy(
                src_ref=part.at[to], dst_ref=boxes2.at[d - 1], send_sem=send.at[at], recv_sem=recv.at[at],
                device_id=(me + (to - self.level) * low,), device_id_type=MESH,
            ))

    def begin(self):
        for c in self.one:
            c.start()

    def middle(self):
        total = self.src[:, self.place]
        for d, c in enumerate(self.one):
            c.wait()
            total = total + self.boxes[d]
        self.part[...] = total
        for c in self.two:
            c.start()

    def end(self):
        total = self.part[self.level]
        for d, c in enumerate(self.two):
            c.wait()
            total = total + self.boxes2[d]
        return total


def back_kernel(*refs, plan, hd, mols, wide, seq, steps, steps2):
    refs = list(refs)
    take = lambda k: [refs.pop(0) for _ in range(k)]
    counts, proj, lse, inp, emb, dmid, dmix, labt, w_in, small_t, gvec, g_out, g_up, g_down = take(14)
    tg_o, o_in, o_out, o_up, o_down, o_small, o_norm = take(7)
    masks, pt_buf, dst_buf, ds_buf, dproj_s, acc_in, g_in, acc_vec, acc_lab = take(9)
    k = plan.chip_bits + 1
    count = 6 * len(units(hd.dim * HEADS))
    slots = [take(k) for _ in range(count)]
    part_sums, lasts = take(count), take(count)
    send, recv = take(2)
    small_s, small_box, small_part, small_box2, ssend, srecv = take(6)
    mine, boxes, nsend, nrecv = take(4)
    step = pl.program_id(0)
    width = g_out.shape[-1]
    across_tiles = width // LANES
    score = hd.dim ** -0.5
    rows_all = mols * seq
    me, bit, other = my_place(plan)
    scatter = Scatter(plan, bit, other, send, recv)
    parts, late, early = [], [], []
    for src, out, group in ((g_in, o_in, late), (g_out, o_out, early), (g_up, o_up, early), (g_down, o_down, early)):
        for at, unit in units(src.shape[-1]):
            i = len(parts)
            part = dict(i=i, src=src, slots=slots[i], at=at, width=unit, split=True, turn=i, sum=part_sums[i],
                        last=lasts[i], out=out)
            parts.append(part)
            group.append(part)
    final = plan.chip_bits + 1

    @pl.when(step == 0)
    def _():
        barrier = pltpu.get_barrier_semaphore()
        partners = ring_partners(plan, me)
        for p in partners:
            pl.semaphore_signal(barrier, inc=1, device_id=(p,), device_id_type=MESH)
        pl.semaphore_wait(barrier, len(partners))
        for part in early:
            scatter.start(part, 0)
        set_masks(hd, masks)
        acc_in[...] = jnp.zeros_like(acc_in)
        acc_vec[...] = gvec[...]
        acc_lab[...] = jnp.zeros_like(acc_lab)

    row = lambda i: small_t[i : i + 1, :]

    def attend(some):
        for m in some:
            nodes = counts[0, step * mols + m]
            live = nodes + counts[1, step * mols + m]
            key_live = lax.broadcasted_iota(jnp.int32, (seq, 2 * seq), 0) < live
            rows = slice(m * seq, (m + 1) * seq)
            put = pl.ds(pl.multiple_of(step * rows_all + m * seq, seq), seq)
            for b in range(hd.blocks):
                get = lambda ref, part: [ref[part * across_tiles + b * hd.tiles + t, rows, :] for t in range(hd.tiles)]
                q, k, v, do = [dense(x) for x in get(proj, 0)], get(proj, 1), get(proj, 2), [dense(x) for x in get(dmix, 0)]
                k_dense = [dense(x) for x in k]
                for pair in range(hd.block // 2):
                    scores = nt(pair_full(hd, k, pair), pair_rows(hd, masks, q, pair))
                    scores = jnp.where(key_live, scores, MASK_FILL)
                    at = b * (hd.block // 2) + pair
                    p = jnp.exp2((scores - lse[m, at : at + 1, :]) * (score * LOG2E))
                    dp = nt(pair_full(hd, v, pair), pair_rows(hd, masks, do, pair))
                    inner = jnp.sum(p * dp, 0, keepdims=True)
                    ds = (p * (dp - inner)).astype(BF)
                    p = p.astype(BF)
                    for i in range(2):
                        h = b * hd.block + 2 * pair + i
                        pt_buf[h] = p[:, i * seq : (i + 1) * seq]
                        dst_buf[h] = ds[:, i * seq : (i + 1) * seq]
                        ds_buf[h] = ds[:, i * seq : (i + 1) * seq].T
                for t in range(hd.tiles):
                    hs = [b * hd.block + h for h in hd.heads_of(t)]
                    at = b * hd.tiles + t
                    d_v = nn(across([pt_buf[h] for h in hs]), tile_rows(hd, masks, do[t], t))
                    d_k = nn(across([dst_buf[h] for h in hs]), tile_rows(hd, masks, q[t], t)) * score
                    d_q = nn(across([ds_buf[h] for h in hs]), tile_rows(hd, masks, k_dense[t], t)) * score
                    dproj_s[at, put, :] = d_q.astype(BF)
                    dproj_s[across_tiles + at, put, :] = d_k.astype(BF)
                    dproj_s[2 * across_tiles + at, put, :] = d_v.astype(BF)

    @pl.when(step < steps)
    def _():
        attend(range(mols // 2))

    def pump(half):
        for phase in range(final + 1):
            slot = min(SLOTS_SCATTER[min(phase, 4)] + max(phase - 4, 0), 2 * steps - 1)
            if slot % 2 == half:
                @pl.when(step == slot // 2)
                def _():
                    for part in early:
                        scatter.advance(part, phase)

    pump(0)

    @pl.when(step < steps)
    def _():
        attend(range(mols // 2, mols))
        here = pl.ds(pl.multiple_of(step * rows_all, rows_all), rows_all)
        input_one = across([inp[t] for t in range(across_tiles)])
        d_proj = across([dproj_s[t, here, :] for t in range(3 * across_tiles)])
        acc_in[...] += tn(input_one, d_proj)
        add = lambda v: jnp.sum(v, 0, keepdims=True)
        acc_vec[QBIAS - 34 : QBIAS - 33, :] += add(d_proj[:, :width].astype(F32))
        acc_vec[VBIAS - 34 : VBIAS - 33, :] += add(d_proj[:, 2 * width :].astype(F32))

    pump(1)

    @pl.when(step == steps - 1)
    def _():
        for part in late:
            cols = slice(part["at"], part["at"] + part["width"])
            g_in[(slice(None),) * (plan.chip_bits + 1) + (cols,)] = acc_in[:, cols].astype(BF).reshape(
                g_in.shape[:-1] + (part["width"],)
            )
            scatter.start(part, 0)

    @pl.when(step >= steps)
    def _():
        here = pl.ds(pl.multiple_of((step - steps) * wide, wide), wide)
        normed, recip = layer_stats(emb[...])
        d_proj = across([dproj_s[t, here, :] for t in range(3 * across_tiles)])
        d_in1 = nt(d_proj, mat(w_in))
        tg = dmid[...] + norm_back(d_in1, normed, recip, row(GAIN1))
        tg_o[...] = tg
        tg_hi = tg.astype(BF)
        tg_lo = (tg - tg_hi.astype(F32)).astype(BF)
        lab = jnp.concatenate([labt[m] for m in range(wide // seq)], 1)
        acc_lab[...] += nn(lab, tg_hi)
        acc_lab[32:48, :] += nn(lab[32:48, :], tg_lo)
        add = lambda v: jnp.sum(v, 0, keepdims=True)
        acc_vec[GAIN1 - 34 : GAIN1 - 33, :] += add(d_in1 * normed)
        acc_vec[SHIFT1 - 34 : SHIFT1 - 33, :] += add(d_in1)

    for phase in range(min(final, steps2 - 1)):
        @pl.when(step == steps + phase)
        def _():
            for part in late:
                scatter.advance(part, phase)

    @pl.when(step == steps + steps2 - 1)
    def _():
        full = jnp.concatenate(
            [acc_lab[0:32, :], acc_lab[32:34, :], acc_vec[0:9, :], jnp.zeros((SMALL - 43, width), F32)], 0
        )
        small_s[...] = full.T.reshape(small_s.shape)
        share = ShareSmall(plan, me, small_s, small_box, small_part, small_box2, ssend, srecv)
        share.begin()
        for phase in range(min(final, steps2 - 1), final + 1):
            for part in late:
                scatter.advance(part, phase)
            if phase == final - 1:
                share.middle()
        o_small[...] = share.end()
        for part in parts:
            scatter.finish(part, part["out"])
        total = sum(jnp.sum(o[...] * o[...]) for o in (o_small, o_in, o_out, o_up, o_down))
        o_norm[...] = jnp.sqrt(norm_exchange(plan, me, total, mine, boxes, nsend, nrecv))


def paired_layer(plan, tokens, eig_t, counts_t, ends_t, cot, shards, mols_step):
    count, width = tokens.shape
    mols_all, lap, seq = eig_t.shape
    shard = shards[0].shape[0]
    parts = len(units(width))
    hd = Heads(width)
    steps = mols_all // mols_step
    rows = mols_step * seq
    wide = min(WIDE, count)
    steps2 = count // wide
    across_tiles = width // LANES
    last = steps - 1
    first = lambda i: lax.min(i, last)
    second = lambda i: lax.max(i - steps, 0)
    tok2 = lambda w: pl.BlockSpec((wide, w), lambda i: (second(i), 0))
    mol = lambda a, b: pl.BlockSpec((mols_step, a, b), lambda i: (first(i), 0, 0))
    tiled = lambda n: pl.BlockSpec((n, rows, LANES), lambda i: (0, first(i), 0))
    tiled2 = lambda n: pl.BlockSpec((n, wide, LANES), lambda i: (0, second(i), 0))
    sizes = dict(plan=plan, hd=hd, mols=mols_step, wide=wide, seq=seq, steps=steps, steps2=steps2)
    vm, sm, hbm = (pl.BlockSpec(memory_space=m) for m in (pltpu.VMEM, pltpu.SMEM, pl.ANY))
    sq = (width, width)
    buf = lambda c: plan.dims + (2 * shard, c)
    f32 = lambda *shape: jax.ShapeDtypeStruct(shape, F32)
    bf = lambda *shape: jax.ShapeDtypeStruct(shape, BF)
    params = lambda cid: pltpu.CompilerParams(
        vmem_limit_bytes=VMEM_LIMIT, dimension_semantics=("arbitrary",), collective_id=cid,
        has_side_effects=True,
    )
    out, proj, lse, dmid, dmix, labt, g_out, g_up, g_down, g_vec, small_t, emb, inp, w_in = pl.pallas_call(
        functools.partial(front_kernel, **sizes),
        grid=(steps + steps2,),
        in_specs=[sm, hbm, vm, vm, tok2(width)] + [vm] * 6,
        out_specs=[tok2(width), tiled(3 * across_tiles), mol(HEADS // 2, 2 * seq), tok2(width), tiled2(across_tiles)]
        + [vm] * 6 + [hbm] * 3,
        out_shape=[bf(count, width), bf(3 * across_tiles, count, LANES), f32(mols_all, HEADS // 2, 2 * seq),
                   f32(count, width), bf(across_tiles, count, LANES), bf(mols_all, 48, seq),
                   bf(*sq), bf(*sq), bf(*sq), f32(16, width), f32(SMALL, width),
                   f32(count, width), bf(across_tiles, count, LANES), bf(*buf(3 * width))],
        scratch_shapes=[pltpu.VMEM(buf(c), BF) for c in (3 * width, width, width, width, SMALL)]
        + [pltpu.VMEM((shard, SMALL), F32)] + [pltpu.VMEM((shard, LANES), F32)] * (6 * parts)
        + [
            pltpu.VMEM((SMALL, width), F32),
            pltpu.VMEM((hd.slots(), 16, LANES), BF),
            pltpu.VMEM((count, width), BF),
            pltpu.VMEM((count, width), F32),
            pltpu.VMEM((across_tiles, count, LANES), BF),
            pltpu.VMEM((across_tiles, count, LANES), BF),
            pltpu.VMEM((HEADS, seq, seq), BF),
            pltpu.VMEM(sq, F32), pltpu.VMEM(sq, F32), pltpu.VMEM(sq, F32),
            pltpu.VMEM((16, width), F32),
        ]
        + [pltpu.SemaphoreType.DMA((6 * parts + 1, plan.chip_bits + 2))] * 2 + [pltpu.SemaphoreType.DMA((4,))]
        + [pltpu.VMEM((shard, SMALL), F32), pltpu.VMEM((SMALL, LANES), F32)],
        compiler_params=params(0),
        name="front",
    )(counts_t, tokens, eig_t, ends_t, cot, *shards)

    low = 1 << min(3, plan.bits)
    high = plan.count // low
    boxes = low - 1 + high - 1
    slots = [pltpu.VMEM(plan.dims[j:] + (2 * shard, LANES), BF) for j in range(plan.chip_bits + 1)]
    shaped = [g.reshape(buf(width)) for g in (g_out, g_up, g_down)]
    tg, *sums, norm = pl.pallas_call(
        functools.partial(back_kernel, **sizes),
        grid=(steps + steps2,),
        in_specs=[sm, tiled(3 * across_tiles), mol(HEADS // 2, 2 * seq), tiled(across_tiles), tok2(width), tok2(width),
                  tiled(across_tiles), pl.BlockSpec((wide // seq, 48, seq), lambda i: (second(i), 0, 0))] + [vm] * 6,
        out_specs=[tok2(width)] + [vm] * 6,
        out_shape=[f32(count, width), f32(shard, 3 * width), f32(shard, width), f32(shard, width), f32(shard, width),
                   f32(shard, SMALL), f32(8, LANES)],
        scratch_shapes=[
            pltpu.VMEM((hd.slots(), 16, LANES), BF),
            pltpu.VMEM((HEADS, seq, seq), BF),
            pltpu.VMEM((HEADS, seq, seq), BF),
            pltpu.VMEM((HEADS, seq, seq), BF),
            pltpu.VMEM((3 * across_tiles, count, LANES), BF),
            pltpu.VMEM((width, 3 * width), F32),
            pltpu.VMEM(buf(3 * width), BF),
            pltpu.VMEM((16, width), F32),
            pltpu.VMEM((48, width), F32),
        ]
        + slots * (6 * parts)
        + [pltpu.VMEM((2 * shard, LANES), F32)] * (6 * parts) + [pltpu.VMEM((shard, LANES), F32)] * (6 * parts)
        + [pltpu.SemaphoreType.DMA((6 * parts, plan.chip_bits + 2))] * 2
        + [
            pltpu.VMEM((high, low, shard, SMALL), F32),
            pltpu.VMEM((low - 1, high, shard, SMALL), F32),
            pltpu.VMEM((high, shard, SMALL), F32),
            pltpu.VMEM((max(high - 1, 1), shard, SMALL), F32),
        ]
        + [pltpu.SemaphoreType.DMA((boxes,))] * 2
        + [pltpu.VMEM((8, LANES), F32), pltpu.VMEM((plan.count - 1, 8, LANES), F32)]
        + [pltpu.SemaphoreType.DMA((plan.count - 1,))] * 2,
        compiler_params=params(1),
        name="back",
    )(counts_t, proj, lse, inp, emb, dmid, dmix, labt, w_in, small_t, g_vec, *shaped)
    return out, tg, sums, norm


def plain_front_kernel(
    counts, tokens, eig, ends, cot, w_in, w_out, w_up, w_down, small,
    out_o, proj_o, lse_o, emb_o, dmid_o, dmix_o, labt_o, gout_o, gup_o, gdown_o, gvec_o,
    small_t, masks, mixed_s, p_buf, acc_out, acc_up, acc_down, acc_vec,
    *, hd, mols, seq, steps,
):
    step = pl.program_id(0)
    width = w_in.shape[0]
    across_tiles = width // LANES
    score = hd.dim ** -0.5

    @pl.when(step == 0)
    def _():
        small_t[...] = small[...].astype(F32).T
        set_masks(hd, masks)
        acc_out[...] = jnp.zeros_like(acc_out)
        acc_up[...] = jnp.zeros_like(acc_up)
        acc_down[...] = jnp.zeros_like(acc_down)
        acc_vec[...] = jnp.zeros_like(acc_vec)

    row = lambda i: small_t[i : i + 1, :]
    iota0 = lax.broadcasted_iota(jnp.int32, (seq, seq), 0)
    iota1 = lax.broadcasted_iota(jnp.int32, (seq, seq), 1)
    token_row = lax.broadcasted_iota(jnp.int32, (1, seq), 1)
    one = lambda c: c.astype(F32).astype(BF)
    label_rows = []
    for m in range(mols):
        nodes = counts[0, step * mols + m]
        live = nodes + counts[1, step * mols + m]
        eig_f = eig[m]
        eig_low = eig_f.astype(BF)
        shift = one(jnp.logical_and(iota1 - iota0 == nodes, iota1 < live))
        halves = []
        for end in range(2):
            pick = one(iota0 == ends[m, end : end + 1, :])
            edge_lab = nn(eig_low, pick).astype(BF)
            moved = nn(edge_lab, shift)
            halves.append(jnp.where(token_row < nodes, eig_f, moved))
        is_node = (token_row < nodes).astype(F32)
        is_edge = jnp.logical_and(token_row >= nodes, token_row < live).astype(F32)
        kind = jnp.where(lax.broadcasted_iota(jnp.int32, (16, seq), 0) == 0, is_node,
                         jnp.where(lax.broadcasted_iota(jnp.int32, (16, seq), 0) == 1, is_edge, 0.0))
        lab = jnp.concatenate(halves + [kind], 0)
        labt_o[m] = lab.astype(BF)
        pad = jnp.zeros((SMALL - lab.shape[0], seq), F32)
        label_rows.append(jnp.concatenate([lab, pad], 0).T.astype(BF))
    labels = jnp.concatenate(label_rows, 0)
    embedded = tokens[...].astype(F32) + nn(labels, small_t[...].astype(BF))
    emb_o[...] = embedded
    normed, recip = layer_stats(embedded)
    input_one = (normed * row(GAIN1) + row(SHIFT1)).astype(BF)
    for part in range(3):
        cols = slice(part * width, (part + 1) * width)
        value = nn(input_one, w_in[:, cols])
        if part == 0:
            value = value + row(QBIAS)
        if part == 2:
            value = value + row(VBIAS)
        value = value.astype(BF)
        for t in range(across_tiles):
            proj_o[part * across_tiles + t] = value[:, t * LANES : (t + 1) * LANES]

    for m in range(mols):
        nodes = counts[0, step * mols + m]
        live = nodes + counts[1, step * mols + m]
        key_live = lax.broadcasted_iota(jnp.int32, (seq, 2 * seq), 0) < live
        rows = slice(m * seq, (m + 1) * seq)
        for b in range(hd.blocks):
            base = b * hd.tiles * LANES
            get = lambda part: [proj_o[part * across_tiles + b * hd.tiles + t, rows, :] for t in range(hd.tiles)]
            q, k, v = get(0), get(1), get(2)
            for pair in range(hd.block // 2):
                scores = nt(pair_full(hd, k, pair), pair_rows(hd, masks, q, pair))
                scores = jnp.where(key_live, scores, MASK_FILL)
                top = jnp.max(scores, 0, keepdims=True)
                ex = jnp.exp2((scores - top) * (score * LOG2E))
                total = jnp.sum(ex, 0, keepdims=True)
                shares = (ex * (1.0 / total)).astype(BF)
                lse_o[m, b * (hd.block // 2) + pair : b * (hd.block // 2) + pair + 1, :] = (
                    top + jnp.log2(total) * (1.0 / (score * LOG2E))
                )
                for i in range(2):
                    h = 2 * pair + i
                    p_buf[b * hd.block + h] = shares[:, i * seq : (i + 1) * seq].T
            for t in range(hd.tiles):
                hs = hd.heads_of(t)
                mixed = nn(across([p_buf[b * hd.block + h] for h in hs]), tile_rows(hd, masks, v[t], t))
                mixed_s[b * hd.tiles + t, rows, :] = mixed.astype(BF)

    mixed = across([mixed_s[t] for t in range(across_tiles)])
    middle = embedded + (nt(mixed, w_out[...]) + row(OBIAS))
    normed2, recip2 = layer_stats(middle)
    input_two = (normed2 * row(GAIN2) + row(SHIFT2)).astype(BF)
    pre = nn(input_two, w_up[...]) + row(UBIAS)
    half_erf = 0.5 * (1.0 + lax.erf(pre * SQRT_HALF))
    act = (pre * half_erf).astype(BF)
    slope = half_erf + pre * jnp.exp(-0.5 * pre * pre) * INV_SQRT_TWO_PI
    out_o[...] = (middle + (nt(act, w_down[...]) + row(DBIAS))).astype(BF)
    back = cot[...]
    back_f = back.astype(F32)
    d_pre_f = nn(back, w_down[...]) * slope
    d_pre = d_pre_f.astype(BF)
    acc_down[...] += tn(back, act)
    acc_up[...] += tn(input_two, d_pre)
    d_in2 = nt(d_pre, w_up[...])
    d_mid = back_f + norm_back(d_in2, normed2, recip2, row(GAIN2))
    dmid_o[...] = d_mid
    branch = d_mid.astype(BF)
    acc_out[...] += tn(branch, mixed)
    d_mixed = nn(branch, w_out[...]).astype(BF)
    for t in range(across_tiles):
        dmix_o[t] = d_mixed[:, t * LANES : (t + 1) * LANES]
    add = lambda v: jnp.sum(v, 0, keepdims=True)
    sums = {
        OBIAS: add(branch.astype(F32)),
        GAIN2: add(d_in2 * normed2),
        SHIFT2: add(d_in2),
        UBIAS: add(d_pre.astype(F32)),
        DBIAS: add(back_f),
    }
    for i, v in sums.items():
        acc_vec[i - 34 : i - 33, :] += v

    @pl.when(step == steps - 1)
    def _():
        gout_o[...] = acc_out[...].astype(BF)
        gup_o[...] = acc_up[...].astype(BF)
        gdown_o[...] = acc_down[...].astype(BF)
        gvec_o[...] = acc_vec[...]


def plain_back_kernel(
    counts, proj, lse, emb, dmid, dmix, labt, w_in, small, gvec,
    tg_o, gin_o, gsmall_o,
    small_t, masks, pt_buf, dst_buf, ds_buf, dproj_s, acc_in, acc_vec, acc_lab,
    *, hd, mols, seq, steps,
):
    step = pl.program_id(0)
    width = w_in.shape[0]
    across_tiles = width // LANES
    score = hd.dim ** -0.5

    @pl.when(step == 0)
    def _():
        small_t[...] = small[...].astype(F32).T
        set_masks(hd, masks)
        acc_in[...] = jnp.zeros_like(acc_in)
        acc_vec[...] = gvec[...]
        acc_lab[...] = jnp.zeros_like(acc_lab)

    row = lambda i: small_t[i : i + 1, :]
    for m in range(mols):
        nodes = counts[0, step * mols + m]
        live = nodes + counts[1, step * mols + m]
        key_live = lax.broadcasted_iota(jnp.int32, (seq, 2 * seq), 0) < live
        rows = slice(m * seq, (m + 1) * seq)
        for b in range(hd.blocks):
            base = b * hd.tiles * LANES
            get = lambda ref, part: [ref[part * across_tiles + b * hd.tiles + t, rows, :] for t in range(hd.tiles)]
            q, k, v, do = get(proj, 0), get(proj, 1), get(proj, 2), get(dmix, 0)
            for pair in range(hd.block // 2):
                scores = nt(pair_full(hd, k, pair), pair_rows(hd, masks, q, pair))
                scores = jnp.where(key_live, scores, MASK_FILL)
                at = b * (hd.block // 2) + pair
                p = jnp.exp2((scores - lse[m, at : at + 1, :]) * (score * LOG2E))
                dp = nt(pair_full(hd, v, pair), pair_rows(hd, masks, do, pair))
                inner = jnp.sum(p * dp, 0, keepdims=True)
                ds = (p * (dp - inner)).astype(BF)
                p = p.astype(BF)
                for i in range(2):
                    h = b * hd.block + 2 * pair + i
                    pt_buf[h] = p[:, i * seq : (i + 1) * seq]
                    dst_buf[h] = ds[:, i * seq : (i + 1) * seq]
                    ds_buf[h] = ds[:, i * seq : (i + 1) * seq].T
            for t in range(hd.tiles):
                hs = [b * hd.block + h for h in hd.heads_of(t)]
                at = b * hd.tiles + t
                d_v = nn(across([pt_buf[h] for h in hs]), tile_rows(hd, masks, do[t], t))
                d_k = nn(across([dst_buf[h] for h in hs]), tile_rows(hd, masks, q[t], t)) * score
                d_q = nn(across([ds_buf[h] for h in hs]), tile_rows(hd, masks, k[t], t)) * score
                dproj_s[at, rows, :] = d_q.astype(BF)
                dproj_s[across_tiles + at, rows, :] = d_k.astype(BF)
                dproj_s[2 * across_tiles + at, rows, :] = d_v.astype(BF)

    normed, recip = layer_stats(emb[...])
    input_one = (normed * row(GAIN1) + row(SHIFT1)).astype(BF)
    d_proj = across([dproj_s[t] for t in range(3 * across_tiles)])
    acc_in[...] += tn(input_one, d_proj)
    d_in1 = nt(d_proj, w_in[...])
    tg = dmid[...] + norm_back(d_in1, normed, recip, row(GAIN1))
    tg_o[...] = tg
    tg_hi = tg.astype(BF)
    tg_lo = (tg - tg_hi.astype(F32)).astype(BF)
    lab = jnp.concatenate([labt[m] for m in range(mols)], 1)
    acc_lab[...] += nn(lab, tg_hi)
    acc_lab[32:48, :] += nn(lab[32:48, :], tg_lo)
    add = lambda v: jnp.sum(v, 0, keepdims=True)
    sums = {
        GAIN1: add(d_in1 * normed),
        SHIFT1: add(d_in1),
        QBIAS: add(d_proj[:, :width].astype(F32)),
        VBIAS: add(d_proj[:, 2 * width :].astype(F32)),
    }
    for i, v in sums.items():
        acc_vec[i - 34 : i - 33, :] += v

    @pl.when(step == steps - 1)
    def _():
        gin_o[...] = acc_in[...].astype(BF)
        full = jnp.concatenate(
            [acc_lab[0:32, :], acc_lab[32:34, :], acc_vec[0:9, :], jnp.zeros((SMALL - 43, width), F32)], 0
        )
        gsmall_o[...] = full.T.astype(BF)


def whole(shape):
    return pl.BlockSpec(shape, lambda *_: (0,) * len(shape), pipeline_mode=pl.Buffered(1))


def out_whole(shape):
    return pl.BlockSpec(shape, lambda *_: (0,) * len(shape))


def plain_layer(tokens, eig_t, counts_t, ends_t, cot, w_in, w_out, w_up, w_down, small, mols_step):
    count, width = tokens.shape
    mols_all, lap, seq = eig_t.shape
    hd = Heads(width)
    steps = mols_all // mols_step
    rows = mols_step * seq
    tok = lambda w: pl.BlockSpec((rows, w), lambda i, *_: (i, 0))
    tiled = lambda n: pl.BlockSpec((n, rows, LANES), lambda i, *_: (0, i, 0))
    across_tiles = width // LANES
    mol = lambda a, b: pl.BlockSpec((mols_step, a, b), lambda i, *_: (i, 0, 0))
    params = pltpu.CompilerParams(vmem_limit_bytes=VMEM_LIMIT, dimension_semantics=("arbitrary",))
    sq = (width, width)
    front = pl.pallas_call(
        functools.partial(plain_front_kernel, hd=hd, mols=mols_step, seq=seq, steps=steps),
        grid_spec=pltpu.PrefetchScalarGridSpec(
            num_scalar_prefetch=1,
            grid=(steps,),
            in_specs=[tok(width), mol(lap, seq), mol(2, seq), tok(width), whole((width, 3 * width)),
                      whole(sq), whole(sq), whole(sq), whole((width, SMALL))],
            out_specs=[tok(width), tiled(3 * across_tiles), mol(HEADS // 2, 2 * seq), tok(width), tok(width), tiled(across_tiles),
                       mol(48, seq), out_whole(sq), out_whole(sq), out_whole(sq), out_whole((16, width))],
            scratch_shapes=[
                pltpu.VMEM((SMALL, width), F32),
                pltpu.VMEM((hd.slots(), 16, LANES), BF),
                pltpu.VMEM((across_tiles, rows, LANES), BF),
                pltpu.VMEM((HEADS, seq, seq), BF),
                pltpu.VMEM(sq, F32), pltpu.VMEM(sq, F32), pltpu.VMEM(sq, F32),
                pltpu.VMEM((16, width), F32),
            ],
        ),
        out_shape=[
            jax.ShapeDtypeStruct((count, width), BF),
            jax.ShapeDtypeStruct((3 * across_tiles, count, LANES), BF),
            jax.ShapeDtypeStruct((mols_all, HEADS // 2, 2 * seq), F32),
            jax.ShapeDtypeStruct((count, width), F32),
            jax.ShapeDtypeStruct((count, width), F32),
            jax.ShapeDtypeStruct((across_tiles, count, LANES), BF),
            jax.ShapeDtypeStruct((mols_all, 48, seq), BF),
            jax.ShapeDtypeStruct(sq, BF),
            jax.ShapeDtypeStruct(sq, BF),
            jax.ShapeDtypeStruct(sq, BF),
            jax.ShapeDtypeStruct((16, width), F32),
        ],
        compiler_params=params,
        name="plain_front",
    )(counts_t, tokens, eig_t, ends_t, cot, w_in, w_out, w_up, w_down, small)
    out, proj, lse, emb, dmid, dmix, labt, g_out, g_up, g_down, g_vec = front
    tg, g_in, g_small = pl.pallas_call(
        functools.partial(plain_back_kernel, hd=hd, mols=mols_step, seq=seq, steps=steps),
        grid_spec=pltpu.PrefetchScalarGridSpec(
            num_scalar_prefetch=1,
            grid=(steps,),
            in_specs=[tiled(3 * across_tiles), mol(HEADS // 2, 2 * seq), tok(width), tok(width), tiled(across_tiles), mol(48, seq),
                      whole((width, 3 * width)), whole((width, SMALL)), whole((16, width))],
            out_specs=[tok(width), out_whole((width, 3 * width)), out_whole((width, SMALL))],
            scratch_shapes=[
                pltpu.VMEM((SMALL, width), F32),
                pltpu.VMEM((hd.slots(), 16, LANES), BF),
                pltpu.VMEM((HEADS, seq, seq), BF),
                pltpu.VMEM((HEADS, seq, seq), BF),
                pltpu.VMEM((HEADS, seq, seq), BF),
                pltpu.VMEM((3 * across_tiles, rows, LANES), BF),
                pltpu.VMEM((width, 3 * width), F32),
                pltpu.VMEM((16, width), F32),
                pltpu.VMEM((48, width), F32),
            ],
        ),
        out_shape=[
            jax.ShapeDtypeStruct((count, width), F32),
            jax.ShapeDtypeStruct((width, 3 * width), BF),
            jax.ShapeDtypeStruct((width, SMALL), BF),
        ],
        compiler_params=params,
        name="plain_back",
    )(counts_t, proj, lse, emb, dmid, dmix, labt, w_in, small, g_vec)
    return out, tg, g_in, g_out, g_up, g_down, g_small


def update_kernel(
    steps, rates, large_a, large_b, norm, g_in, g_out, g_up, g_down, g_small, *refs,
):
    states, outs, norm_o = refs[:18], refs[18:42], refs[42]
    moves = []
    for i, (source, target, stay) in enumerate(((large_b, refs[44], refs[46]), (large_a, refs[43], refs[45]))):
        size = source.shape[0] // MOVES
        for j in range(MOVES):
            part = pl.ds(j * size, size)
            moves.append((
                pltpu.make_async_copy(source.at[part], stay.at[part], refs[47].at[2 * (MOVES * i + j)]),
                pltpu.make_async_copy(stay.at[part], target.at[part], refs[47].at[2 * (MOVES * i + j) + 1]),
            ))
    for load, _ in moves:
        load.start()
    for load, store in moves:
        load.wait()
        store.start()
    norm_o[0, 0] = norm[0, 0]
    total = norm[0:1, 0:1]
    factor = jnp.minimum(1.0, CLIP_LIMIT / (total + NORM_EPS))
    t = jnp.full((1, 1), steps[0].astype(F32), F32)
    rate = rates[0]
    fix_one = 1.0 / (1.0 - jnp.exp(t * math.log(BETA_ONE)))
    fix_two = 1.0 / (1.0 - jnp.exp(t * math.log(BETA_TWO)))
    small = g_small[...]
    turned = jnp.concatenate([small, jnp.zeros((LANES - small.shape[0], SMALL), F32)], 0).T
    vec = turned[32:43, : small.shape[0]]
    vec = jnp.concatenate([vec[2:, :], vec[:2, :]], 0)
    grads = (g_in[...], g_out[...], g_up[...], g_down[...], small[:, :32], vec)
    for i, g in enumerate(grads):
        master, first, second = (states[3 * i + j][...] for j in range(3))
        g = g * factor
        first = BETA_ONE * first + (1.0 - BETA_ONE) * g
        second = BETA_TWO * second + (1.0 - BETA_TWO) * g * g
        change = first * fix_one / (jnp.sqrt(second * fix_two) + ADAM_EPS)
        if i < 5:
            change = change + DECAY_RATE * master
        for j, v in enumerate((g, first, second, master - rate * change)):
            outs[4 * i + j][...] = v
    for _, store in moves:
        store.wait()


def update_call(step_count, learn_rate, large, norm, grads, states):
    vm, sm, hbm = (pl.BlockSpec(memory_space=m) for m in (pltpu.VMEM, pltpu.SMEM, pl.ANY))
    shapes = [jax.ShapeDtypeStruct(states[3 * i].shape, F32) for i in range(6) for _ in range(4)]
    return pl.pallas_call(
        update_kernel,
        in_specs=[sm, sm, hbm, hbm] + [vm] * 24,
        out_specs=[vm] * 24 + [sm, hbm, hbm],
        out_shape=shapes + [jax.ShapeDtypeStruct((1, 1), F32)] + [jax.ShapeDtypeStruct(v.shape, v.dtype) for v in large],
        scratch_shapes=[pltpu.VMEM(v.shape, v.dtype) for v in large] + [pltpu.SemaphoreType.DMA((4 * MOVES,))],
        compiler_params=pltpu.CompilerParams(vmem_limit_bytes=VMEM_LIMIT),
        name="update",
    )(step_count.reshape(1), learn_rate.reshape(1), *large, norm, *grads, *states)


def body(
    count,
    tokens, eigvecs, counts, endpoints, cotangent,
    attend_in, attend_in_first, attend_in_second,
    attend_out, attend_out_first, attend_out_second,
    feed_up, feed_up_first, feed_up_second,
    feed_down, feed_down_first, feed_down_second,
    label_in, label_in_first, label_in_second,
    vectors, vectors_first, vectors_second,
    step_count, learn_rate,
):
    shard, width = feed_up.shape
    squares = (attend_in, attend_out.T, feed_up, feed_down.T)
    arrays = (tokens, jnp.swapaxes(eigvecs, 1, 2), counts.T, jnp.swapaxes(endpoints, 1, 2), cotangent)
    if Plan.fits(count, shard):
        out, tg, sums, norm = paired_layer(Plan(count), *arrays, squares + (label_in.T, vectors), MOLS_STEP)
    else:
        small_shard = jnp.concatenate(
            [label_in.T, vectors[9:].T, vectors[:9].T, jnp.zeros((shard, SMALL - 43), F32)], 1
        )
        shards = squares + (small_shard,)
        weights = [lax.all_gather(v.astype(BF), "dp", axis=0, tiled=True) for v in shards]
        out, tg, *grads = plain_layer(*arrays, *weights, 2)
        sums = [lax.psum_scatter(v.astype(F32), "dp", scatter_dimension=0, tiled=True) for v in grads]
        total = lax.psum(sum(jnp.sum(v * v) for v in sums), "dp")
        norm = jnp.full((8, LANES), jnp.sqrt(total), F32)
    states = (
        attend_in, attend_in_first, attend_in_second,
        attend_out.T, attend_out_first.T, attend_out_second.T,
        feed_up, feed_up_first, feed_up_second,
        feed_down.T, feed_down_first.T, feed_down_second.T,
        label_in.T, label_in_first.T, label_in_second.T,
        vectors, vectors_first, vectors_second,
    )
    *new, norm, out, tg = update_call(step_count, learn_rate, (out, tg), norm, sums, states)
    new = [v.T if i // 4 in (1, 3, 4) else v for i, v in enumerate(new)]
    return (out, tg, norm.reshape(()), *new)


MOLS_STEP = 4
SLOTS_GATHER = (1, 2, 4, 6)
SLOTS_SCATTER = (0, 2, 3, 4, 6)
WIDE = 512
MOVES = 8


def solution(mesh):
    rows, cols = P("dp", None), P(None, "dp")
    state = (rows,) * 3 + (cols,) * 3 + (rows,) * 3 + (cols,) * 9
    placed = (rows, P("dp", None, None), rows, P("dp", None, None), rows) + state + (P(), P())
    results = (rows,) * 4 + (cols,) * 4 + (rows,) * 4 + (cols,) * 12
    return jax.shard_map(
        functools.partial(body, mesh.shape["dp"]),
        mesh=mesh, in_specs=placed, out_specs=(rows, rows, P()) + results, check_vma=False,
    )
```

```python
import functools
import math

import jax
import jax.numpy as jnp
from jax import lax
from jax.experimental import pallas as pl
from jax.experimental.pallas import tpu as pltpu
from jax.sharding import PartitionSpec as P

HEADS = 32
EPS_NORM = 1e-05
MASK_FILL = -1e30
SQRT_HALF = 0.7071067811865476
INV_SQRT_TWO_PI = 0.3989422804014327
BETA_ONE = 0.9
BETA_TWO = 0.999
ADAM_EPS = 1e-08
DECAY_RATE = 0.01
CLIP_LIMIT = 1.0
NORM_EPS = 1e-06
LOG2E = 1.4426950408889634

BF = jnp.bfloat16
F32 = jnp.float32
MESH = pl.DeviceIdType.MESH
LANES = 128
VMEM_LIMIT = 60 << 20

SMALL = 128
NODE, EDGE = 32, 33
GAIN1, SHIFT1, QBIAS, VBIAS, OBIAS, GAIN2, SHIFT2, UBIAS, DBIAS = range(34, 43)


def nn(a, b):
    return lax.dot_general(a, b, (((1,), (0,)), ((), ())), preferred_element_type=F32)


def nt(a, b):
    return lax.dot_general(a, b, (((1,), (1,)), ((), ())), preferred_element_type=F32)


def tn(a, b):
    return lax.dot_general(a, b, (((0,), (0,)), ((), ())), preferred_element_type=F32)


def layer_stats(values):
    centred = values - jnp.mean(values, -1, keepdims=True)
    recip_std = lax.rsqrt(jnp.mean(centred * centred, -1, keepdims=True) + EPS_NORM)
    return centred * recip_std, recip_std


def norm_back(grad_out, normed, recip_std, gain_row):
    scaled = grad_out * gain_row
    return recip_std * (
        scaled
        - jnp.mean(scaled, -1, keepdims=True)
        - normed * jnp.mean(scaled * normed, -1, keepdims=True)
    )


class Heads:
    def __init__(self, width):
        self.dim = width // HEADS
        span = 1
        while (span * self.dim) % LANES:
            span *= 2
        self.block = span
        self.tiles = span * self.dim // LANES
        self.blocks = HEADS // span

    def first(self, head):
        return head * self.dim // LANES

    def last(self, head):
        return ((head + 1) * self.dim - 1) // LANES

    def heads_of(self, tile):
        return [h for h in range(self.block) if self.first(h) <= tile <= self.last(h)]

    def slot(self, tile, head):
        return sum(len(self.heads_of(t)) for t in range(tile)) + head - self.heads_of(tile)[0]

    def slots(self):
        return sum(len(self.heads_of(t)) for t in range(self.tiles))

    def mask(self, tile, head):
        lane = lax.broadcasted_iota(jnp.int32, (1, LANES), 1) + tile * LANES
        inside = jnp.logical_and(lane >= head * self.dim, lane < (head + 1) * self.dim)
        return inside.astype(F32).astype(BF)


def masked(value, mask):
    rows = value.shape[0]
    return (value.reshape(rows // 16, 16, LANES) * mask[None]).reshape(rows, LANES)


def dense(value):
    return value.astype(F32).astype(BF)


def set_masks(hd, masks):
    for t in range(hd.tiles):
        for h in hd.heads_of(t):
            masks[hd.slot(t, h)] = jnp.broadcast_to(hd.mask(t, h), (16, LANES))


def across(parts):
    return parts[0] if len(parts) == 1 else jnp.concatenate(parts, 1)


def pair_rows(hd, masks, tiles_of, pair):
    h0, h1 = 2 * pair, 2 * pair + 1
    lo, hi = hd.first(h0), hd.last(h1)
    rows = []
    for h in (h0, h1):
        parts = []
        for t in range(lo, hi + 1):
            if hd.first(h) <= t <= hd.last(h):
                parts.append(masked(tiles_of[t], masks[hd.slot(t, h)]))
            else:
                parts.append(jnp.zeros_like(tiles_of[t]))
        rows.append(across(parts))
    return jnp.concatenate(rows, 0)


def pair_full(hd, tiles_of, pair):
    return across([tiles_of[t] for t in range(hd.first(2 * pair), hd.last(2 * pair + 1) + 1)])


def tile_rows(hd, masks, tile_value, tile):
    return jnp.concatenate([masked(tile_value, masks[hd.slot(tile, h)]) for h in hd.heads_of(tile)], 0)


def units(width):
    unit = 2 * LANES
    return [(at, unit) for at in range(0, width, unit)]


class Plan:
    def __init__(self, count):
        self.count = count
        self.bits = count.bit_length() - 1
        self.chip_bits = self.bits - 1
        self.dims = (2,) * self.chip_bits
        near = list(range(1, min(4, self.bits)))
        self.far = list(range(self.bits - 1, near[-1], -1))
        self.turns = [near[i:] + near[:i] for i in range(len(near))]

    def order(self, part):
        return self.far + self.turns[part % len(self.turns)]

    @staticmethod
    def fits(count, rows):
        return count >= 16 and count & (count - 1) == 0 and rows % 8 == 0


def my_place(plan):
    me = lax.axis_index("dp")
    bit = [lax.rem(lax.div(me, jnp.int32(1 << b)), jnp.int32(2)) for b in range(plan.bits)]
    other = [me + (1 - 2 * bit[b]) * (1 << b) for b in range(plan.bits)]
    return me, bit, other


def greet(plan, other):
    barrier = pltpu.get_barrier_semaphore()
    for b in range(plan.bits):
        pl.semaphore_signal(barrier, inc=1, device_id=(other[b],), device_id_type=MESH)
    pl.semaphore_wait(barrier, plan.bits)


class Gather:
    def __init__(self, plan, bit, other, send, recv):
        self.plan, self.bit, self.other, self.send, self.recv = plan, bit, other, send, recv

    def cols(self, part, mine):
        buf, src, stage, at, width = part["buf"], part["src"], part["stage"], part["at"], part["width"]
        if not part["split"]:
            return pl.ds(at, width)
        half = width // 2
        which = self.bit[0] if mine else 1 - self.bit[0]
        return pl.ds(pl.multiple_of(at + which * half, LANES), half)

    def copy(self, part, phase):
        plan, i = self.plan, part["i"]
        if phase == 0:
            cols = self.cols(part, False)
            src, dst, to = part["src"].at[:, cols], part["stage"], self.other[0]
        elif phase <= plan.chip_bits:
            order = plan.order(part["turn"])
            done, b = order[: phase - 1], order[phase - 1]
            idx = tuple(
                slice(None) if bb in done else self.bit[bb] for bb in range(plan.bits - 1, 0, -1)
            )
            ref = part["buf"].at[idx + (slice(None), self.cols(part, True))]
            src, dst, to = ref, ref, self.other[b]
        else:
            ref = part["buf"].at[(slice(None),) * (plan.chip_bits + 1) + (self.cols(part, True),)]
            src, dst, to = ref, ref, self.other[0]
        return pltpu.make_async_remote_copy(
            src_ref=src, dst_ref=dst, send_sem=self.send.at[i, phase], recv_sem=self.recv.at[i, phase],
            device_id=(to,), device_id_type=MESH,
        )

    def phases(self, part):
        return self.plan.chip_bits + (2 if part["split"] else 1)

    def start(self, part, phase):
        self.copy(part, phase).start()

    def wait(self, part, phase):
        self.copy(part, phase).wait()
        if phase == 0:
            cols = self.cols(part, True)
            own, got = part["src"][:, cols], part["stage"][...]
            lower = self.bit[0] == 0
            rows = jnp.concatenate([jnp.where(lower, own, got), jnp.where(lower, got, own)], 0)
            idx = tuple(self.bit[bb] for bb in range(self.plan.bits - 1, 0, -1))
            part["buf"][idx + (slice(None), cols)] = rows.astype(BF)

    def advance(self, part, phase):
        self.wait(part, phase)
        if phase + 1 < self.phases(part):
            self.start(part, phase + 1)


class Scatter:
    def __init__(self, plan, bit, other, send, recv):
        self.plan, self.bit, self.other, self.send, self.recv = plan, bit, other, send, recv

    def cols(self, part, mine):
        half = part["width"] // 2
        which = self.bit[0] if mine else 1 - self.bit[0]
        return pl.ds(pl.multiple_of(part["at"] + which * half, LANES), half)

    def order(self, part):
        return self.plan.order(part["turn"])[::-1]

    def index(self, part, phase, mine):
        done, b = self.order(part)[: phase - 1], self.order(part)[phase - 1]
        idx = []
        for bb in range(self.plan.bits - 1, 0, -1):
            if bb in done:
                continue
            idx.append((self.bit[b] if mine else 1 - self.bit[b]) if bb == b else slice(None))
        return tuple(idx)

    def rows(self, which):
        r = self.plan_rows
        return pl.ds(pl.multiple_of(which * r, 8), r)

    def copy(self, part, phase):
        plan, i = self.plan, part["i"]
        every = (slice(None),) * (plan.chip_bits + 1)
        if phase == 0:
            if part["split"]:
                src = part["src"].at[every + (self.cols(part, False),)]
            else:
                src = part["src"]
            dst, to = part["slots"][0], self.other[0]
        elif phase <= plan.chip_bits:
            src = part["slots"][phase - 1].at[self.index(part, phase, False)]
            dst, to = part["slots"][phase], self.other[self.order(part)[phase - 1]]
        else:
            r = part["sum"].shape[0] // 2
            src = part["sum"].at[pl.ds(pl.multiple_of((1 - self.bit[0]) * r, 8), r)]
            dst, to = part["last"], self.other[0]
        return pltpu.make_async_remote_copy(
            src_ref=src, dst_ref=dst, send_sem=self.send.at[i, phase], recv_sem=self.recv.at[i, phase],
            device_id=(to,), device_id_type=MESH,
        )

    def phases(self, part):
        return self.plan.chip_bits + (2 if part["split"] else 1)

    def start(self, part, phase):
        self.copy(part, phase).start()

    def wait(self, part, phase):
        plan = self.plan
        self.copy(part, phase).wait()
        every = (slice(None),) * (plan.chip_bits + 1)
        if phase > plan.chip_bits:
            return
        slot = part["slots"][phase]
        if phase == 0:
            if part["split"]:
                mine = part["src"][every + (self.cols(part, True),)]
            else:
                mine = part["src"][...]
        else:
            mine = part["slots"][phase - 1][self.index(part, phase, True)]
        if phase == plan.chip_bits:
            part["sum"][...] = mine.astype(F32) + slot[...].astype(F32)
        else:
            slot[...] = mine + slot[...]

    def advance(self, part, phase):
        self.wait(part, phase)
        if phase + 1 < self.phases(part):
            self.start(part, phase + 1)

    def finish(self, part, out):
        r = part["sum"].shape[0] // 2
        own = part["sum"][pl.ds(pl.multiple_of(self.bit[0] * r, 8), r), :]
        if not part["split"]:
            out[...] = own
            return
        half = part["width"] // 2
        out[:, self.cols(part, True)] = own
        out[:, self.cols(part, False)] = part["last"][...]


def norm_exchange(plan, me, squares, mine, boxes, send, recv):
    mine[...] = jnp.full((8, LANES), squares, F32)
    copies = []
    for d in range(1, plan.count):
        copies.append(pltpu.make_async_remote_copy(
            src_ref=mine, dst_ref=boxes.at[d - 1], send_sem=send.at[d - 1], recv_sem=recv.at[d - 1],
            device_id=(lax.rem(me + d, jnp.int32(plan.count)),), device_id_type=MESH,
        ))
    for c in copies:
        c.start()
    for c in copies:
        c.wait()
    return mine[...] + jnp.sum(boxes[...], 0)


def ring_partners(plan, me):
    return [lax.rem(me + d, jnp.int32(plan.count)) for d in range(1, plan.count)]


def mat(ref, *cols):
    value = ref[(slice(None),) * (len(ref.shape) - 1) + cols] if cols else ref[...]
    return value.reshape(-1, value.shape[-1])


def front_kernel(*refs, plan, hd, mols, wide, seq, steps, steps2):
    refs = list(refs)
    take = lambda k: [refs.pop(0) for _ in range(k)]
    counts, tokens, eig, ends, cot = take(5)
    s_in, s_out, s_up, s_down, label_t, vec = take(6)
    out_o, proj_o, lse_o, dmid_o, dmix_o, labt_o, gout_o, gup_o, gdown_o, gvec_o, smallt_o, emb_o, inp_o, win_o = take(14)
    w_in, w_out, w_up, w_down, small = take(5)
    stages = take(1 + 6 * len(units(hd.dim * HEADS)))
    small_t, masks, tok_s, emb_s, inp_s, mixed_s, p_buf, acc_out, acc_up, acc_down, acc_vec = take(11)
    send, recv, keep = take(3)
    s_small, vec_s = take(2)
    step = pl.program_id(0)
    width = w_out.shape[-1]
    across_tiles = width // LANES
    score = hd.dim ** -0.5
    rows_all = mols * seq
    me, bit, other = my_place(plan)
    gather = Gather(plan, bit, other, send, recv)
    make = lambda i, src, buf, at, wide, split, t: dict(
        i=i, src=src, buf=buf, stage=stages[i], at=at, width=wide, split=split, turn=t
    )
    early = [make(0, s_small, small, 0, SMALL, False, 0)]
    late = []
    for src, buf, group in ((s_in, w_in, early), (s_out, w_out, late), (s_up, w_up, late), (s_down, w_down, late)):
        for at, unit in units(buf.shape[-1]):
            n = len(early) + len(late)
            group.append(make(n, src, buf, at, unit, True, n))
    final = plan.chip_bits + 1
    kept = [pltpu.make_async_copy(a, b, keep.at[i]) for i, (a, b) in enumerate(((w_in, win_o), (emb_s, emb_o), (inp_s, inp_o)))]
    get_tokens = pltpu.make_async_copy(tokens, tok_s, keep.at[3])

    row = lambda i: small_t[i : i + 1, :]

    def embed(group, carry):
        iota0 = lax.broadcasted_iota(jnp.int32, (seq, seq), 0)
        iota1 = lax.broadcasted_iota(jnp.int32, (seq, seq), 1)
        token_row = lax.broadcasted_iota(jnp.int32, (1, seq), 1)
        kind_row = lax.broadcasted_iota(jnp.int32, (16, seq), 0)
        one = lambda c: c.astype(F32).astype(BF)
        label_rows = []
        for g in range(mols):
            m = group * mols + g
            nodes = counts[0, m]
            live = nodes + counts[1, m]
            eig_f = eig[m]
            shift = one(jnp.logical_and(iota1 - iota0 == nodes, iota1 < live))
            picks = jnp.concatenate([one(iota0 == ends[m, end : end + 1, :]) for end in range(2)], 1)
            edge_lab = nn(eig_f.astype(BF), picks).astype(BF)
            moved = nn(jnp.concatenate([edge_lab[:, :seq], edge_lab[:, seq:]], 0), shift)
            at_node = token_row < nodes
            is_node = at_node.astype(F32)
            is_edge = jnp.logical_and(token_row >= nodes, token_row < live).astype(F32)
            kind = jnp.where(kind_row == 0, is_node, jnp.where(kind_row == 1, is_edge, 0.0))
            lab = jnp.concatenate(
                [jnp.where(at_node, eig_f, moved[:16]), jnp.where(at_node, eig_f, moved[16:]), kind], 0
            )
            labt_o[m] = lab.astype(BF)
            pad = jnp.zeros((SMALL - lab.shape[0], seq), F32)
            label_rows.append(jnp.concatenate([lab, pad], 0).T.astype(BF))
        labels = jnp.concatenate(label_rows, 0)
        here = pl.ds(pl.multiple_of(group * rows_all, rows_all), rows_all)
        embedded = tok_s[here, :].astype(F32) + nn(labels, small_t[...].astype(BF))
        emb_s[here, :] = embedded
        normed, _ = layer_stats(embedded)
        value = (normed * row(GAIN1) + row(SHIFT1)).astype(BF)
        for t in range(across_tiles):
            inp_s[t, here, :] = value[:, t * LANES : (t + 1) * LANES]
        return carry

    @pl.when(step == 0)
    def _():
        get_tokens.start()
        vec_s[...] = jnp.zeros_like(vec_s)
        vec_s[32:34, : vec.shape[1]] = vec[9:11, :]
        vec_s[34:43, : vec.shape[1]] = vec[0:9, :]
        s_small[...] = vec_s[...].T[: s_small.shape[0], :]
        s_small[:, :32] = label_t[...]
        greet(plan, other)
        for part in early + late:
            gather.start(part, 0)
        set_masks(hd, masks)
        acc_out[...] = jnp.zeros_like(acc_out)
        acc_up[...] = jnp.zeros_like(acc_up)
        acc_down[...] = jnp.zeros_like(acc_down)
        acc_vec[...] = jnp.zeros_like(acc_vec)
        for phase in range(final):
            for part in early:
                if part["split"] and phase == final - 1:
                    continue
                gather.advance(part, phase)
        small_t[...] = mat(small).astype(F32).T
        smallt_o[...] = small_t[...]
        get_tokens.wait()
        cut = (steps + 1) // 2
        lax.fori_loop(0, cut, embed, 0)
        for part in early[1:]:
            gather.advance(part, final - 1)
        lax.fori_loop(cut, steps, embed, 0)
        for part in early[1:]:
            gather.advance(part, final)
        for part in late:
            gather.advance(part, 0)
        for copy in kept:
            copy.start()

    def attend(some, between=()):
        between = list(between)
        for m in some:
            nodes = counts[0, step * mols + m]
            live = nodes + counts[1, step * mols + m]
            key_live = lax.broadcasted_iota(jnp.int32, (seq, 2 * seq), 0) < live
            rows = slice(m * seq, (m + 1) * seq)
            for b in range(hd.blocks):
                get = lambda part: [proj_o[part * across_tiles + b * hd.tiles + t, rows, :] for t in range(hd.tiles)]
                q, k, v = [dense(x) for x in get(0)], get(1), [dense(x) for x in get(2)]
                for pair in range(hd.block // 2):
                    scores = nt(pair_full(hd, k, pair), pair_rows(hd, masks, q, pair))
                    scores = jnp.where(key_live, scores, MASK_FILL)
                    top = jnp.max(scores, 0, keepdims=True)
                    ex = jnp.exp2((scores - top) * (score * LOG2E))
                    total = jnp.sum(ex, 0, keepdims=True)
                    shares = (ex * (1.0 / total)).astype(BF)
                    at = b * (hd.block // 2) + pair
                    lse_o[m, at : at + 1, :] = top + jnp.log2(total) * (1.0 / (score * LOG2E))
                    for i in range(2):
                        p_buf[b * hd.block + 2 * pair + i] = shares[:, i * seq : (i + 1) * seq].T
                    if between and pair % EVERY == 0:
                        between.pop(0)()
                for t in range(hd.tiles):
                    hs = hd.heads_of(t)
                    mixed = nn(across([p_buf[b * hd.block + h] for h in hs]), tile_rows(hd, masks, v[t], t))
                    put = pl.ds(pl.multiple_of(step * rows_all + m * seq, seq), seq)
                    mixed_s[b * hd.tiles + t, put, :] = mixed.astype(BF)
        for run in between:
            run()

    @pl.when(step < steps)
    def _():
        here = pl.ds(pl.multiple_of(step * rows_all, rows_all), rows_all)
        half = rows_all // 2

        def project(n, part, cols):
            at = pl.ds(pl.multiple_of(step * rows_all + n * half, half), half)
            value = nn(
                across([inp_s[t, at, :] for t in range(across_tiles)]),
                mat(w_in, slice(part * width + cols.start, part * width + cols.stop)),
            )
            if part == 0:
                value = value + small_t[QBIAS : QBIAS + 1, cols]
            if part == 2:
                value = value + small_t[VBIAS : VBIAS + 1, cols]
            value = value.astype(BF)
            for t in range((cols.stop - cols.start) // LANES):
                tile = part * across_tiles + cols.start // LANES + t
                proj_o[tile, n * half : (n + 1) * half, :] = value[:, t * LANES : (t + 1) * LANES]

        for part in range(3):
            project(0, part, slice(0, width))
        later = [
            functools.partial(project, 1, part, slice(at, at + unit)) for part in range(3) for at, unit in units(width)
        ]
        attend(range(mols // 2), later)

    def pump(half):
        for phase in range(1, final + 1):
            slot = min(SLOTS_GATHER[min(phase, 4) - 1] + max(phase - 4, 0), 2 * steps - 1)
            if slot % 2 == half:
                @pl.when(step == slot // 2)
                def _():
                    for part in late:
                        gather.advance(part, phase)

    pump(0)

    @pl.when(step < steps)
    def _():
        attend(range(mols // 2, mols))

    pump(1)

    @pl.when(step >= steps)
    def _():
        parts = 1
        size = wide // parts
        add = lambda v: jnp.sum(v, 0, keepdims=True)
        stack = lambda vs: vs[0] if parts == 1 else jnp.concatenate(vs, 0)
        runs = [slice(r * size, (r + 1) * size) for r in range(parts)]
        here = [pl.ds(pl.multiple_of((step - steps) * wide + r * size, size), size) for r in range(parts)]
        mixed = [across([mixed_s[t, h, :] for t in range(across_tiles)]) for h in here]
        branch_in = [nt(x, mat(w_out)) for x in mixed]
        middle, norms, inputs = [], [], []
        for h, x in zip(here, branch_in):
            middle.append(emb_s[h, :] + (x + row(OBIAS)))
            norms.append(layer_stats(middle[-1]))
            inputs.append((norms[-1][0] * row(GAIN2) + row(SHIFT2)).astype(BF))
        acts, d_pres, backs = [], [], [cot[r, :] for r in runs]
        for x, back in zip(inputs, backs):
            pre = nn(x, mat(w_up)) + row(UBIAS)
            half_erf = 0.5 * (1.0 + lax.erf(pre * SQRT_HALF))
            acts.append((pre * half_erf).astype(BF))
            slope = half_erf + pre * jnp.exp(-0.5 * pre * pre) * INV_SQRT_TWO_PI
            d_pres.append((nn(back, mat(w_down)) * slope).astype(BF))
        d_ins = [nt(x, mat(w_up)) for x in d_pres]
        branches = []
        totals = {i: [] for i in (OBIAS, GAIN2, SHIFT2, UBIAS, DBIAS)}
        def close(n):
            r, back_f, d_in2, (normed2, recip2) = runs[n], backs[n].astype(F32), d_ins[n], norms[n]
            d_mid = back_f + norm_back(d_in2, normed2, recip2, row(GAIN2))
            dmid_o[r, :] = d_mid
            branches.append(d_mid.astype(BF))
            totals[OBIAS].append(add(branches[-1].astype(F32)))
            totals[GAIN2].append(add(d_in2 * normed2))
            totals[SHIFT2].append(add(d_in2))
            totals[UBIAS].append(add(d_pres[n].astype(F32)))
            totals[DBIAS].append(add(back_f))
        def output():
            for r, mid, act in zip(runs, middle, acts):
                out_o[r, :] = (mid + (nt(act, mat(w_down)) + row(DBIAS))).astype(BF)
        def down():
            acc_down[...] += tn(stack(backs), stack(acts))
        def up():
            acc_up[...] += tn(stack(inputs), stack(d_pres))
        output()
        close(0)
        down()
        up()
        for r, x in zip(runs, branches):
            d_mixed = nn(x, mat(w_out)).astype(BF)
            for t in range(across_tiles):
                dmix_o[t, r, :] = d_mixed[:, t * LANES : (t + 1) * LANES]
        acc_out[...] += tn(stack(branches), stack(mixed))
        for i, vs in totals.items():
            acc_vec[i - 34 : i - 33, :] += sum(vs)

    @pl.when(step == steps + steps2 - 1)
    def _():
        for acc, out in ((acc_out, gout_o), (acc_up, gup_o), (acc_down, gdown_o)):
            out[...] = acc[...].astype(BF)
        gvec_o[...] = acc_vec[...]
        for copy in kept:
            copy.wait()


class ShareSmall:
    def __init__(self, plan, me, src, boxes, part, boxes2, send, recv):
        self.src, self.boxes, self.part, self.boxes2 = src, boxes, part, boxes2
        low = src.shape[1]
        high = plan.count // low
        self.place, self.level = lax.rem(me, jnp.int32(low)), lax.div(me, jnp.int32(low))
        self.one, self.two = [], []
        for d in range(1, low):
            to = lax.rem(self.place + d, jnp.int32(low))
            self.one.append(pltpu.make_async_remote_copy(
                src_ref=src.at[:, to], dst_ref=boxes.at[d - 1], send_sem=send.at[d - 1], recv_sem=recv.at[d - 1],
                device_id=(me + to - self.place,), device_id_type=MESH,
            ))
        for d in range(1, high):
            to = lax.rem(self.level + d, jnp.int32(high))
            at = low - 2 + d
            self.two.append(pltpu.make_async_remote_copy(
                src_ref=part.at[to], dst_ref=boxes2.at[d - 1], send_sem=send.at[at], recv_sem=recv.at[at],
                device_id=(me + (to - self.level) * low,), device_id_type=MESH,
            ))

    def begin(self):
        for c in self.one:
            c.start()

    def middle(self):
        total = self.src[:, self.place]
        for d, c in enumerate(self.one):
            c.wait()
            total = total + self.boxes[d]
        self.part[...] = total
        for c in self.two:
            c.start()

    def end(self):
        total = self.part[self.level]
        for d, c in enumerate(self.two):
            c.wait()
            total = total + self.boxes2[d]
        return total


def back_kernel(*refs, plan, hd, mols, wide, seq, steps, steps2):
    refs = list(refs)
    take = lambda k: [refs.pop(0) for _ in range(k)]
    counts, proj, lse, inp, emb, dmid, dmix, labt, w_in, small_t, gvec, g_out, g_up, g_down = take(14)
    tg_o, o_in, o_out, o_up, o_down, o_small, o_norm = take(7)
    masks, pt_buf, dst_buf, ds_buf, dproj_s, acc_in, g_in, acc_vec, acc_lab = take(9)
    k = plan.chip_bits + 1
    count = 6 * len(units(hd.dim * HEADS))
    slots = [take(k) for _ in range(count)]
    part_sums, lasts = take(count), take(count)
    send, recv = take(2)
    small_s, small_box, small_part, small_box2, ssend, srecv = take(6)
    mine, boxes, nsend, nrecv = take(4)
    step = pl.program_id(0)
    width = g_out.shape[-1]
    across_tiles = width // LANES
    score = hd.dim ** -0.5
    rows_all = mols * seq
    me, bit, other = my_place(plan)
    scatter = Scatter(plan, bit, other, send, recv)
    parts, late, early = [], [], []
    for src, out, group in ((g_in, o_in, late), (g_out, o_out, early), (g_up, o_up, early), (g_down, o_down, early)):
        for at, unit in units(src.shape[-1]):
            i = len(parts)
            part = dict(i=i, src=src, slots=slots[i], at=at, width=unit, split=True, turn=i, sum=part_sums[i],
                        last=lasts[i], out=out)
            parts.append(part)
            group.append(part)
    final = plan.chip_bits + 1

    @pl.when(step == 0)
    def _():
        barrier = pltpu.get_barrier_semaphore()
        partners = ring_partners(plan, me)
        for p in partners:
            pl.semaphore_signal(barrier, inc=1, device_id=(p,), device_id_type=MESH)
        pl.semaphore_wait(barrier, len(partners))
        for part in early:
            scatter.start(part, 0)
        set_masks(hd, masks)
        acc_in[...] = jnp.zeros_like(acc_in)
        acc_vec[...] = gvec[...]
        acc_lab[...] = jnp.zeros_like(acc_lab)

    row = lambda i: small_t[i : i + 1, :]

    def attend(some):
        for m in some:
            nodes = counts[0, step * mols + m]
            live = nodes + counts[1, step * mols + m]
            key_live = lax.broadcasted_iota(jnp.int32, (seq, 2 * seq), 0) < live
            rows = slice(m * seq, (m + 1) * seq)
            put = pl.ds(pl.multiple_of(step * rows_all + m * seq, seq), seq)
            for b in range(hd.blocks):
                get = lambda ref, part: [ref[part * across_tiles + b * hd.tiles + t, rows, :] for t in range(hd.tiles)]
                q, k, v, do = [dense(x) for x in get(proj, 0)], get(proj, 1), get(proj, 2), [dense(x) for x in get(dmix, 0)]
                k_dense = [dense(x) for x in k]
                for pair in range(hd.block // 2):
                    scores = nt(pair_full(hd, k, pair), pair_rows(hd, masks, q, pair))
                    scores = jnp.where(key_live, scores, MASK_FILL)
                    at = b * (hd.block // 2) + pair
                    p = jnp.exp2((scores - lse[m, at : at + 1, :]) * (score * LOG2E))
                    dp = nt(pair_full(hd, v, pair), pair_rows(hd, masks, do, pair))
                    inner = jnp.sum(p * dp, 0, keepdims=True)
                    ds = (p * (dp - inner)).astype(BF)
                    p = p.astype(BF)
                    for i in range(2):
                        h = b * hd.block + 2 * pair + i
                        pt_buf[h] = p[:, i * seq : (i + 1) * seq]
                        dst_buf[h] = ds[:, i * seq : (i + 1) * seq]
                        ds_buf[h] = ds[:, i * seq : (i + 1) * seq].T
                for t in range(hd.tiles):
                    hs = [b * hd.block + h for h in hd.heads_of(t)]
                    at = b * hd.tiles + t
                    d_v = nn(across([pt_buf[h] for h in hs]), tile_rows(hd, masks, do[t], t))
                    d_k = nn(across([dst_buf[h] for h in hs]), tile_rows(hd, masks, q[t], t)) * score
                    d_q = nn(across([ds_buf[h] for h in hs]), tile_rows(hd, masks, k_dense[t], t)) * score
                    dproj_s[at, put, :] = d_q.astype(BF)
                    dproj_s[across_tiles + at, put, :] = d_k.astype(BF)
                    dproj_s[2 * across_tiles + at, put, :] = d_v.astype(BF)

    @pl.when(step < steps)
    def _():
        attend(range(mols // 2))

    def pump(half):
        for phase in range(final + 1):
            slot = min(SLOTS_SCATTER[min(phase, 4)] + max(phase - 4, 0), 2 * steps - 1)
            if slot % 2 == half:
                @pl.when(step == slot // 2)
                def _():
                    for part in early:
                        scatter.advance(part, phase)

    pump(0)

    @pl.when(step < steps)
    def _():
        attend(range(mols // 2, mols))
        here = pl.ds(pl.multiple_of(step * rows_all, rows_all), rows_all)
        input_one = across([inp[t] for t in range(across_tiles)])
        d_proj = across([dproj_s[t, here, :] for t in range(3 * across_tiles)])
        acc_in[...] += tn(input_one, d_proj)
        add = lambda v: jnp.sum(v, 0, keepdims=True)
        acc_vec[QBIAS - 34 : QBIAS - 33, :] += add(d_proj[:, :width].astype(F32))
        acc_vec[VBIAS - 34 : VBIAS - 33, :] += add(d_proj[:, 2 * width :].astype(F32))

    pump(1)

    @pl.when(step == steps - 1)
    def _():
        for part in late:
            cols = slice(part["at"], part["at"] + part["width"])
            g_in[(slice(None),) * (plan.chip_bits + 1) + (cols,)] = acc_in[:, cols].astype(BF).reshape(
                g_in.shape[:-1] + (part["width"],)
            )
            scatter.start(part, 0)

    @pl.when(step >= steps)
    def _():
        here = pl.ds(pl.multiple_of((step - steps) * wide, wide), wide)
        normed, recip = layer_stats(emb[...])
        d_proj = across([dproj_s[t, here, :] for t in range(3 * across_tiles)])
        d_in1 = nt(d_proj, mat(w_in))
        tg = dmid[...] + norm_back(d_in1, normed, recip, row(GAIN1))
        tg_o[...] = tg
        tg_hi = tg.astype(BF)
        tg_lo = (tg - tg_hi.astype(F32)).astype(BF)
        lab = jnp.concatenate([labt[m] for m in range(wide // seq)], 1)
        acc_lab[...] += nn(lab, tg_hi)
        acc_lab[32:48, :] += nn(lab[32:48, :], tg_lo)
        add = lambda v: jnp.sum(v, 0, keepdims=True)
        acc_vec[GAIN1 - 34 : GAIN1 - 33, :] += add(d_in1 * normed)
        acc_vec[SHIFT1 - 34 : SHIFT1 - 33, :] += add(d_in1)

    for phase in range(min(final, steps2 - 1)):
        @pl.when(step == steps + phase)
        def _():
            for part in late:
                scatter.advance(part, phase)

    @pl.when(step == steps + steps2 - 1)
    def _():
        full = jnp.concatenate(
            [acc_lab[0:32, :], acc_lab[32:34, :], acc_vec[0:9, :], jnp.zeros((SMALL - 43, width), F32)], 0
        )
        small_s[...] = full.T.reshape(small_s.shape)
        share = ShareSmall(plan, me, small_s, small_box, small_part, small_box2, ssend, srecv)
        share.begin()
        for phase in range(min(final, steps2 - 1), final + 1):
            for part in late:
                scatter.advance(part, phase)
            if phase == final - 1:
                share.middle()
        o_small[...] = share.end()
        for part in parts:
            scatter.finish(part, part["out"])
        total = sum(jnp.sum(o[...] * o[...]) for o in (o_small, o_in, o_out, o_up, o_down))
        o_norm[...] = jnp.sqrt(norm_exchange(plan, me, total, mine, boxes, nsend, nrecv))


def paired_layer(plan, tokens, eig_t, counts_t, ends_t, cot, shards, mols_step):
    count, width = tokens.shape
    mols_all, lap, seq = eig_t.shape
    shard = shards[0].shape[0]
    parts = len(units(width))
    hd = Heads(width)
    steps = mols_all // mols_step
    rows = mols_step * seq
    wide = min(WIDE, count)
    steps2 = count // wide
    across_tiles = width // LANES
    last = steps - 1
    first = lambda i: lax.min(i, last)
    second = lambda i: lax.max(i - steps, 0)
    tok2 = lambda w: pl.BlockSpec((wide, w), lambda i: (second(i), 0))
    mol = lambda a, b: pl.BlockSpec((mols_step, a, b), lambda i: (first(i), 0, 0))
    tiled = lambda n: pl.BlockSpec((n, rows, LANES), lambda i: (0, first(i), 0))
    tiled2 = lambda n: pl.BlockSpec((n, wide, LANES), lambda i: (0, second(i), 0))
    sizes = dict(plan=plan, hd=hd, mols=mols_step, wide=wide, seq=seq, steps=steps, steps2=steps2)
    vm, sm, hbm = (pl.BlockSpec(memory_space=m) for m in (pltpu.VMEM, pltpu.SMEM, pl.ANY))
    sq = (width, width)
    buf = lambda c: plan.dims + (2 * shard, c)
    f32 = lambda *shape: jax.ShapeDtypeStruct(shape, F32)
    bf = lambda *shape: jax.ShapeDtypeStruct(shape, BF)
    params = lambda cid: pltpu.CompilerParams(
        vmem_limit_bytes=VMEM_LIMIT, dimension_semantics=("arbitrary",), collective_id=cid,
        has_side_effects=True,
    )
    out, proj, lse, dmid, dmix, labt, g_out, g_up, g_down, g_vec, small_t, emb, inp, w_in = pl.pallas_call(
        functools.partial(front_kernel, **sizes),
        grid=(steps + steps2,),
        in_specs=[sm, hbm, vm, vm, tok2(width)] + [vm] * 6,
        out_specs=[tok2(width), tiled(3 * across_tiles), mol(HEADS // 2, 2 * seq), tok2(width), tiled2(across_tiles)]
        + [vm] * 6 + [hbm] * 3,
        out_shape=[bf(count, width), bf(3 * across_tiles, count, LANES), f32(mols_all, HEADS // 2, 2 * seq),
                   f32(count, width), bf(across_tiles, count, LANES), bf(mols_all, 48, seq),
                   bf(*sq), bf(*sq), bf(*sq), f32(16, width), f32(SMALL, width),
                   f32(count, width), bf(across_tiles, count, LANES), bf(*buf(3 * width))],
        scratch_shapes=[pltpu.VMEM(buf(c), BF) for c in (3 * width, width, width, width, SMALL)]
        + [pltpu.VMEM((shard, SMALL), F32)] + [pltpu.VMEM((shard, LANES), F32)] * (6 * parts)
        + [
            pltpu.VMEM((SMALL, width), F32),
            pltpu.VMEM((hd.slots(), 16, LANES), BF),
            pltpu.VMEM((count, width), BF),
            pltpu.VMEM((count, width), F32),
            pltpu.VMEM((across_tiles, count, LANES), BF),
            pltpu.VMEM((across_tiles, count, LANES), BF),
            pltpu.VMEM((HEADS, seq, seq), BF),
            pltpu.VMEM(sq, F32), pltpu.VMEM(sq, F32), pltpu.VMEM(sq, F32),
            pltpu.VMEM((16, width), F32),
        ]
        + [pltpu.SemaphoreType.DMA((6 * parts + 1, plan.chip_bits + 2))] * 2 + [pltpu.SemaphoreType.DMA((4,))]
        + [pltpu.VMEM((shard, SMALL), F32), pltpu.VMEM((SMALL, LANES), F32)],
        compiler_params=params(0),
        name="front",
    )(counts_t, tokens, eig_t, ends_t, cot, *shards)

    low = 1 << min(3, plan.bits)
    high = plan.count // low
    boxes = low - 1 + high - 1
    slots = [pltpu.VMEM(plan.dims[j:] + (2 * shard, LANES), BF) for j in range(plan.chip_bits + 1)]
    shaped = [g.reshape(buf(width)) for g in (g_out, g_up, g_down)]
    tg, *sums, norm = pl.pallas_call(
        functools.partial(back_kernel, **sizes),
        grid=(steps + steps2,),
        in_specs=[sm, tiled(3 * across_tiles), mol(HEADS // 2, 2 * seq), tiled(across_tiles), tok2(width), tok2(width),
                  tiled(across_tiles), pl.BlockSpec((wide // seq, 48, seq), lambda i: (second(i), 0, 0))] + [vm] * 6,
        out_specs=[tok2(width)] + [vm] * 6,
        out_shape=[f32(count, width), f32(shard, 3 * width), f32(shard, width), f32(shard, width), f32(shard, width),
                   f32(shard, SMALL), f32(8, LANES)],
        scratch_shapes=[
            pltpu.VMEM((hd.slots(), 16, LANES), BF),
            pltpu.VMEM((HEADS, seq, seq), BF),
            pltpu.VMEM((HEADS, seq, seq), BF),
            pltpu.VMEM((HEADS, seq, seq), BF),
            pltpu.VMEM((3 * across_tiles, count, LANES), BF),
            pltpu.VMEM((width, 3 * width), F32),
            pltpu.VMEM(buf(3 * width), BF),
            pltpu.VMEM((16, width), F32),
            pltpu.VMEM((48, width), F32),
        ]
        + slots * (6 * parts)
        + [pltpu.VMEM((2 * shard, LANES), F32)] * (6 * parts) + [pltpu.VMEM((shard, LANES), F32)] * (6 * parts)
        + [pltpu.SemaphoreType.DMA((6 * parts, plan.chip_bits + 2))] * 2
        + [
            pltpu.VMEM((high, low, shard, SMALL), F32),
            pltpu.VMEM((low - 1, high, shard, SMALL), F32),
            pltpu.VMEM((high, shard, SMALL), F32),
            pltpu.VMEM((max(high - 1, 1), shard, SMALL), F32),
        ]
        + [pltpu.SemaphoreType.DMA((boxes,))] * 2
        + [pltpu.VMEM((8, LANES), F32), pltpu.VMEM((plan.count - 1, 8, LANES), F32)]
        + [pltpu.SemaphoreType.DMA((plan.count - 1,))] * 2,
        compiler_params=params(1),
        name="back",
    )(counts_t, proj, lse, inp, emb, dmid, dmix, labt, w_in, small_t, g_vec, *shaped)
    return out, tg, sums, norm


def plain_front_kernel(
    counts, tokens, eig, ends, cot, w_in, w_out, w_up, w_down, small,
    out_o, proj_o, lse_o, emb_o, dmid_o, dmix_o, labt_o, gout_o, gup_o, gdown_o, gvec_o,
    small_t, masks, mixed_s, p_buf, acc_out, acc_up, acc_down, acc_vec,
    *, hd, mols, seq, steps,
):
    step = pl.program_id(0)
    width = w_in.shape[0]
    across_tiles = width // LANES
    score = hd.dim ** -0.5

    @pl.when(step == 0)
    def _():
        small_t[...] = small[...].astype(F32).T
        set_masks(hd, masks)
        acc_out[...] = jnp.zeros_like(acc_out)
        acc_up[...] = jnp.zeros_like(acc_up)
        acc_down[...] = jnp.zeros_like(acc_down)
        acc_vec[...] = jnp.zeros_like(acc_vec)

    row = lambda i: small_t[i : i + 1, :]
    iota0 = lax.broadcasted_iota(jnp.int32, (seq, seq), 0)
    iota1 = lax.broadcasted_iota(jnp.int32, (seq, seq), 1)
    token_row = lax.broadcasted_iota(jnp.int32, (1, seq), 1)
    one = lambda c: c.astype(F32).astype(BF)
    label_rows = []
    for m in range(mols):
        nodes = counts[0, step * mols + m]
        live = nodes + counts[1, step * mols + m]
        eig_f = eig[m]
        eig_low = eig_f.astype(BF)
        shift = one(jnp.logical_and(iota1 - iota0 == nodes, iota1 < live))
        halves = []
        for end in range(2):
            pick = one(iota0 == ends[m, end : end + 1, :])
            edge_lab = nn(eig_low, pick).astype(BF)
            moved = nn(edge_lab, shift)
            halves.append(jnp.where(token_row < nodes, eig_f, moved))
        is_node = (token_row < nodes).astype(F32)
        is_edge = jnp.logical_and(token_row >= nodes, token_row < live).astype(F32)
        kind = jnp.where(lax.broadcasted_iota(jnp.int32, (16, seq), 0) == 0, is_node,
                         jnp.where(lax.broadcasted_iota(jnp.int32, (16, seq), 0) == 1, is_edge, 0.0))
        lab = jnp.concatenate(halves + [kind], 0)
        labt_o[m] = lab.astype(BF)
        pad = jnp.zeros((SMALL - lab.shape[0], seq), F32)
        label_rows.append(jnp.concatenate([lab, pad], 0).T.astype(BF))
    labels = jnp.concatenate(label_rows, 0)
    embedded = tokens[...].astype(F32) + nn(labels, small_t[...].astype(BF))
    emb_o[...] = embedded
    normed, recip = layer_stats(embedded)
    input_one = (normed * row(GAIN1) + row(SHIFT1)).astype(BF)
    for part in range(3):
        cols = slice(part * width, (part + 1) * width)
        value = nn(input_one, w_in[:, cols])
        if part == 0:
            value = value + row(QBIAS)
        if part == 2:
            value = value + row(VBIAS)
        value = value.astype(BF)
        for t in range(across_tiles):
            proj_o[part * across_tiles + t] = value[:, t * LANES : (t + 1) * LANES]

    for m in range(mols):
        nodes = counts[0, step * mols + m]
        live = nodes + counts[1, step * mols + m]
        key_live = lax.broadcasted_iota(jnp.int32, (seq, 2 * seq), 0) < live
        rows = slice(m * seq, (m + 1) * seq)
        for b in range(hd.blocks):
            base = b * hd.tiles * LANES
            get = lambda part: [proj_o[part * across_tiles + b * hd.tiles + t, rows, :] for t in range(hd.tiles)]
            q, k, v = get(0), get(1), get(2)
            for pair in range(hd.block // 2):
                scores = nt(pair_full(hd, k, pair), pair_rows(hd, masks, q, pair))
                scores = jnp.where(key_live, scores, MASK_FILL)
                top = jnp.max(scores, 0, keepdims=True)
                ex = jnp.exp2((scores - top) * (score * LOG2E))
                total = jnp.sum(ex, 0, keepdims=True)
                shares = (ex * (1.0 / total)).astype(BF)
                lse_o[m, b * (hd.block // 2) + pair : b * (hd.block // 2) + pair + 1, :] = (
                    top + jnp.log2(total) * (1.0 / (score * LOG2E))
                )
                for i in range(2):
                    h = 2 * pair + i
                    p_buf[b * hd.block + h] = shares[:, i * seq : (i + 1) * seq].T
            for t in range(hd.tiles):
                hs = hd.heads_of(t)
                mixed = nn(across([p_buf[b * hd.block + h] for h in hs]), tile_rows(hd, masks, v[t], t))
                mixed_s[b * hd.tiles + t, rows, :] = mixed.astype(BF)

    mixed = across([mixed_s[t] for t in range(across_tiles)])
    middle = embedded + (nt(mixed, w_out[...]) + row(OBIAS))
    normed2, recip2 = layer_stats(middle)
    input_two = (normed2 * row(GAIN2) + row(SHIFT2)).astype(BF)
    pre = nn(input_two, w_up[...]) + row(UBIAS)
    half_erf = 0.5 * (1.0 + lax.erf(pre * SQRT_HALF))
    act = (pre * half_erf).astype(BF)
    slope = half_erf + pre * jnp.exp(-0.5 * pre * pre) * INV_SQRT_TWO_PI
    out_o[...] = (middle + (nt(act, w_down[...]) + row(DBIAS))).astype(BF)
    back = cot[...]
    back_f = back.astype(F32)
    d_pre_f = nn(back, w_down[...]) * slope
    d_pre = d_pre_f.astype(BF)
    acc_down[...] += tn(back, act)
    acc_up[...] += tn(input_two, d_pre)
    d_in2 = nt(d_pre, w_up[...])
    d_mid = back_f + norm_back(d_in2, normed2, recip2, row(GAIN2))
    dmid_o[...] = d_mid
    branch = d_mid.astype(BF)
    acc_out[...] += tn(branch, mixed)
    d_mixed = nn(branch, w_out[...]).astype(BF)
    for t in range(across_tiles):
        dmix_o[t] = d_mixed[:, t * LANES : (t + 1) * LANES]
    add = lambda v: jnp.sum(v, 0, keepdims=True)
    sums = {
        OBIAS: add(branch.astype(F32)),
        GAIN2: add(d_in2 * normed2),
        SHIFT2: add(d_in2),
        UBIAS: add(d_pre.astype(F32)),
        DBIAS: add(back_f),
    }
    for i, v in sums.items():
        acc_vec[i - 34 : i - 33, :] += v

    @pl.when(step == steps - 1)
    def _():
        gout_o[...] = acc_out[...].astype(BF)
        gup_o[...] = acc_up[...].astype(BF)
        gdown_o[...] = acc_down[...].astype(BF)
        gvec_o[...] = acc_vec[...]


def plain_back_kernel(
    counts, proj, lse, emb, dmid, dmix, labt, w_in, small, gvec,
    tg_o, gin_o, gsmall_o,
    small_t, masks, pt_buf, dst_buf, ds_buf, dproj_s, acc_in, acc_vec, acc_lab,
    *, hd, mols, seq, steps,
):
    step = pl.program_id(0)
    width = w_in.shape[0]
    across_tiles = width // LANES
    score = hd.dim ** -0.5

    @pl.when(step == 0)
    def _():
        small_t[...] = small[...].astype(F32).T
        set_masks(hd, masks)
        acc_in[...] = jnp.zeros_like(acc_in)
        acc_vec[...] = gvec[...]
        acc_lab[...] = jnp.zeros_like(acc_lab)

    row = lambda i: small_t[i : i + 1, :]
    for m in range(mols):
        nodes = counts[0, step * mols + m]
        live = nodes + counts[1, step * mols + m]
        key_live = lax.broadcasted_iota(jnp.int32, (seq, 2 * seq), 0) < live
        rows = slice(m * seq, (m + 1) * seq)
        for b in range(hd.blocks):
            base = b * hd.tiles * LANES
            get = lambda ref, part: [ref[part * across_tiles + b * hd.tiles + t, rows, :] for t in range(hd.tiles)]
            q, k, v, do = get(proj, 0), get(proj, 1), get(proj, 2), get(dmix, 0)
            for pair in range(hd.block // 2):
                scores = nt(pair_full(hd, k, pair), pair_rows(hd, masks, q, pair))
                scores = jnp.where(key_live, scores, MASK_FILL)
                at = b * (hd.block // 2) + pair
                p = jnp.exp2((scores - lse[m, at : at + 1, :]) * (score * LOG2E))
                dp = nt(pair_full(hd, v, pair), pair_rows(hd, masks, do, pair))
                inner = jnp.sum(p * dp, 0, keepdims=True)
                ds = (p * (dp - inner)).astype(BF)
                p = p.astype(BF)
                for i in range(2):
                    h = b * hd.block + 2 * pair + i
                    pt_buf[h] = p[:, i * seq : (i + 1) * seq]
                    dst_buf[h] = ds[:, i * seq : (i + 1) * seq]
                    ds_buf[h] = ds[:, i * seq : (i + 1) * seq].T
            for t in range(hd.tiles):
                hs = [b * hd.block + h for h in hd.heads_of(t)]
                at = b * hd.tiles + t
                d_v = nn(across([pt_buf[h] for h in hs]), tile_rows(hd, masks, do[t], t))
                d_k = nn(across([dst_buf[h] for h in hs]), tile_rows(hd, masks, q[t], t)) * score
                d_q = nn(across([ds_buf[h] for h in hs]), tile_rows(hd, masks, k[t], t)) * score
                dproj_s[at, rows, :] = d_q.astype(BF)
                dproj_s[across_tiles + at, rows, :] = d_k.astype(BF)
                dproj_s[2 * across_tiles + at, rows, :] = d_v.astype(BF)

    normed, recip = layer_stats(emb[...])
    input_one = (normed * row(GAIN1) + row(SHIFT1)).astype(BF)
    d_proj = across([dproj_s[t] for t in range(3 * across_tiles)])
    acc_in[...] += tn(input_one, d_proj)
    d_in1 = nt(d_proj, w_in[...])
    tg = dmid[...] + norm_back(d_in1, normed, recip, row(GAIN1))
    tg_o[...] = tg
    tg_hi = tg.astype(BF)
    tg_lo = (tg - tg_hi.astype(F32)).astype(BF)
    lab = jnp.concatenate([labt[m] for m in range(mols)], 1)
    acc_lab[...] += nn(lab, tg_hi)
    acc_lab[32:48, :] += nn(lab[32:48, :], tg_lo)
    add = lambda v: jnp.sum(v, 0, keepdims=True)
    sums = {
        GAIN1: add(d_in1 * normed),
        SHIFT1: add(d_in1),
        QBIAS: add(d_proj[:, :width].astype(F32)),
        VBIAS: add(d_proj[:, 2 * width :].astype(F32)),
    }
    for i, v in sums.items():
        acc_vec[i - 34 : i - 33, :] += v

    @pl.when(step == steps - 1)
    def _():
        gin_o[...] = acc_in[...].astype(BF)
        full = jnp.concatenate(
            [acc_lab[0:32, :], acc_lab[32:34, :], acc_vec[0:9, :], jnp.zeros((SMALL - 43, width), F32)], 0
        )
        gsmall_o[...] = full.T.astype(BF)


def whole(shape):
    return pl.BlockSpec(shape, lambda *_: (0,) * len(shape), pipeline_mode=pl.Buffered(1))


def out_whole(shape):
    return pl.BlockSpec(shape, lambda *_: (0,) * len(shape))


def plain_layer(tokens, eig_t, counts_t, ends_t, cot, w_in, w_out, w_up, w_down, small, mols_step):
    count, width = tokens.shape
    mols_all, lap, seq = eig_t.shape
    hd = Heads(width)
    steps = mols_all // mols_step
    rows = mols_step * seq
    tok = lambda w: pl.BlockSpec((rows, w), lambda i, *_: (i, 0))
    tiled = lambda n: pl.BlockSpec((n, rows, LANES), lambda i, *_: (0, i, 0))
    across_tiles = width // LANES
    mol = lambda a, b: pl.BlockSpec((mols_step, a, b), lambda i, *_: (i, 0, 0))
    params = pltpu.CompilerParams(vmem_limit_bytes=VMEM_LIMIT, dimension_semantics=("arbitrary",))
    sq = (width, width)
    front = pl.pallas_call(
        functools.partial(plain_front_kernel, hd=hd, mols=mols_step, seq=seq, steps=steps),
        grid_spec=pltpu.PrefetchScalarGridSpec(
            num_scalar_prefetch=1,
            grid=(steps,),
            in_specs=[tok(width), mol(lap, seq), mol(2, seq), tok(width), whole((width, 3 * width)),
                      whole(sq), whole(sq), whole(sq), whole((width, SMALL))],
            out_specs=[tok(width), tiled(3 * across_tiles), mol(HEADS // 2, 2 * seq), tok(width), tok(width), tiled(across_tiles),
                       mol(48, seq), out_whole(sq), out_whole(sq), out_whole(sq), out_whole((16, width))],
            scratch_shapes=[
                pltpu.VMEM((SMALL, width), F32),
                pltpu.VMEM((hd.slots(), 16, LANES), BF),
                pltpu.VMEM((across_tiles, rows, LANES), BF),
                pltpu.VMEM((HEADS, seq, seq), BF),
                pltpu.VMEM(sq, F32), pltpu.VMEM(sq, F32), pltpu.VMEM(sq, F32),
                pltpu.VMEM((16, width), F32),
            ],
        ),
        out_shape=[
            jax.ShapeDtypeStruct((count, width), BF),
            jax.ShapeDtypeStruct((3 * across_tiles, count, LANES), BF),
            jax.ShapeDtypeStruct((mols_all, HEADS // 2, 2 * seq), F32),
            jax.ShapeDtypeStruct((count, width), F32),
            jax.ShapeDtypeStruct((count, width), F32),
            jax.ShapeDtypeStruct((across_tiles, count, LANES), BF),
            jax.ShapeDtypeStruct((mols_all, 48, seq), BF),
            jax.ShapeDtypeStruct(sq, BF),
            jax.ShapeDtypeStruct(sq, BF),
            jax.ShapeDtypeStruct(sq, BF),
            jax.ShapeDtypeStruct((16, width), F32),
        ],
        compiler_params=params,
        name="plain_front",
    )(counts_t, tokens, eig_t, ends_t, cot, w_in, w_out, w_up, w_down, small)
    out, proj, lse, emb, dmid, dmix, labt, g_out, g_up, g_down, g_vec = front
    tg, g_in, g_small = pl.pallas_call(
        functools.partial(plain_back_kernel, hd=hd, mols=mols_step, seq=seq, steps=steps),
        grid_spec=pltpu.PrefetchScalarGridSpec(
            num_scalar_prefetch=1,
            grid=(steps,),
            in_specs=[tiled(3 * across_tiles), mol(HEADS // 2, 2 * seq), tok(width), tok(width), tiled(across_tiles), mol(48, seq),
                      whole((width, 3 * width)), whole((width, SMALL)), whole((16, width))],
            out_specs=[tok(width), out_whole((width, 3 * width)), out_whole((width, SMALL))],
            scratch_shapes=[
                pltpu.VMEM((SMALL, width), F32),
                pltpu.VMEM((hd.slots(), 16, LANES), BF),
                pltpu.VMEM((HEADS, seq, seq), BF),
                pltpu.VMEM((HEADS, seq, seq), BF),
                pltpu.VMEM((HEADS, seq, seq), BF),
                pltpu.VMEM((3 * across_tiles, rows, LANES), BF),
                pltpu.VMEM((width, 3 * width), F32),
                pltpu.VMEM((16, width), F32),
                pltpu.VMEM((48, width), F32),
            ],
        ),
        out_shape=[
            jax.ShapeDtypeStruct((count, width), F32),
            jax.ShapeDtypeStruct((width, 3 * width), BF),
            jax.ShapeDtypeStruct((width, SMALL), BF),
        ],
        compiler_params=params,
        name="plain_back",
    )(counts_t, proj, lse, emb, dmid, dmix, labt, w_in, small, g_vec)
    return out, tg, g_in, g_out, g_up, g_down, g_small


def update_kernel(
    steps, rates, large_a, large_b, norm, g_in, g_out, g_up, g_down, g_small, *refs,
):
    states, outs, norm_o = refs[:18], refs[18:42], refs[42]
    moves = []
    for i, (source, target, stay) in enumerate(((large_b, refs[44], refs[46]), (large_a, refs[43], refs[45]))):
        size = source.shape[0] // MOVES
        for j in range(MOVES):
            part = pl.ds(j * size, size)
            moves.append((
                pltpu.make_async_copy(source.at[part], stay.at[part], refs[47].at[2 * (MOVES * i + j)]),
                pltpu.make_async_copy(stay.at[part], target.at[part], refs[47].at[2 * (MOVES * i + j) + 1]),
            ))
    for load, _ in moves:
        load.start()
    for load, store in moves:
        load.wait()
        store.start()
    norm_o[0, 0] = norm[0, 0]
    total = norm[0:1, 0:1]
    factor = jnp.minimum(1.0, CLIP_LIMIT / (total + NORM_EPS))
    t = jnp.full((1, 1), steps[0].astype(F32), F32)
    rate = rates[0]
    fix_one = 1.0 / (1.0 - jnp.exp(t * math.log(BETA_ONE)))
    fix_two = 1.0 / (1.0 - jnp.exp(t * math.log(BETA_TWO)))
    small = g_small[...]
    turned = jnp.concatenate([small, jnp.zeros((LANES - small.shape[0], SMALL), F32)], 0).T
    vec = turned[32:43, : small.shape[0]]
    vec = jnp.concatenate([vec[2:, :], vec[:2, :]], 0)
    grads = (g_in[...], g_out[...], g_up[...], g_down[...], small[:, :32], vec)
    for i, g in enumerate(grads):
        master, first, second = (states[3 * i + j][...] for j in range(3))
        g = g * factor
        first = BETA_ONE * first + (1.0 - BETA_ONE) * g
        second = BETA_TWO * second + (1.0 - BETA_TWO) * g * g
        change = first * fix_one / (jnp.sqrt(second * fix_two) + ADAM_EPS)
        if i < 5:
            change = change + DECAY_RATE * master
        for j, v in enumerate((g, first, second, master - rate * change)):
            outs[4 * i + j][...] = v
    for _, store in moves:
        store.wait()


def update_call(step_count, learn_rate, large, norm, grads, states):
    vm, sm, hbm = (pl.BlockSpec(memory_space=m) for m in (pltpu.VMEM, pltpu.SMEM, pl.ANY))
    shapes = [jax.ShapeDtypeStruct(states[3 * i].shape, F32) for i in range(6) for _ in range(4)]
    return pl.pallas_call(
        update_kernel,
        in_specs=[sm, sm, hbm, hbm] + [vm] * 24,
        out_specs=[vm] * 24 + [sm, hbm, hbm],
        out_shape=shapes + [jax.ShapeDtypeStruct((1, 1), F32)] + [jax.ShapeDtypeStruct(v.shape, v.dtype) for v in large],
        scratch_shapes=[pltpu.VMEM(v.shape, v.dtype) for v in large] + [pltpu.SemaphoreType.DMA((4 * MOVES,))],
        compiler_params=pltpu.CompilerParams(vmem_limit_bytes=VMEM_LIMIT),
        name="update",
    )(step_count.reshape(1), learn_rate.reshape(1), *large, norm, *grads, *states)


def body(
    count,
    tokens, eigvecs, counts, endpoints, cotangent,
    attend_in, attend_in_first, attend_in_second,
    attend_out, attend_out_first, attend_out_second,
    feed_up, feed_up_first, feed_up_second,
    feed_down, feed_down_first, feed_down_second,
    label_in, label_in_first, label_in_second,
    vectors, vectors_first, vectors_second,
    step_count, learn_rate,
):
    shard, width = feed_up.shape
    squares = (attend_in, attend_out.T, feed_up, feed_down.T)
    arrays = (tokens, jnp.swapaxes(eigvecs, 1, 2), counts.T, jnp.swapaxes(endpoints, 1, 2), cotangent)
    if Plan.fits(count, shard):
        out, tg, sums, norm = paired_layer(Plan(count), *arrays, squares + (label_in.T, vectors), MOLS_STEP)
    else:
        small_shard = jnp.concatenate(
            [label_in.T, vectors[9:].T, vectors[:9].T, jnp.zeros((shard, SMALL - 43), F32)], 1
        )
        shards = squares + (small_shard,)
        weights = [lax.all_gather(v.astype(BF), "dp", axis=0, tiled=True) for v in shards]
        out, tg, *grads = plain_layer(*arrays, *weights, 2)
        sums = [lax.psum_scatter(v.astype(F32), "dp", scatter_dimension=0, tiled=True) for v in grads]
        total = lax.psum(sum(jnp.sum(v * v) for v in sums), "dp")
        norm = jnp.full((8, LANES), jnp.sqrt(total), F32)
    states = (
        attend_in, attend_in_first, attend_in_second,
        attend_out.T, attend_out_first.T, attend_out_second.T,
        feed_up, feed_up_first, feed_up_second,
        feed_down.T, feed_down_first.T, feed_down_second.T,
        label_in.T, label_in_first.T, label_in_second.T,
        vectors, vectors_first, vectors_second,
    )
    *new, norm, out, tg = update_call(step_count, learn_rate, (out, tg), norm, sums, states)
    new = [v.T if i // 4 in (1, 3, 4) else v for i, v in enumerate(new)]
    return (out, tg, norm.reshape(()), *new)


MOLS_STEP = 4
SLOTS_GATHER = (1, 3, 4, 6)
SLOTS_SCATTER = (0, 2, 3, 4, 6)
WIDE = 512
EVERY = 2
MOVES = 8


def solution(mesh):
    rows, cols = P("dp", None), P(None, "dp")
    state = (rows,) * 3 + (cols,) * 3 + (rows,) * 3 + (cols,) * 9
    placed = (rows, P("dp", None, None), rows, P("dp", None, None), rows) + state + (P(), P())
    results = (rows,) * 4 + (cols,) * 4 + (rows,) * 4 + (cols,) * 12
    return jax.shard_map(
        functools.partial(body, mesh.shape["dp"]),
        mesh=mesh, in_specs=placed, out_specs=(rows, rows, P()) + results, check_vma=False,
    )
```

```python
import functools
import math

import jax
import jax.numpy as jnp
from jax import lax
from jax.experimental import pallas as pl
from jax.experimental.pallas import tpu as pltpu
from jax.sharding import PartitionSpec as P

HEADS = 32
EPS_NORM = 1e-05
MASK_FILL = -1e30
SQRT_HALF = 0.7071067811865476
INV_SQRT_TWO_PI = 0.3989422804014327
BETA_ONE = 0.9
BETA_TWO = 0.999
ADAM_EPS = 1e-08
DECAY_RATE = 0.01
CLIP_LIMIT = 1.0
NORM_EPS = 1e-06
LOG2E = 1.4426950408889634

BF = jnp.bfloat16
F32 = jnp.float32
MESH = pl.DeviceIdType.MESH
LANES = 128
VMEM_LIMIT = 60 << 20

SMALL = 128
NODE, EDGE = 32, 33
GAIN1, SHIFT1, QBIAS, VBIAS, OBIAS, GAIN2, SHIFT2, UBIAS, DBIAS = range(34, 43)


def nn(a, b):
    return lax.dot_general(a, b, (((1,), (0,)), ((), ())), preferred_element_type=F32)


def nt(a, b):
    return lax.dot_general(a, b, (((1,), (1,)), ((), ())), preferred_element_type=F32)


def tn(a, b):
    return lax.dot_general(a, b, (((0,), (0,)), ((), ())), preferred_element_type=F32)


def layer_stats(values):
    centred = values - jnp.mean(values, -1, keepdims=True)
    recip_std = lax.rsqrt(jnp.mean(centred * centred, -1, keepdims=True) + EPS_NORM)
    return centred * recip_std, recip_std


def norm_back(grad_out, normed, recip_std, gain_row):
    scaled = grad_out * gain_row
    return recip_std * (
        scaled
        - jnp.mean(scaled, -1, keepdims=True)
        - normed * jnp.mean(scaled * normed, -1, keepdims=True)
    )


class Heads:
    def __init__(self, width):
        self.dim = width // HEADS
        span = 1
        while (span * self.dim) % LANES:
            span *= 2
        self.block = span
        self.tiles = span * self.dim // LANES
        self.blocks = HEADS // span

    def first(self, head):
        return head * self.dim // LANES

    def last(self, head):
        return ((head + 1) * self.dim - 1) // LANES

    def heads_of(self, tile):
        return [h for h in range(self.block) if self.first(h) <= tile <= self.last(h)]

    def slot(self, tile, head):
        return sum(len(self.heads_of(t)) for t in range(tile)) + head - self.heads_of(tile)[0]

    def slots(self):
        return sum(len(self.heads_of(t)) for t in range(self.tiles))

    def mask(self, tile, head):
        lane = lax.broadcasted_iota(jnp.int32, (1, LANES), 1) + tile * LANES
        inside = jnp.logical_and(lane >= head * self.dim, lane < (head + 1) * self.dim)
        return inside.astype(F32).astype(BF)


def masked(value, mask):
    rows = value.shape[0]
    return (value.reshape(rows // 16, 16, LANES) * mask[None]).reshape(rows, LANES)


def dense(value):
    return value.astype(F32).astype(BF)


def set_masks(hd, masks):
    for t in range(hd.tiles):
        for h in hd.heads_of(t):
            masks[hd.slot(t, h)] = jnp.broadcast_to(hd.mask(t, h), (16, LANES))


def across(parts):
    return parts[0] if len(parts) == 1 else jnp.concatenate(parts, 1)


def pair_rows(hd, masks, tiles_of, pair):
    h0, h1 = 2 * pair, 2 * pair + 1
    lo, hi = hd.first(h0), hd.last(h1)
    rows = []
    for h in (h0, h1):
        parts = []
        for t in range(lo, hi + 1):
            if hd.first(h) <= t <= hd.last(h):
                parts.append(masked(tiles_of[t], masks[hd.slot(t, h)]))
            else:
                parts.append(jnp.zeros_like(tiles_of[t]))
        rows.append(across(parts))
    return jnp.concatenate(rows, 0)


def pair_full(hd, tiles_of, pair):
    return across([tiles_of[t] for t in range(hd.first(2 * pair), hd.last(2 * pair + 1) + 1)])


def tile_rows(hd, masks, tile_value, tile):
    return jnp.concatenate([masked(tile_value, masks[hd.slot(tile, h)]) for h in hd.heads_of(tile)], 0)


def units(width):
    unit = 2 * LANES
    return [(at, unit) for at in range(0, width, unit)]


class Plan:
    def __init__(self, count):
        self.count = count
        self.bits = count.bit_length() - 1
        self.chip_bits = self.bits - 1
        self.dims = (2,) * self.chip_bits
        near = list(range(1, min(4, self.bits)))
        self.far = list(range(self.bits - 1, near[-1], -1))
        self.turns = [near[i:] + near[:i] for i in range(len(near))]

    def order(self, part):
        return self.far + self.turns[part % len(self.turns)]

    @staticmethod
    def fits(count, rows):
        return count >= 16 and count & (count - 1) == 0 and rows % 8 == 0


def my_place(plan):
    me = lax.axis_index("dp")
    bit = [lax.rem(lax.div(me, jnp.int32(1 << b)), jnp.int32(2)) for b in range(plan.bits)]
    other = [me + (1 - 2 * bit[b]) * (1 << b) for b in range(plan.bits)]
    return me, bit, other


def greet(plan, other):
    barrier = pltpu.get_barrier_semaphore()
    for b in range(plan.bits):
        pl.semaphore_signal(barrier, inc=1, device_id=(other[b],), device_id_type=MESH)
    pl.semaphore_wait(barrier, plan.bits)


class Gather:
    def __init__(self, plan, bit, other, send, recv):
        self.plan, self.bit, self.other, self.send, self.recv = plan, bit, other, send, recv

    def cols(self, part, mine):
        buf, src, stage, at, width = part["buf"], part["src"], part["stage"], part["at"], part["width"]
        if not part["split"]:
            return pl.ds(at, width)
        half = width // 2
        which = self.bit[0] if mine else 1 - self.bit[0]
        return pl.ds(pl.multiple_of(at + which * half, LANES), half)

    def copy(self, part, phase):
        plan, i = self.plan, part["i"]
        if phase == 0:
            cols = self.cols(part, False)
            src, dst, to = part["src"].at[:, cols], part["stage"], self.other[0]
        elif phase <= plan.chip_bits:
            order = plan.order(part["turn"])
            done, b = order[: phase - 1], order[phase - 1]
            idx = tuple(
                slice(None) if bb in done else self.bit[bb] for bb in range(plan.bits - 1, 0, -1)
            )
            ref = part["buf"].at[idx + (slice(None), self.cols(part, True))]
            src, dst, to = ref, ref, self.other[b]
        else:
            ref = part["buf"].at[(slice(None),) * (plan.chip_bits + 1) + (self.cols(part, True),)]
            src, dst, to = ref, ref, self.other[0]
        return pltpu.make_async_remote_copy(
            src_ref=src, dst_ref=dst, send_sem=self.send.at[i, phase], recv_sem=self.recv.at[i, phase],
            device_id=(to,), device_id_type=MESH,
        )

    def phases(self, part):
        return self.plan.chip_bits + (2 if part["split"] else 1)

    def start(self, part, phase):
        self.copy(part, phase).start()

    def wait(self, part, phase):
        self.copy(part, phase).wait()
        if phase == 0:
            cols = self.cols(part, True)
            own, got = part["src"][:, cols], part["stage"][...]
            lower = self.bit[0] == 0
            rows = jnp.concatenate([jnp.where(lower, own, got), jnp.where(lower, got, own)], 0)
            idx = tuple(self.bit[bb] for bb in range(self.plan.bits - 1, 0, -1))
            part["buf"][idx + (slice(None), cols)] = rows.astype(BF)

    def advance(self, part, phase):
        self.wait(part, phase)
        if phase + 1 < self.phases(part):
            self.start(part, phase + 1)


class Scatter:
    def __init__(self, plan, bit, other, send, recv):
        self.plan, self.bit, self.other, self.send, self.recv = plan, bit, other, send, recv

    def cols(self, part, mine):
        half = part["width"] // 2
        which = self.bit[0] if mine else 1 - self.bit[0]
        return pl.ds(pl.multiple_of(part["at"] + which * half, LANES), half)

    def order(self, part):
        return self.plan.order(part["turn"])[::-1]

    def index(self, part, phase, mine):
        done, b = self.order(part)[: phase - 1], self.order(part)[phase - 1]
        idx = []
        for bb in range(self.plan.bits - 1, 0, -1):
            if bb in done:
                continue
            idx.append((self.bit[b] if mine else 1 - self.bit[b]) if bb == b else slice(None))
        return tuple(idx)

    def rows(self, which):
        r = self.plan_rows
        return pl.ds(pl.multiple_of(which * r, 8), r)

    def copy(self, part, phase):
        plan, i = self.plan, part["i"]
        every = (slice(None),) * (plan.chip_bits + 1)
        if phase == 0:
            if part["split"]:
                src = part["src"].at[every + (self.cols(part, False),)]
            else:
                src = part["src"]
            dst, to = part["slots"][0], self.other[0]
        elif phase <= plan.chip_bits:
            src = part["slots"][phase - 1].at[self.index(part, phase, False)]
            dst, to = part["slots"][phase], self.other[self.order(part)[phase - 1]]
        else:
            r = part["sum"].shape[0] // 2
            src = part["sum"].at[pl.ds(pl.multiple_of((1 - self.bit[0]) * r, 8), r)]
            dst, to = part["last"], self.other[0]
        return pltpu.make_async_remote_copy(
            src_ref=src, dst_ref=dst, send_sem=self.send.at[i, phase], recv_sem=self.recv.at[i, phase],
            device_id=(to,), device_id_type=MESH,
        )

    def phases(self, part):
        return self.plan.chip_bits + (2 if part["split"] else 1)

    def start(self, part, phase):
        self.copy(part, phase).start()

    def wait(self, part, phase):
        plan = self.plan
        self.copy(part, phase).wait()
        every = (slice(None),) * (plan.chip_bits + 1)
        if phase > plan.chip_bits:
            return
        slot = part["slots"][phase]
        if phase == 0:
            if part["split"]:
                mine = part["src"][every + (self.cols(part, True),)]
            else:
                mine = part["src"][...]
        else:
            mine = part["slots"][phase - 1][self.index(part, phase, True)]
        if phase == plan.chip_bits:
            part["sum"][...] = mine.astype(F32) + slot[...].astype(F32)
        else:
            slot[...] = mine + slot[...]

    def advance(self, part, phase):
        self.wait(part, phase)
        if phase + 1 < self.phases(part):
            self.start(part, phase + 1)

    def finish(self, part, out):
        r = part["sum"].shape[0] // 2
        own = part["sum"][pl.ds(pl.multiple_of(self.bit[0] * r, 8), r), :]
        if not part["split"]:
            out[...] = own
            return
        half = part["width"] // 2
        out[:, self.cols(part, True)] = own
        out[:, self.cols(part, False)] = part["last"][...]


def norm_exchange(plan, me, squares, mine, boxes, send, recv):
    mine[...] = jnp.full((8, LANES), squares, F32)
    copies = []
    for d in range(1, plan.count):
        copies.append(pltpu.make_async_remote_copy(
            src_ref=mine, dst_ref=boxes.at[d - 1], send_sem=send.at[d - 1], recv_sem=recv.at[d - 1],
            device_id=(lax.rem(me + d, jnp.int32(plan.count)),), device_id_type=MESH,
        ))
    for c in copies:
        c.start()
    for c in copies:
        c.wait()
    return mine[...] + jnp.sum(boxes[...], 0)


def ring_partners(plan, me):
    return [lax.rem(me + d, jnp.int32(plan.count)) for d in range(1, plan.count)]


def mat(ref, *cols):
    value = ref[(slice(None),) * (len(ref.shape) - 1) + cols] if cols else ref[...]
    return value.reshape(-1, value.shape[-1])


def front_kernel(*refs, plan, hd, mols, wide, seq, steps, steps2):
    refs = list(refs)
    take = lambda k: [refs.pop(0) for _ in range(k)]
    counts, tokens, eig, ends, cot = take(5)
    s_in, s_out, s_up, s_down, label_t, vec = take(6)
    out_o, proj_o, lse_o, dmid_o, dmix_o, labt_o, gout_o, gup_o, gdown_o, gvec_o, smallt_o, emb_o, inp_o, win_o = take(14)
    w_in, w_out, w_up, w_down, small = take(5)
    stages = take(1 + 6 * len(units(hd.dim * HEADS)))
    small_t, masks, tok_s, emb_s, inp_s, mixed_s, p_buf, acc_out, acc_up, acc_down, acc_vec = take(11)
    send, recv, keep = take(3)
    s_small, vec_s = take(2)
    step = pl.program_id(0)
    width = w_out.shape[-1]
    across_tiles = width // LANES
    score = hd.dim ** -0.5
    rows_all = mols * seq
    me, bit, other = my_place(plan)
    gather = Gather(plan, bit, other, send, recv)
    make = lambda i, src, buf, at, wide, split, t: dict(
        i=i, src=src, buf=buf, stage=stages[i], at=at, width=wide, split=split, turn=t
    )
    early = [make(0, s_small, small, 0, SMALL, False, 0)]
    late = []
    for src, buf, group in ((s_in, w_in, early), (s_out, w_out, late), (s_up, w_up, late), (s_down, w_down, late)):
        for at, unit in units(buf.shape[-1]):
            n = len(early) + len(late)
            group.append(make(n, src, buf, at, unit, True, n))
    final = plan.chip_bits + 1
    kept = [pltpu.make_async_copy(a, b, keep.at[i]) for i, (a, b) in enumerate(((w_in, win_o), (emb_s, emb_o), (inp_s, inp_o)))]
    get_tokens = pltpu.make_async_copy(tokens, tok_s, keep.at[3])

    row = lambda i: small_t[i : i + 1, :]

    def embed(group, carry):
        iota0 = lax.broadcasted_iota(jnp.int32, (seq, seq), 0)
        iota1 = lax.broadcasted_iota(jnp.int32, (seq, seq), 1)
        token_row = lax.broadcasted_iota(jnp.int32, (1, seq), 1)
        kind_row = lax.broadcasted_iota(jnp.int32, (16, seq), 0)
        one = lambda c: c.astype(F32).astype(BF)
        label_rows = []
        for g in range(mols):
            m = group * mols + g
            nodes = counts[0, m]
            live = nodes + counts[1, m]
            eig_f = eig[m]
            shift = one(jnp.logical_and(iota1 - iota0 == nodes, iota1 < live))
            picks = jnp.concatenate([one(iota0 == ends[m, end : end + 1, :]) for end in range(2)], 1)
            edge_lab = nn(eig_f.astype(BF), picks).astype(BF)
            moved = nn(jnp.concatenate([edge_lab[:, :seq], edge_lab[:, seq:]], 0), shift)
            at_node = token_row < nodes
            is_node = at_node.astype(F32)
            is_edge = jnp.logical_and(token_row >= nodes, token_row < live).astype(F32)
            kind = jnp.where(kind_row == 0, is_node, jnp.where(kind_row == 1, is_edge, 0.0))
            lab = jnp.concatenate(
                [jnp.where(at_node, eig_f, moved[:16]), jnp.where(at_node, eig_f, moved[16:]), kind], 0
            )
            labt_o[m] = lab.astype(BF)
            pad = jnp.zeros((SMALL - lab.shape[0], seq), F32)
            label_rows.append(jnp.concatenate([lab, pad], 0).T.astype(BF))
        labels = jnp.concatenate(label_rows, 0)
        here = pl.ds(pl.multiple_of(group * rows_all, rows_all), rows_all)
        embedded = tok_s[here, :].astype(F32) + nn(labels, small_t[...].astype(BF))
        emb_s[here, :] = embedded
        normed, _ = layer_stats(embedded)
        value = (normed * row(GAIN1) + row(SHIFT1)).astype(BF)
        for t in range(across_tiles):
            inp_s[t, here, :] = value[:, t * LANES : (t + 1) * LANES]
        return carry

    @pl.when(step == 0)
    def _():
        get_tokens.start()
        vec_s[...] = jnp.zeros_like(vec_s)
        vec_s[32:34, : vec.shape[1]] = vec[9:11, :]
        vec_s[34:43, : vec.shape[1]] = vec[0:9, :]
        s_small[...] = vec_s[...].T[: s_small.shape[0], :]
        s_small[:, :32] = label_t[...]
        greet(plan, other)
        for part in early + late:
            gather.start(part, 0)
        set_masks(hd, masks)
        acc_out[...] = jnp.zeros_like(acc_out)
        acc_up[...] = jnp.zeros_like(acc_up)
        acc_down[...] = jnp.zeros_like(acc_down)
        acc_vec[...] = jnp.zeros_like(acc_vec)
        for phase in range(final):
            for part in early:
                if part["split"] and phase == final - 1:
                    continue
                gather.advance(part, phase)
        small_t[...] = mat(small).astype(F32).T
        smallt_o[...] = small_t[...]
        get_tokens.wait()
        cut = (steps + 1) // 2
        lax.fori_loop(0, cut, embed, 0)
        for part in early[1:]:
            gather.advance(part, final - 1)
        lax.fori_loop(cut, steps, embed, 0)
        for part in early[1:]:
            gather.advance(part, final)
        for part in late:
            gather.advance(part, 0)
        for copy in kept:
            copy.start()

    def attend(some, between=()):
        between = list(between)
        for m in some:
            nodes = counts[0, step * mols + m]
            live = nodes + counts[1, step * mols + m]
            key_live = lax.broadcasted_iota(jnp.int32, (seq, 2 * seq), 0) < live
            rows = slice(m * seq, (m + 1) * seq)
            for b in range(hd.blocks):
                get = lambda part: [proj_o[part * across_tiles + b * hd.tiles + t, rows, :] for t in range(hd.tiles)]
                q, k, v = [dense(x) for x in get(0)], get(1), [dense(x) for x in get(2)]
                for pair in range(hd.block // 2):
                    scores = nt(pair_full(hd, k, pair), pair_rows(hd, masks, q, pair))
                    scores = jnp.where(key_live, scores, MASK_FILL)
                    top = jnp.max(scores, 0, keepdims=True)
                    ex = jnp.exp2((scores - top) * (score * LOG2E))
                    total = jnp.sum(ex, 0, keepdims=True)
                    shares = (ex * (1.0 / total)).astype(BF)
                    at = b * (hd.block // 2) + pair
                    lse_o[m, at : at + 1, :] = top + jnp.log2(total) * (1.0 / (score * LOG2E))
                    for i in range(2):
                        p_buf[b * hd.block + 2 * pair + i] = shares[:, i * seq : (i + 1) * seq].T
                    if between and pair % EVERY == 0:
                        between.pop(0)()
                for t in range(hd.tiles):
                    hs = hd.heads_of(t)
                    mixed = nn(across([p_buf[b * hd.block + h] for h in hs]), tile_rows(hd, masks, v[t], t))
                    put = pl.ds(pl.multiple_of(step * rows_all + m * seq, seq), seq)
                    mixed_s[b * hd.tiles + t, put, :] = mixed.astype(BF)
        for run in between:
            run()

    @pl.when(step < steps)
    def _():
        here = pl.ds(pl.multiple_of(step * rows_all, rows_all), rows_all)
        half = rows_all // 2

        def project(n, part, cols):
            at = pl.ds(pl.multiple_of(step * rows_all + n * half, half), half)
            value = nn(
                across([inp_s[t, at, :] for t in range(across_tiles)]),
                mat(w_in, slice(part * width + cols.start, part * width + cols.stop)),
            )
            if part == 0:
                value = value + small_t[QBIAS : QBIAS + 1, cols]
            if part == 2:
                value = value + small_t[VBIAS : VBIAS + 1, cols]
            value = value.astype(BF)
            for t in range((cols.stop - cols.start) // LANES):
                tile = part * across_tiles + cols.start // LANES + t
                proj_o[tile, n * half : (n + 1) * half, :] = value[:, t * LANES : (t + 1) * LANES]

        for part in range(3):
            project(0, part, slice(0, width))
        later = [
            functools.partial(project, 1, part, slice(at, at + unit)) for part in range(3) for at, unit in units(width)
        ]
        attend(range(mols // 2), later)

    def pump(half):
        for phase in range(1, final + 1):
            slot = min(SLOTS_GATHER[min(phase, 4) - 1] + max(phase - 4, 0), 2 * steps - 1)
            if slot % 2 == half:
                @pl.when(step == slot // 2)
                def _():
                    for part in late:
                        gather.advance(part, phase)

    pump(0)

    @pl.when(step < steps)
    def _():
        attend(range(mols // 2, mols))

    pump(1)

    @pl.when(step >= steps)
    def _():
        parts = 1
        size = wide // parts
        add = lambda v: jnp.sum(v, 0, keepdims=True)
        stack = lambda vs: vs[0] if parts == 1 else jnp.concatenate(vs, 0)
        runs = [slice(r * size, (r + 1) * size) for r in range(parts)]
        here = [pl.ds(pl.multiple_of((step - steps) * wide + r * size, size), size) for r in range(parts)]
        mixed = [across([mixed_s[t, h, :] for t in range(across_tiles)]) for h in here]
        branch_in = [nt(x, mat(w_out)) for x in mixed]
        middle, norms, inputs = [], [], []
        for h, x in zip(here, branch_in):
            middle.append(emb_s[h, :] + (x + row(OBIAS)))
            norms.append(layer_stats(middle[-1]))
            inputs.append((norms[-1][0] * row(GAIN2) + row(SHIFT2)).astype(BF))
        acts, d_pres, backs = [], [], [cot[r, :] for r in runs]
        for x, back in zip(inputs, backs):
            pre = nn(x, mat(w_up)) + row(UBIAS)
            half_erf = 0.5 * (1.0 + lax.erf(pre * SQRT_HALF))
            acts.append((pre * half_erf).astype(BF))
            slope = half_erf + pre * jnp.exp(-0.5 * pre * pre) * INV_SQRT_TWO_PI
            d_pres.append((nn(back, mat(w_down)) * slope).astype(BF))
        d_ins = [nt(x, mat(w_up)) for x in d_pres]
        branches = []
        totals = {i: [] for i in (OBIAS, GAIN2, SHIFT2, UBIAS, DBIAS)}
        def close(n):
            r, back_f, d_in2, (normed2, recip2) = runs[n], backs[n].astype(F32), d_ins[n], norms[n]
            d_mid = back_f + norm_back(d_in2, normed2, recip2, row(GAIN2))
            dmid_o[r, :] = d_mid
            branches.append(d_mid.astype(BF))
            totals[OBIAS].append(add(branches[-1].astype(F32)))
            totals[GAIN2].append(add(d_in2 * normed2))
            totals[SHIFT2].append(add(d_in2))
            totals[UBIAS].append(add(d_pres[n].astype(F32)))
            totals[DBIAS].append(add(back_f))
        def output():
            for r, mid, act in zip(runs, middle, acts):
                out_o[r, :] = (mid + (nt(act, mat(w_down)) + row(DBIAS))).astype(BF)
        def down():
            acc_down[...] += tn(stack(backs), stack(acts))
        def up():
            acc_up[...] += tn(stack(inputs), stack(d_pres))
        output()
        close(0)
        down()
        up()
        for r, x in zip(runs, branches):
            d_mixed = nn(x, mat(w_out)).astype(BF)
            for t in range(across_tiles):
                dmix_o[t, r, :] = d_mixed[:, t * LANES : (t + 1) * LANES]
        acc_out[...] += tn(stack(branches), stack(mixed))
        for i, vs in totals.items():
            acc_vec[i - 34 : i - 33, :] += sum(vs)

    @pl.when(step == steps + steps2 - 1)
    def _():
        for acc, out in ((acc_out, gout_o), (acc_up, gup_o), (acc_down, gdown_o)):
            out[...] = acc[...].astype(BF)
        gvec_o[...] = acc_vec[...]
        for copy in kept:
            copy.wait()


class ShareSmall:
    def __init__(self, plan, me, src, boxes, part, boxes2, send, recv):
        self.src, self.boxes, self.part, self.boxes2 = src, boxes, part, boxes2
        low = src.shape[1]
        high = plan.count // low
        self.place, self.level = lax.rem(me, jnp.int32(low)), lax.div(me, jnp.int32(low))
        self.one, self.two = [], []
        for d in range(1, low):
            to = lax.rem(self.place + d, jnp.int32(low))
            self.one.append(pltpu.make_async_remote_copy(
                src_ref=src.at[:, to], dst_ref=boxes.at[d - 1], send_sem=send.at[d - 1], recv_sem=recv.at[d - 1],
                device_id=(me + to - self.place,), device_id_type=MESH,
            ))
        for d in range(1, high):
            to = lax.rem(self.level + d, jnp.int32(high))
            at = low - 2 + d
            self.two.append(pltpu.make_async_remote_copy(
                src_ref=part.at[to], dst_ref=boxes2.at[d - 1], send_sem=send.at[at], recv_sem=recv.at[at],
                device_id=(me + (to - self.level) * low,), device_id_type=MESH,
            ))

    def begin(self):
        for c in self.one:
            c.start()

    def middle(self):
        total = self.src[:, self.place]
        for d, c in enumerate(self.one):
            c.wait()
            total = total + self.boxes[d]
        self.part[...] = total
        for c in self.two:
            c.start()

    def end(self):
        total = self.part[self.level]
        for d, c in enumerate(self.two):
            c.wait()
            total = total + self.boxes2[d]
        return total


def back_kernel(*refs, plan, hd, mols, wide, seq, steps, steps2):
    refs = list(refs)
    take = lambda k: [refs.pop(0) for _ in range(k)]
    counts, proj, lse, inp, emb, dmid, dmix, labt, w_in, small_t, gvec, g_out, g_up, g_down = take(14)
    tg_o, o_in, o_out, o_up, o_down, o_small, o_norm = take(7)
    masks, pt_buf, dst_buf, ds_buf, dproj_s, acc_in, g_in, acc_vec, acc_lab = take(9)
    k = plan.chip_bits + 1
    count = 6 * len(units(hd.dim * HEADS))
    slots = [take(k) for _ in range(count)]
    part_sums, lasts = take(count), take(count)
    send, recv = take(2)
    small_s, small_box, small_part, small_box2, ssend, srecv = take(6)
    mine, boxes, nsend, nrecv = take(4)
    step = pl.program_id(0)
    width = g_out.shape[-1]
    across_tiles = width // LANES
    score = hd.dim ** -0.5
    rows_all = mols * seq
    me, bit, other = my_place(plan)
    scatter = Scatter(plan, bit, other, send, recv)
    parts, late, early = [], [], []
    for src, out, group in ((g_in, o_in, late), (g_out, o_out, early), (g_up, o_up, early), (g_down, o_down, early)):
        for at, unit in units(src.shape[-1]):
            i = len(parts)
            part = dict(i=i, src=src, slots=slots[i], at=at, width=unit, split=True, turn=i, sum=part_sums[i],
                        last=lasts[i], out=out)
            parts.append(part)
            group.append(part)
    final = plan.chip_bits + 1

    @pl.when(step == 0)
    def _():
        barrier = pltpu.get_barrier_semaphore()
        partners = ring_partners(plan, me)
        for p in partners:
            pl.semaphore_signal(barrier, inc=1, device_id=(p,), device_id_type=MESH)
        pl.semaphore_wait(barrier, len(partners))
        for part in early:
            scatter.start(part, 0)
        set_masks(hd, masks)
        acc_in[...] = jnp.zeros_like(acc_in)
        acc_vec[...] = gvec[...]
        acc_lab[...] = jnp.zeros_like(acc_lab)

    row = lambda i: small_t[i : i + 1, :]

    def attend(some):
        for m in some:
            nodes = counts[0, step * mols + m]
            live = nodes + counts[1, step * mols + m]
            key_live = lax.broadcasted_iota(jnp.int32, (seq, 2 * seq), 0) < live
            rows = slice(m * seq, (m + 1) * seq)
            put = pl.ds(pl.multiple_of(step * rows_all + m * seq, seq), seq)
            for b in range(hd.blocks):
                get = lambda ref, part: [ref[part * across_tiles + b * hd.tiles + t, rows, :] for t in range(hd.tiles)]
                q, k, v, do = [dense(x) for x in get(proj, 0)], get(proj, 1), get(proj, 2), [dense(x) for x in get(dmix, 0)]
                k_dense = [dense(x) for x in k]
                for pair in range(hd.block // 2):
                    scores = nt(pair_full(hd, k, pair), pair_rows(hd, masks, q, pair))
                    scores = jnp.where(key_live, scores, MASK_FILL)
                    at = b * (hd.block // 2) + pair
                    p = jnp.exp2((scores - lse[m, at : at + 1, :]) * (score * LOG2E))
                    dp = nt(pair_full(hd, v, pair), pair_rows(hd, masks, do, pair))
                    inner = jnp.sum(p * dp, 0, keepdims=True)
                    ds = (p * (dp - inner)).astype(BF)
                    p = p.astype(BF)
                    for i in range(2):
                        h = b * hd.block + 2 * pair + i
                        pt_buf[h] = p[:, i * seq : (i + 1) * seq]
                        dst_buf[h] = ds[:, i * seq : (i + 1) * seq]
                        ds_buf[h] = ds[:, i * seq : (i + 1) * seq].T
                for t in range(hd.tiles):
                    hs = [b * hd.block + h for h in hd.heads_of(t)]
                    at = b * hd.tiles + t
                    d_v = nn(across([pt_buf[h] for h in hs]), tile_rows(hd, masks, do[t], t))
                    d_k = nn(across([dst_buf[h] for h in hs]), tile_rows(hd, masks, q[t], t)) * score
                    d_q = nn(across([ds_buf[h] for h in hs]), tile_rows(hd, masks, k_dense[t], t)) * score
                    dproj_s[at, put, :] = d_q.astype(BF)
                    dproj_s[across_tiles + at, put, :] = d_k.astype(BF)
                    dproj_s[2 * across_tiles + at, put, :] = d_v.astype(BF)

    @pl.when(step < steps)
    def _():
        attend(range(mols // 2))

    def pump(half):
        for phase in range(final + 1):
            slot = min(SLOTS_SCATTER[min(phase, 4)] + max(phase - 4, 0), 2 * steps - 1)
            if slot % 2 == half:
                @pl.when(step == slot // 2)
                def _():
                    for part in early:
                        scatter.advance(part, phase)

    pump(0)

    @pl.when(step < steps)
    def _():
        attend(range(mols // 2, mols))
        here = pl.ds(pl.multiple_of(step * rows_all, rows_all), rows_all)
        input_one = across([inp[t] for t in range(across_tiles)])
        d_proj = across([dproj_s[t, here, :] for t in range(3 * across_tiles)])
        acc_in[...] += tn(input_one, d_proj)
        add = lambda v: jnp.sum(v, 0, keepdims=True)
        acc_vec[QBIAS - 34 : QBIAS - 33, :] += add(d_proj[:, :width].astype(F32))
        acc_vec[VBIAS - 34 : VBIAS - 33, :] += add(d_proj[:, 2 * width :].astype(F32))

    pump(1)

    @pl.when(step == steps - 1)
    def _():
        for part in late:
            cols = slice(part["at"], part["at"] + part["width"])
            g_in[(slice(None),) * (plan.chip_bits + 1) + (cols,)] = acc_in[:, cols].astype(BF).reshape(
                g_in.shape[:-1] + (part["width"],)
            )
            scatter.start(part, 0)

    @pl.when(step >= steps)
    def _():
        here = pl.ds(pl.multiple_of((step - steps) * wide, wide), wide)
        normed, recip = layer_stats(emb[...])
        d_proj = across([dproj_s[t, here, :] for t in range(3 * across_tiles)])
        d_in1 = nt(d_proj, mat(w_in))
        tg = dmid[...] + norm_back(d_in1, normed, recip, row(GAIN1))
        tg_o[...] = tg
        tg_hi = tg.astype(BF)
        tg_lo = (tg - tg_hi.astype(F32)).astype(BF)
        lab = jnp.concatenate([labt[m] for m in range(wide // seq)], 1)
        acc_lab[...] += nn(lab, tg_hi)
        acc_lab[32:48, :] += nn(lab[32:48, :], tg_lo)
        add = lambda v: jnp.sum(v, 0, keepdims=True)
        acc_vec[GAIN1 - 34 : GAIN1 - 33, :] += add(d_in1 * normed)
        acc_vec[SHIFT1 - 34 : SHIFT1 - 33, :] += add(d_in1)

    for phase in range(min(final, steps2 - 1)):
        @pl.when(step == steps + phase)
        def _():
            for part in late:
                scatter.advance(part, phase)

    @pl.when(step == steps + steps2 - 1)
    def _():
        full = jnp.concatenate(
            [acc_lab[0:32, :], acc_lab[32:34, :], acc_vec[0:9, :], jnp.zeros((SMALL - 43, width), F32)], 0
        )
        small_s[...] = full.T.reshape(small_s.shape)
        share = ShareSmall(plan, me, small_s, small_box, small_part, small_box2, ssend, srecv)
        share.begin()
        for phase in range(min(final, steps2 - 1), final + 1):
            for part in late:
                scatter.advance(part, phase)
            if phase == min(final, steps2 - 1):
                share.middle()
        o_small[...] = share.end()
        for part in parts:
            scatter.finish(part, part["out"])
        total = sum(jnp.sum(o[...] * o[...]) for o in (o_small, o_in, o_out, o_up, o_down))
        o_norm[...] = jnp.sqrt(norm_exchange(plan, me, total, mine, boxes, nsend, nrecv))


def paired_layer(plan, tokens, eig_t, counts_t, ends_t, cot, shards, mols_step):
    count, width = tokens.shape
    mols_all, lap, seq = eig_t.shape
    shard = shards[0].shape[0]
    parts = len(units(width))
    hd = Heads(width)
    steps = mols_all // mols_step
    rows = mols_step * seq
    wide = min(WIDE, count)
    steps2 = count // wide
    across_tiles = width // LANES
    last = steps - 1
    first = lambda i: lax.min(i, last)
    second = lambda i: lax.max(i - steps, 0)
    tok2 = lambda w: pl.BlockSpec((wide, w), lambda i: (second(i), 0))
    mol = lambda a, b: pl.BlockSpec((mols_step, a, b), lambda i: (first(i), 0, 0))
    tiled = lambda n: pl.BlockSpec((n, rows, LANES), lambda i: (0, first(i), 0))
    tiled2 = lambda n: pl.BlockSpec((n, wide, LANES), lambda i: (0, second(i), 0))
    sizes = dict(plan=plan, hd=hd, mols=mols_step, wide=wide, seq=seq, steps=steps, steps2=steps2)
    vm, sm, hbm = (pl.BlockSpec(memory_space=m) for m in (pltpu.VMEM, pltpu.SMEM, pl.ANY))
    sq = (width, width)
    buf = lambda c: plan.dims + (2 * shard, c)
    f32 = lambda *shape: jax.ShapeDtypeStruct(shape, F32)
    bf = lambda *shape: jax.ShapeDtypeStruct(shape, BF)
    params = lambda cid: pltpu.CompilerParams(
        vmem_limit_bytes=VMEM_LIMIT, dimension_semantics=("arbitrary",), collective_id=cid,
        has_side_effects=True,
    )
    out, proj, lse, dmid, dmix, labt, g_out, g_up, g_down, g_vec, small_t, emb, inp, w_in = pl.pallas_call(
        functools.partial(front_kernel, **sizes),
        grid=(steps + steps2,),
        in_specs=[sm, hbm, vm, vm, tok2(width)] + [vm] * 6,
        out_specs=[tok2(width), tiled(3 * across_tiles), mol(HEADS // 2, 2 * seq), tok2(width), tiled2(across_tiles)]
        + [vm] * 6 + [hbm] * 3,
        out_shape=[bf(count, width), bf(3 * across_tiles, count, LANES), f32(mols_all, HEADS // 2, 2 * seq),
                   f32(count, width), bf(across_tiles, count, LANES), bf(mols_all, 48, seq),
                   bf(*sq), bf(*sq), bf(*sq), f32(16, width), f32(SMALL, width),
                   f32(count, width), bf(across_tiles, count, LANES), bf(*buf(3 * width))],
        scratch_shapes=[pltpu.VMEM(buf(c), BF) for c in (3 * width, width, width, width, SMALL)]
        + [pltpu.VMEM((shard, SMALL), F32)] + [pltpu.VMEM((shard, LANES), F32)] * (6 * parts)
        + [
            pltpu.VMEM((SMALL, width), F32),
            pltpu.VMEM((hd.slots(), 16, LANES), BF),
            pltpu.VMEM((count, width), BF),
            pltpu.VMEM((count, width), F32),
            pltpu.VMEM((across_tiles, count, LANES), BF),
            pltpu.VMEM((across_tiles, count, LANES), BF),
            pltpu.VMEM((HEADS, seq, seq), BF),
            pltpu.VMEM(sq, F32), pltpu.VMEM(sq, F32), pltpu.VMEM(sq, F32),
            pltpu.VMEM((16, width), F32),
        ]
        + [pltpu.SemaphoreType.DMA((6 * parts + 1, plan.chip_bits + 2))] * 2 + [pltpu.SemaphoreType.DMA((4,))]
        + [pltpu.VMEM((shard, SMALL), F32), pltpu.VMEM((SMALL, LANES), F32)],
        compiler_params=params(0),
        name="front",
    )(counts_t, tokens, eig_t, ends_t, cot, *shards)

    low = 1 << min(3, plan.bits)
    high = plan.count // low
    boxes = low - 1 + high - 1
    slots = [pltpu.VMEM(plan.dims[j:] + (2 * shard, LANES), BF) for j in range(plan.chip_bits + 1)]
    shaped = [g.reshape(buf(width)) for g in (g_out, g_up, g_down)]
    tg, *sums, norm = pl.pallas_call(
        functools.partial(back_kernel, **sizes),
        grid=(steps + steps2,),
        in_specs=[sm, tiled(3 * across_tiles), mol(HEADS // 2, 2 * seq), tiled(across_tiles), tok2(width), tok2(width),
                  tiled(across_tiles), pl.BlockSpec((wide // seq, 48, seq), lambda i: (second(i), 0, 0))] + [vm] * 6,
        out_specs=[tok2(width)] + [vm] * 6,
        out_shape=[f32(count, width), f32(shard, 3 * width), f32(shard, width), f32(shard, width), f32(shard, width),
                   f32(shard, SMALL), f32(8, LANES)],
        scratch_shapes=[
            pltpu.VMEM((hd.slots(), 16, LANES), BF),
            pltpu.VMEM((HEADS, seq, seq), BF),
            pltpu.VMEM((HEADS, seq, seq), BF),
            pltpu.VMEM((HEADS, seq, seq), BF),
            pltpu.VMEM((3 * across_tiles, count, LANES), BF),
            pltpu.VMEM((width, 3 * width), F32),
            pltpu.VMEM(buf(3 * width), BF),
            pltpu.VMEM((16, width), F32),
            pltpu.VMEM((48, width), F32),
        ]
        + slots * (6 * parts)
        + [pltpu.VMEM((2 * shard, LANES), F32)] * (6 * parts) + [pltpu.VMEM((shard, LANES), F32)] * (6 * parts)
        + [pltpu.SemaphoreType.DMA((6 * parts, plan.chip_bits + 2))] * 2
        + [
            pltpu.VMEM((high, low, shard, SMALL), F32),
            pltpu.VMEM((low - 1, high, shard, SMALL), F32),
            pltpu.VMEM((high, shard, SMALL), F32),
            pltpu.VMEM((max(high - 1, 1), shard, SMALL), F32),
        ]
        + [pltpu.SemaphoreType.DMA((boxes,))] * 2
        + [pltpu.VMEM((8, LANES), F32), pltpu.VMEM((plan.count - 1, 8, LANES), F32)]
        + [pltpu.SemaphoreType.DMA((plan.count - 1,))] * 2,
        compiler_params=params(1),
        name="back",
    )(counts_t, proj, lse, inp, emb, dmid, dmix, labt, w_in, small_t, g_vec, *shaped)
    return out, tg, sums, norm


def plain_front_kernel(
    counts, tokens, eig, ends, cot, w_in, w_out, w_up, w_down, small,
    out_o, proj_o, lse_o, emb_o, dmid_o, dmix_o, labt_o, gout_o, gup_o, gdown_o, gvec_o,
    small_t, masks, mixed_s, p_buf, acc_out, acc_up, acc_down, acc_vec,
    *, hd, mols, seq, steps,
):
    step = pl.program_id(0)
    width = w_in.shape[0]
    across_tiles = width // LANES
    score = hd.dim ** -0.5

    @pl.when(step == 0)
    def _():
        small_t[...] = small[...].astype(F32).T
        set_masks(hd, masks)
        acc_out[...] = jnp.zeros_like(acc_out)
        acc_up[...] = jnp.zeros_like(acc_up)
        acc_down[...] = jnp.zeros_like(acc_down)
        acc_vec[...] = jnp.zeros_like(acc_vec)

    row = lambda i: small_t[i : i + 1, :]
    iota0 = lax.broadcasted_iota(jnp.int32, (seq, seq), 0)
    iota1 = lax.broadcasted_iota(jnp.int32, (seq, seq), 1)
    token_row = lax.broadcasted_iota(jnp.int32, (1, seq), 1)
    one = lambda c: c.astype(F32).astype(BF)
    label_rows = []
    for m in range(mols):
        nodes = counts[0, step * mols + m]
        live = nodes + counts[1, step * mols + m]
        eig_f = eig[m]
        eig_low = eig_f.astype(BF)
        shift = one(jnp.logical_and(iota1 - iota0 == nodes, iota1 < live))
        halves = []
        for end in range(2):
            pick = one(iota0 == ends[m, end : end + 1, :])
            edge_lab = nn(eig_low, pick).astype(BF)
            moved = nn(edge_lab, shift)
            halves.append(jnp.where(token_row < nodes, eig_f, moved))
        is_node = (token_row < nodes).astype(F32)
        is_edge = jnp.logical_and(token_row >= nodes, token_row < live).astype(F32)
        kind = jnp.where(lax.broadcasted_iota(jnp.int32, (16, seq), 0) == 0, is_node,
                         jnp.where(lax.broadcasted_iota(jnp.int32, (16, seq), 0) == 1, is_edge, 0.0))
        lab = jnp.concatenate(halves + [kind], 0)
        labt_o[m] = lab.astype(BF)
        pad = jnp.zeros((SMALL - lab.shape[0], seq), F32)
        label_rows.append(jnp.concatenate([lab, pad], 0).T.astype(BF))
    labels = jnp.concatenate(label_rows, 0)
    embedded = tokens[...].astype(F32) + nn(labels, small_t[...].astype(BF))
    emb_o[...] = embedded
    normed, recip = layer_stats(embedded)
    input_one = (normed * row(GAIN1) + row(SHIFT1)).astype(BF)
    for part in range(3):
        cols = slice(part * width, (part + 1) * width)
        value = nn(input_one, w_in[:, cols])
        if part == 0:
            value = value + row(QBIAS)
        if part == 2:
            value = value + row(VBIAS)
        value = value.astype(BF)
        for t in range(across_tiles):
            proj_o[part * across_tiles + t] = value[:, t * LANES : (t + 1) * LANES]

    for m in range(mols):
        nodes = counts[0, step * mols + m]
        live = nodes + counts[1, step * mols + m]
        key_live = lax.broadcasted_iota(jnp.int32, (seq, 2 * seq), 0) < live
        rows = slice(m * seq, (m + 1) * seq)
        for b in range(hd.blocks):
            base = b * hd.tiles * LANES
            get = lambda part: [proj_o[part * across_tiles + b * hd.tiles + t, rows, :] for t in range(hd.tiles)]
            q, k, v = get(0), get(1), get(2)
            for pair in range(hd.block // 2):
                scores = nt(pair_full(hd, k, pair), pair_rows(hd, masks, q, pair))
                scores = jnp.where(key_live, scores, MASK_FILL)
                top = jnp.max(scores, 0, keepdims=True)
                ex = jnp.exp2((scores - top) * (score * LOG2E))
                total = jnp.sum(ex, 0, keepdims=True)
                shares = (ex * (1.0 / total)).astype(BF)
                lse_o[m, b * (hd.block // 2) + pair : b * (hd.block // 2) + pair + 1, :] = (
                    top + jnp.log2(total) * (1.0 / (score * LOG2E))
                )
                for i in range(2):
                    h = 2 * pair + i
                    p_buf[b * hd.block + h] = shares[:, i * seq : (i + 1) * seq].T
            for t in range(hd.tiles):
                hs = hd.heads_of(t)
                mixed = nn(across([p_buf[b * hd.block + h] for h in hs]), tile_rows(hd, masks, v[t], t))
                mixed_s[b * hd.tiles + t, rows, :] = mixed.astype(BF)

    mixed = across([mixed_s[t] for t in range(across_tiles)])
    middle = embedded + (nt(mixed, w_out[...]) + row(OBIAS))
    normed2, recip2 = layer_stats(middle)
    input_two = (normed2 * row(GAIN2) + row(SHIFT2)).astype(BF)
    pre = nn(input_two, w_up[...]) + row(UBIAS)
    half_erf = 0.5 * (1.0 + lax.erf(pre * SQRT_HALF))
    act = (pre * half_erf).astype(BF)
    slope = half_erf + pre * jnp.exp(-0.5 * pre * pre) * INV_SQRT_TWO_PI
    out_o[...] = (middle + (nt(act, w_down[...]) + row(DBIAS))).astype(BF)
    back = cot[...]
    back_f = back.astype(F32)
    d_pre_f = nn(back, w_down[...]) * slope
    d_pre = d_pre_f.astype(BF)
    acc_down[...] += tn(back, act)
    acc_up[...] += tn(input_two, d_pre)
    d_in2 = nt(d_pre, w_up[...])
    d_mid = back_f + norm_back(d_in2, normed2, recip2, row(GAIN2))
    dmid_o[...] = d_mid
    branch = d_mid.astype(BF)
    acc_out[...] += tn(branch, mixed)
    d_mixed = nn(branch, w_out[...]).astype(BF)
    for t in range(across_tiles):
        dmix_o[t] = d_mixed[:, t * LANES : (t + 1) * LANES]
    add = lambda v: jnp.sum(v, 0, keepdims=True)
    sums = {
        OBIAS: add(branch.astype(F32)),
        GAIN2: add(d_in2 * normed2),
        SHIFT2: add(d_in2),
        UBIAS: add(d_pre.astype(F32)),
        DBIAS: add(back_f),
    }
    for i, v in sums.items():
        acc_vec[i - 34 : i - 33, :] += v

    @pl.when(step == steps - 1)
    def _():
        gout_o[...] = acc_out[...].astype(BF)
        gup_o[...] = acc_up[...].astype(BF)
        gdown_o[...] = acc_down[...].astype(BF)
        gvec_o[...] = acc_vec[...]


def plain_back_kernel(
    counts, proj, lse, emb, dmid, dmix, labt, w_in, small, gvec,
    tg_o, gin_o, gsmall_o,
    small_t, masks, pt_buf, dst_buf, ds_buf, dproj_s, acc_in, acc_vec, acc_lab,
    *, hd, mols, seq, steps,
):
    step = pl.program_id(0)
    width = w_in.shape[0]
    across_tiles = width // LANES
    score = hd.dim ** -0.5

    @pl.when(step == 0)
    def _():
        small_t[...] = small[...].astype(F32).T
        set_masks(hd, masks)
        acc_in[...] = jnp.zeros_like(acc_in)
        acc_vec[...] = gvec[...]
        acc_lab[...] = jnp.zeros_like(acc_lab)

    row = lambda i: small_t[i : i + 1, :]
    for m in range(mols):
        nodes = counts[0, step * mols + m]
        live = nodes + counts[1, step * mols + m]
        key_live = lax.broadcasted_iota(jnp.int32, (seq, 2 * seq), 0) < live
        rows = slice(m * seq, (m + 1) * seq)
        for b in range(hd.blocks):
            base = b * hd.tiles * LANES
            get = lambda ref, part: [ref[part * across_tiles + b * hd.tiles + t, rows, :] for t in range(hd.tiles)]
            q, k, v, do = get(proj, 0), get(proj, 1), get(proj, 2), get(dmix, 0)
            for pair in range(hd.block // 2):
                scores = nt(pair_full(hd, k, pair), pair_rows(hd, masks, q, pair))
                scores = jnp.where(key_live, scores, MASK_FILL)
                at = b * (hd.block // 2) + pair
                p = jnp.exp2((scores - lse[m, at : at + 1, :]) * (score * LOG2E))
                dp = nt(pair_full(hd, v, pair), pair_rows(hd, masks, do, pair))
                inner = jnp.sum(p * dp, 0, keepdims=True)
                ds = (p * (dp - inner)).astype(BF)
                p = p.astype(BF)
                for i in range(2):
                    h = b * hd.block + 2 * pair + i
                    pt_buf[h] = p[:, i * seq : (i + 1) * seq]
                    dst_buf[h] = ds[:, i * seq : (i + 1) * seq]
                    ds_buf[h] = ds[:, i * seq : (i + 1) * seq].T
            for t in range(hd.tiles):
                hs = [b * hd.block + h for h in hd.heads_of(t)]
                at = b * hd.tiles + t
                d_v = nn(across([pt_buf[h] for h in hs]), tile_rows(hd, masks, do[t], t))
                d_k = nn(across([dst_buf[h] for h in hs]), tile_rows(hd, masks, q[t], t)) * score
                d_q = nn(across([ds_buf[h] for h in hs]), tile_rows(hd, masks, k[t], t)) * score
                dproj_s[at, rows, :] = d_q.astype(BF)
                dproj_s[across_tiles + at, rows, :] = d_k.astype(BF)
                dproj_s[2 * across_tiles + at, rows, :] = d_v.astype(BF)

    normed, recip = layer_stats(emb[...])
    input_one = (normed * row(GAIN1) + row(SHIFT1)).astype(BF)
    d_proj = across([dproj_s[t] for t in range(3 * across_tiles)])
    acc_in[...] += tn(input_one, d_proj)
    d_in1 = nt(d_proj, w_in[...])
    tg = dmid[...] + norm_back(d_in1, normed, recip, row(GAIN1))
    tg_o[...] = tg
    tg_hi = tg.astype(BF)
    tg_lo = (tg - tg_hi.astype(F32)).astype(BF)
    lab = jnp.concatenate([labt[m] for m in range(mols)], 1)
    acc_lab[...] += nn(lab, tg_hi)
    acc_lab[32:48, :] += nn(lab[32:48, :], tg_lo)
    add = lambda v: jnp.sum(v, 0, keepdims=True)
    sums = {
        GAIN1: add(d_in1 * normed),
        SHIFT1: add(d_in1),
        QBIAS: add(d_proj[:, :width].astype(F32)),
        VBIAS: add(d_proj[:, 2 * width :].astype(F32)),
    }
    for i, v in sums.items():
        acc_vec[i - 34 : i - 33, :] += v

    @pl.when(step == steps - 1)
    def _():
        gin_o[...] = acc_in[...].astype(BF)
        full = jnp.concatenate(
            [acc_lab[0:32, :], acc_lab[32:34, :], acc_vec[0:9, :], jnp.zeros((SMALL - 43, width), F32)], 0
        )
        gsmall_o[...] = full.T.astype(BF)


def whole(shape):
    return pl.BlockSpec(shape, lambda *_: (0,) * len(shape), pipeline_mode=pl.Buffered(1))


def out_whole(shape):
    return pl.BlockSpec(shape, lambda *_: (0,) * len(shape))


def plain_layer(tokens, eig_t, counts_t, ends_t, cot, w_in, w_out, w_up, w_down, small, mols_step):
    count, width = tokens.shape
    mols_all, lap, seq = eig_t.shape
    hd = Heads(width)
    steps = mols_all // mols_step
    rows = mols_step * seq
    tok = lambda w: pl.BlockSpec((rows, w), lambda i, *_: (i, 0))
    tiled = lambda n: pl.BlockSpec((n, rows, LANES), lambda i, *_: (0, i, 0))
    across_tiles = width // LANES
    mol = lambda a, b: pl.BlockSpec((mols_step, a, b), lambda i, *_: (i, 0, 0))
    params = pltpu.CompilerParams(vmem_limit_bytes=VMEM_LIMIT, dimension_semantics=("arbitrary",))
    sq = (width, width)
    front = pl.pallas_call(
        functools.partial(plain_front_kernel, hd=hd, mols=mols_step, seq=seq, steps=steps),
        grid_spec=pltpu.PrefetchScalarGridSpec(
            num_scalar_prefetch=1,
            grid=(steps,),
            in_specs=[tok(width), mol(lap, seq), mol(2, seq), tok(width), whole((width, 3 * width)),
                      whole(sq), whole(sq), whole(sq), whole((width, SMALL))],
            out_specs=[tok(width), tiled(3 * across_tiles), mol(HEADS // 2, 2 * seq), tok(width), tok(width), tiled(across_tiles),
                       mol(48, seq), out_whole(sq), out_whole(sq), out_whole(sq), out_whole((16, width))],
            scratch_shapes=[
                pltpu.VMEM((SMALL, width), F32),
                pltpu.VMEM((hd.slots(), 16, LANES), BF),
                pltpu.VMEM((across_tiles, rows, LANES), BF),
                pltpu.VMEM((HEADS, seq, seq), BF),
                pltpu.VMEM(sq, F32), pltpu.VMEM(sq, F32), pltpu.VMEM(sq, F32),
                pltpu.VMEM((16, width), F32),
            ],
        ),
        out_shape=[
            jax.ShapeDtypeStruct((count, width), BF),
            jax.ShapeDtypeStruct((3 * across_tiles, count, LANES), BF),
            jax.ShapeDtypeStruct((mols_all, HEADS // 2, 2 * seq), F32),
            jax.ShapeDtypeStruct((count, width), F32),
            jax.ShapeDtypeStruct((count, width), F32),
            jax.ShapeDtypeStruct((across_tiles, count, LANES), BF),
            jax.ShapeDtypeStruct((mols_all, 48, seq), BF),
            jax.ShapeDtypeStruct(sq, BF),
            jax.ShapeDtypeStruct(sq, BF),
            jax.ShapeDtypeStruct(sq, BF),
            jax.ShapeDtypeStruct((16, width), F32),
        ],
        compiler_params=params,
        name="plain_front",
    )(counts_t, tokens, eig_t, ends_t, cot, w_in, w_out, w_up, w_down, small)
    out, proj, lse, emb, dmid, dmix, labt, g_out, g_up, g_down, g_vec = front
    tg, g_in, g_small = pl.pallas_call(
        functools.partial(plain_back_kernel, hd=hd, mols=mols_step, seq=seq, steps=steps),
        grid_spec=pltpu.PrefetchScalarGridSpec(
            num_scalar_prefetch=1,
            grid=(steps,),
            in_specs=[tiled(3 * across_tiles), mol(HEADS // 2, 2 * seq), tok(width), tok(width), tiled(across_tiles), mol(48, seq),
                      whole((width, 3 * width)), whole((width, SMALL)), whole((16, width))],
            out_specs=[tok(width), out_whole((width, 3 * width)), out_whole((width, SMALL))],
            scratch_shapes=[
                pltpu.VMEM((SMALL, width), F32),
                pltpu.VMEM((hd.slots(), 16, LANES), BF),
                pltpu.VMEM((HEADS, seq, seq), BF),
                pltpu.VMEM((HEADS, seq, seq), BF),
                pltpu.VMEM((HEADS, seq, seq), BF),
                pltpu.VMEM((3 * across_tiles, rows, LANES), BF),
                pltpu.VMEM((width, 3 * width), F32),
                pltpu.VMEM((16, width), F32),
                pltpu.VMEM((48, width), F32),
            ],
        ),
        out_shape=[
            jax.ShapeDtypeStruct((count, width), F32),
            jax.ShapeDtypeStruct((width, 3 * width), BF),
            jax.ShapeDtypeStruct((width, SMALL), BF),
        ],
        compiler_params=params,
        name="plain_back",
    )(counts_t, proj, lse, emb, dmid, dmix, labt, w_in, small, g_vec)
    return out, tg, g_in, g_out, g_up, g_down, g_small


def update_kernel(
    steps, rates, large_a, large_b, norm, g_in, g_out, g_up, g_down, g_small, *refs,
):
    states, outs, norm_o = refs[:18], refs[18:42], refs[42]
    moves = []
    for i, (source, target, stay) in enumerate(((large_b, refs[44], refs[46]), (large_a, refs[43], refs[45]))):
        size = source.shape[0] // MOVES
        for j in range(MOVES):
            part = pl.ds(j * size, size)
            moves.append((
                pltpu.make_async_copy(source.at[part], stay.at[part], refs[47].at[2 * (MOVES * i + j)]),
                pltpu.make_async_copy(stay.at[part], target.at[part], refs[47].at[2 * (MOVES * i + j) + 1]),
            ))
    for load, _ in moves:
        load.start()
    for load, store in moves:
        load.wait()
        store.start()
    norm_o[0, 0] = norm[0, 0]
    total = norm[0:1, 0:1]
    factor = jnp.minimum(1.0, CLIP_LIMIT / (total + NORM_EPS))
    t = jnp.full((1, 1), steps[0].astype(F32), F32)
    rate = rates[0]
    fix_one = 1.0 / (1.0 - jnp.exp(t * math.log(BETA_ONE)))
    fix_two = 1.0 / (1.0 - jnp.exp(t * math.log(BETA_TWO)))
    small = g_small[...]
    turned = jnp.concatenate([small, jnp.zeros((LANES - small.shape[0], SMALL), F32)], 0).T
    vec = turned[32:43, : small.shape[0]]
    vec = jnp.concatenate([vec[2:, :], vec[:2, :]], 0)
    grads = (g_in[...], g_out[...], g_up[...], g_down[...], small[:, :32], vec)
    for i, g in enumerate(grads):
        master, first, second = (states[3 * i + j][...] for j in range(3))
        g = g * factor
        first = BETA_ONE * first + (1.0 - BETA_ONE) * g
        second = BETA_TWO * second + (1.0 - BETA_TWO) * g * g
        change = first * fix_one / (jnp.sqrt(second * fix_two) + ADAM_EPS)
        if i < 5:
            change = change + DECAY_RATE * master
        for j, v in enumerate((g, first, second, master - rate * change)):
            outs[4 * i + j][...] = v
    for _, store in moves:
        store.wait()


def update_call(step_count, learn_rate, large, norm, grads, states):
    vm, sm, hbm = (pl.BlockSpec(memory_space=m) for m in (pltpu.VMEM, pltpu.SMEM, pl.ANY))
    shapes = [jax.ShapeDtypeStruct(states[3 * i].shape, F32) for i in range(6) for _ in range(4)]
    return pl.pallas_call(
        update_kernel,
        in_specs=[sm, sm, hbm, hbm] + [vm] * 24,
        out_specs=[vm] * 24 + [sm, hbm, hbm],
        out_shape=shapes + [jax.ShapeDtypeStruct((1, 1), F32)] + [jax.ShapeDtypeStruct(v.shape, v.dtype) for v in large],
        scratch_shapes=[pltpu.VMEM(v.shape, v.dtype) for v in large] + [pltpu.SemaphoreType.DMA((4 * MOVES,))],
        compiler_params=pltpu.CompilerParams(vmem_limit_bytes=VMEM_LIMIT),
        name="update",
    )(step_count.reshape(1), learn_rate.reshape(1), *large, norm, *grads, *states)


def body(
    count,
    tokens, eigvecs, counts, endpoints, cotangent,
    attend_in, attend_in_first, attend_in_second,
    attend_out, attend_out_first, attend_out_second,
    feed_up, feed_up_first, feed_up_second,
    feed_down, feed_down_first, feed_down_second,
    label_in, label_in_first, label_in_second,
    vectors, vectors_first, vectors_second,
    step_count, learn_rate,
):
    shard, width = feed_up.shape
    squares = (attend_in, attend_out.T, feed_up, feed_down.T)
    arrays = (tokens, jnp.swapaxes(eigvecs, 1, 2), counts.T, jnp.swapaxes(endpoints, 1, 2), cotangent)
    if Plan.fits(count, shard):
        out, tg, sums, norm = paired_layer(Plan(count), *arrays, squares + (label_in.T, vectors), MOLS_STEP)
    else:
        small_shard = jnp.concatenate(
            [label_in.T, vectors[9:].T, vectors[:9].T, jnp.zeros((shard, SMALL - 43), F32)], 1
        )
        shards = squares + (small_shard,)
        weights = [lax.all_gather(v.astype(BF), "dp", axis=0, tiled=True) for v in shards]
        out, tg, *grads = plain_layer(*arrays, *weights, 2)
        sums = [lax.psum_scatter(v.astype(F32), "dp", scatter_dimension=0, tiled=True) for v in grads]
        total = lax.psum(sum(jnp.sum(v * v) for v in sums), "dp")
        norm = jnp.full((8, LANES), jnp.sqrt(total), F32)
    states = (
        attend_in, attend_in_first, attend_in_second,
        attend_out.T, attend_out_first.T, attend_out_second.T,
        feed_up, feed_up_first, feed_up_second,
        feed_down.T, feed_down_first.T, feed_down_second.T,
        label_in.T, label_in_first.T, label_in_second.T,
        vectors, vectors_first, vectors_second,
    )
    *new, norm, out, tg = update_call(step_count, learn_rate, (out, tg), norm, sums, states)
    new = [v.T if i // 4 in (1, 3, 4) else v for i, v in enumerate(new)]
    return (out, tg, norm.reshape(()), *new)


MOLS_STEP = 4
SLOTS_GATHER = (1, 3, 4, 6)
SLOTS_SCATTER = (0, 2, 3, 4, 6)
WIDE = 512
EVERY = 2
MOVES = 8


def solution(mesh):
    rows, cols = P("dp", None), P(None, "dp")
    state = (rows,) * 3 + (cols,) * 3 + (rows,) * 3 + (cols,) * 9
    placed = (rows, P("dp", None, None), rows, P("dp", None, None), rows) + state + (P(), P())
    results = (rows,) * 4 + (cols,) * 4 + (rows,) * 4 + (cols,) * 12
    return jax.shard_map(
        functools.partial(body, mesh.shape["dp"]),
        mesh=mesh, in_specs=placed, out_specs=(rows, rows, P()) + results, check_vma=False,
    )
```
